32 devices in a mesh: dp: 4 (over y, core), blk: 8 (over z, x).
Axes of the slice: x: 2, y: 2, z: 4, core: 2. Of those that a mesh axis runs over, the one named last changes fastest.
Arguments:
- block_in: bfloat16 [4, 1024, 512], P('dp', 'blk'), may hold values from -6 to 6
- seq_lengths: int32 [4], P('dp'), may hold values from 897 to 1024, as said below
- norm1_gain: float32 [512], replicated, may hold values from 0.5 to 1.5
- norm1_bias: float32 [512], replicated, may hold values from -3 to 3
- log_step: float32 [512], replicated, may hold values from -7 to -5.5
- log_rate: float32 [512, 64], replicated, may hold values from -12 to -2.99
- frequency: float32 [512, 64], replicated, may hold values from 0 to 192
- out_coef: float32 [2, 512, 64], replicated, may hold values from -3 to 3
- skip_gain: float32 [512], replicated, may hold values from -4 to 4
- glu_weight: bfloat16 [512, 1024], replicated, may hold values from -0.25 to 0.25
- glu_bias: float32 [1024], replicated, may hold values from -3 to 3
- norm2_gain: float32 [512], replicated, may hold values from 0.5 to 1.5
- norm2_bias: float32 [512], replicated, may hold values from -3 to 3
- ffn_in: bfloat16 [512, 2048], replicated, may hold values from -0.25 to 0.25
- ffn_in_bias: float32 [2048], replicated, may hold values from -3 to 3
- ffn_out: bfloat16 [2048, 512], replicated, may hold values from -0.125 to 0.125
- ffn_out_bias: float32 [512], replicated, may hold values from -3 to 3
- cotangent: bfloat16 [4, 1024, 512], P('dp', 'blk'), may hold values from -6 to 6
Outputs:
- block_out: bfloat16 [4, 1024, 512], P('dp', 'blk')
- grad_block_in: float32 [4, 1024, 512], P('dp', 'blk')
- grad_norm1_gain: float32 [512], replicated
- grad_norm1_bias: float32 [512], replicated
- grad_log_step: float32 [512], replicated
- grad_log_rate: float32 [512, 64], replicated
- grad_frequency: float32 [512, 64], replicated
- grad_out_coef: float32 [2, 512, 64], replicated
- grad_skip_gain: float32 [512], replicated
- grad_glu_weight: float32 [512, 1024], replicated
- grad_glu_bias: float32 [1024], replicated
- grad_norm2_gain: float32 [512], replicated
- grad_norm2_bias: float32 [512], replicated
- grad_ffn_in: float32 [512, 2048], replicated
- grad_ffn_in_bias: float32 [2048], replicated
- grad_ffn_out: float32 [2048, 512], replicated
- grad_ffn_out_bias: float32 [512], replicated
The draws below stay inside these ranges and needn't reach their ends.
Inputs may be any that keep to these rules, and one draw needn't show every extreme that they name: `seq_lengths`: every sequence has at least its last block partly live; some sequence is live to its end.
All inputs are finite; a program needn't handle non-finite values.
Results may differ from the reference program's by a relative error of at most 0.014.
Values sent between devices are 32-bit elements; how exact they have to be, the bound alone decides.
A program may use at most 128 MiB of HBM per device.

```python
import jax
import jax.numpy as jnp
from jax import lax

D = 512
STATE = 64
FF = 2048
BLK_TOK = 128
BATCH = 4
SEQ = 1024
N_BLK = 8


def draw_seq_lengths(key, part):
    key = jax.random.fold_in(key, 5)
    first_key, second_key = jax.random.split(key)
    drawn = jax.random.randint(first_key, (BATCH,), SEQ - BLK_TOK + 1, SEQ + 1)
    chosen = jax.random.randint(second_key, (), 0, BATCH)
    return jnp.where(jnp.arange(BATCH) == chosen, SEQ, drawn).astype(jnp.int32)


def draw_log_rate(key, part):
    key = jax.random.fold_in(key, 7)
    lowest = jnp.log(0.3 / SEQ)
    highest = jnp.log(0.05)
    return jax.random.uniform(key, (D, STATE), jnp.float32, lowest, highest)


def levels(key, extent, pieces, least, largest):
    factor_of, own = 1.0, jax.random.fold_in(key, 6)
    for dim, parts in pieces:
        steps = jnp.exp(jax.random.uniform(jax.random.fold_in(own, dim), (parts,), jnp.float32, least / len(pieces), largest / len(pieces)))
        factor_of = factor_of * jnp.repeat(steps, extent[dim] // parts).reshape([-1 if axis == dim else 1 for axis in range(len(extent))])
    return factor_of


def scatter_about(own_key, dims, spread, reach, pieces=(), held_as=jnp.bfloat16):
    values = jax.random.normal(own_key, dims, jnp.float32) * spread
    if len(pieces) > 0:
        values = levels(own_key, dims, pieces, -0.22, 0.18) * values
    return jnp.clip(values, min=-reach, max=reach).astype(held_as)


def setup_inputs(seed: int = 0) -> dict:
    key_list = jax.random.split(jax.random.key(seed), 19)
    return {
        "block_in": scatter_about(key_list[0], (BATCH, SEQ, D), 1.0, 6.0, ((0, 4), (1, 8))),
        "seq_lengths": draw_seq_lengths(jax.random.fold_in(key_list[18], 71), 0),
        "norm1_gain": jnp.clip(1.0 + 0.1 * jax.random.normal(key_list[2], (D,), jnp.float32), 0.5, 1.5),
        "norm1_bias": scatter_about(key_list[3], (D,), 0.3, 3.0, (), jnp.float32),
        "log_step": jnp.clip(jax.random.uniform(key_list[4], (D,), jnp.float32, -7.0, -5.5), -7.0, -5.5),
        "log_rate": draw_log_rate(jax.random.fold_in(key_list[18], 71), 0),
        "frequency": jnp.clip(jax.random.uniform(key_list[6], (D, STATE), jnp.float32, 0.0, 192.0), 0.0, 192.0),
        "out_coef": scatter_about(key_list[7], (2, D, STATE), 0.5, 3.0, (), jnp.float32),
        "skip_gain": scatter_about(key_list[8], (D,), 1.0, 4.0, (), jnp.float32),
        "glu_weight": scatter_about(key_list[9], (D, 2 * D), D ** -0.5, 0.25),
        "glu_bias": scatter_about(key_list[10], (2 * D,), 0.3, 3.0, (), jnp.float32),
        "norm2_gain": jnp.clip(1.0 + 0.1 * jax.random.normal(key_list[11], (D,), jnp.float32), 0.5, 1.5),
        "norm2_bias": scatter_about(key_list[12], (D,), 0.3, 3.0, (), jnp.float32),
        "ffn_in": scatter_about(key_list[13], (D, FF), D ** -0.5, 0.25),
        "ffn_in_bias": scatter_about(key_list[14], (FF,), 0.3, 3.0, (), jnp.float32),
        "ffn_out": scatter_about(key_list[15], (FF, D), FF ** -0.5, 0.125),
        "ffn_out_bias": scatter_about(key_list[16], (D,), 0.3, 3.0, (), jnp.float32),
        "cotangent": scatter_about(key_list[17], (BATCH, SEQ, D), 1.0, 6.0, ((0, 4), (1, 8))),
    }


NORM_EPSILON = 1e-05
PRECISE = lax.Precision.HIGHEST

@jax.custom_vjp
def low(v):
    return lax.optimization_barrier(v.astype(jnp.bfloat16)).astype(jnp.float32)

@jax.custom_vjp
def low_back(v):
    return v

def low_keep(v):
    return (low(v), None)

def low_pass(kept, grad):
    return (grad,)

def back_keep(v):
    return (v, None)

def back_low(kept, grad):
    return (low(grad),)
low.defvjp(low_keep, low_pass)
low_back.defvjp(back_keep, back_low)

def complex_mul(left, right):
    return jnp.stack([left[0] * right[0] - left[1] * right[1], left[0] * right[1] + left[1] * right[0]])

def powers(log_pole, counts):
    growth = jnp.exp(log_pole[0][..., None] * counts)
    angles = log_pole[1][..., None] * counts
    return jnp.stack([growth * jnp.cos(angles), growth * jnp.sin(angles)])

def ssm_setup(log_step, log_rate, frequency, out_coef):
    step_size = jnp.exp(log_step)
    pole_real = -jnp.exp(log_rate)
    pole_imag = step_size[:, None] * frequency
    half_turn = jnp.sin(0.5 * pole_imag)
    minus_real = jnp.expm1(pole_real) * jnp.cos(pole_imag) - 2.0 * half_turn * half_turn
    minus_imag = jnp.exp(pole_real) * jnp.sin(pole_imag)
    modulus = pole_real * pole_real + pole_imag * pole_imag
    ratios = jnp.stack([(minus_real * pole_real + minus_imag * pole_imag) / modulus, (minus_imag * pole_real - minus_real * pole_imag) / modulus])
    return (jnp.stack([pole_real, pole_imag]), complex_mul(out_coef * step_size[None, :, None], ratios))

def group_size(channels):
    return 64 if channels % 64 == 0 else channels

def full_kernel(log_step, log_rate, frequency, out_coef):
    log_pole, residue = ssm_setup(log_step, log_rate, frequency, out_coef)
    size_one = group_size(D)
    groups = D // size_one
    pole_groups = log_pole.reshape(2, groups, size_one, STATE).transpose(1, 0, 2, 3)
    residue_groups = residue.reshape(2, groups, size_one, STATE).transpose(1, 0, 2, 3)
    near_counts = jnp.arange(BLK_TOK).astype(jnp.float32)
    far_counts = (jnp.arange(N_BLK) * BLK_TOK).astype(jnp.float32)

    def per_group(group_args):
        pole_one, residue_one = group_args
        near_powers = powers(pole_one, near_counts)
        far_weights = complex_mul(residue_one[..., None], powers(pole_one, far_counts))
        kernel = jnp.einsum('cnm,cnt->cmt', far_weights[0], near_powers[0], precision=PRECISE)
        kernel = kernel - jnp.einsum('cnm,cnt->cmt', far_weights[1], near_powers[1], precision=PRECISE)
        return 2.0 * kernel.reshape(size_one, N_BLK * BLK_TOK)
    return lax.map(jax.checkpoint(per_group), (pole_groups, residue_groups)).reshape(D, SEQ)

def long_conv(mixed, kernel):
    length = mixed.shape[1]
    spectrum = jnp.fft.rfft(mixed, n=2 * length, axis=1) * jnp.fft.rfft(kernel.T, n=2 * length, axis=0)[None]
    return jnp.fft.irfft(spectrum, n=2 * length, axis=1)[:, :length]

def layer_norm(values, gain, shift):
    center = values - lax.optimization_barrier(jnp.mean(values, axis=-1, keepdims=True))
    variance = lax.optimization_barrier(jnp.mean(center * center, axis=-1, keepdims=True))
    return center * lax.rsqrt(variance + NORM_EPSILON) * gain + shift

def reference(block_in, seq_lengths, norm1_gain, norm1_bias, log_step, log_rate, frequency, out_coef, skip_gain, glu_weight, glu_bias, norm2_gain, norm2_bias, ffn_in, ffn_in_bias, ffn_out, ffn_out_bias, cotangent):
    places = jnp.arange(SEQ).astype(jnp.int32)
    live = (places[None, :] < seq_lengths[:, None]).astype(jnp.float32)[..., None]

    def forward(inputs, gain_one, bias_one, step_log, rate_log, freq_in, coef_in, skip_in, glu_w, glu_b, gain_two, bias_two, first_w, first_b, second_w, second_b):
        mixed = low(layer_norm(inputs, gain_one, bias_one)) * live
        kernel = full_kernel(step_log, rate_log, freq_in, coef_in)
        conv = long_conv(mixed, kernel) + skip_in * mixed
        gelu_out = low(jax.nn.gelu(conv))
        glu_pre = low_back(jnp.matmul(gelu_out, glu_w, precision=PRECISE) + glu_b)
        glu_out = glu_pre[..., :D] * jax.nn.sigmoid(glu_pre[..., D:])
        residual = inputs + live * glu_out
        ffn_feed = low(layer_norm(residual, gain_two, bias_two))
        hidden_pre = low_back(jnp.matmul(ffn_feed, first_w, precision=PRECISE) + first_b)
        hidden = low(jax.nn.gelu(hidden_pre))
        ffn_result = low_back(jnp.matmul(hidden, second_w, precision=PRECISE) + second_b)
        return residual + live * ffn_result
    primals = (block_in.astype(jnp.float32), norm1_gain, norm1_bias, log_step, log_rate, frequency, out_coef, skip_gain, glu_weight.astype(jnp.float32), glu_bias, norm2_gain, norm2_bias, ffn_in.astype(jnp.float32), ffn_in_bias, ffn_out.astype(jnp.float32), ffn_out_bias)
    result, pull = jax.vjp(forward, *primals)
    grads = pull(cotangent.astype(jnp.float32))
    return (result.astype(jnp.bfloat16), grads[0], grads[1], grads[2], grads[3], grads[4], grads[5], grads[6], grads[7], grads[8], grads[9], grads[10], grads[11], grads[12], grads[13], grads[14], grads[15])
```

```python
import functools

import jax
import jax.numpy as jnp
from jax import lax
from jax.experimental import pallas as pl
from jax.experimental.pallas import tpu as pltpu
from jax.sharding import PartitionSpec as P

NORM_EPSILON = 1e-05
F32 = jnp.float32
BF16 = jnp.bfloat16
PRECISE = lax.Precision.HIGHEST
SERIES = 16
VMEM = pltpu.VMEM


def iota(shape, axis):
    return lax.broadcasted_iota(jnp.int32, shape, axis)


def is_left(shape):
    half = shape[-1] // 2
    return iota(shape, len(shape) - 1) < half


def swap(v):
    return pltpu.roll(v, v.shape[-1] // 2, v.ndim - 1)


def times(v, const):
    return v * const[0] + swap(v) * const[1]


def split(v):
    high = v.astype(BF16)
    return high, (v - high.astype(F32)).astype(BF16)


def nn(a, b):
    return lax.dot_general(a, b, (((1,), (0,)), ((), ())), preferred_element_type=F32)


def nt(a, b):
    return lax.dot_general(a, b, (((1,), (1,)), ((), ())), preferred_element_type=F32)


def tn(a, b):
    return lax.dot_general(a, b, (((0,), (0,)), ((), ())), preferred_element_type=F32)


def cmul(a, b):
    return a[0] * b[0] - a[1] * b[1], a[0] * b[1] + a[1] * b[0]


def twice(v):
    return jnp.concatenate([v, v], axis=-1)


def pole_parts(log_step, log_rate, frequency):
    step = jnp.exp(log_step)
    rate = jnp.exp(twice(log_rate))
    pole = (-rate, step * twice(frequency))
    phi = (jnp.full_like(rate, 0.0), jnp.zeros_like(rate))
    slope = (jnp.zeros_like(rate), jnp.zeros_like(rate))
    fact = [1.0]
    for k in range(1, SERIES + 2):
        fact.append(fact[-1] * k)
    for k in range(SERIES, -1, -1):
        phi = cmul(phi, pole)
        phi = (phi[0] + 1.0 / fact[k + 1], phi[1])
    for k in range(SERIES, 0, -1):
        slope = cmul(slope, pole)
        slope = (slope[0] + k / fact[k + 1], slope[1])
    grow = cmul(pole, phi)
    z = (1.0 + grow[0], grow[1])
    return step, rate, z, phi, slope


def as_const(value):
    sign = jnp.where(is_left(value[0].shape), -1.0, 1.0)
    return value[0], value[1] * sign


def packed(value):
    return jnp.where(is_left(value[0].shape), value[0], value[1])


def ssm_setup(chans, rows, refs, consts, base, q_ref, t_ref):
    ls, lr, fr, coef, skip = refs
    step, rate, z, phi, slope = pole_parts(ls[...], lr[...], fr[...])
    b = (twice(coef[0]), twice(coef[1]))
    residue = cmul(b, (step * phi[0], step * phi[1]))
    power = (jnp.ones_like(rate), jnp.zeros_like(rate))
    for r in range(8):
        base[r] = packed(power)
        power = cmul(power, z)
    slot = 0

    def keep(value):
        nonlocal slot
        c = as_const(value)
        consts[2 * slot] = c[0]
        consts[2 * slot + 1] = c[1]
        slot += 1

    for k in range(4):
        keep(power)
        power = cmul(power, power)
    for k in range((rows - 1).bit_length()):
        keep(power)
        power = cmul(power, power)
    lead = cmul(residue, z)
    lead = (2.0 * lead[0], 2.0 * lead[1])
    sign = jnp.where(is_left(rate.shape), 1.0, -1.0)
    consts[2 * slot] = lead[0] * sign
    consts[2 * slot + 1] = -lead[1]
    slot += 1
    kern = jnp.where(is_left(rate.shape), 2.0 * residue[0], -2.0 * residue[1])
    kern_high = kern.astype(BF16).astype(F32)
    consts[2 * slot] = kern_high
    consts[2 * slot + 1] = kern - kern_high
    return slot


def row_of(ref, index, chan):
    return ref[index, pl.ds(chan, 1), :]


def const_of(consts, slot, chan):
    return row_of(consts, 2 * slot, chan), row_of(consts, 2 * slot + 1, chan)


def make_powers(chan, chans, consts, kern_slot, base_flat, q_ref, taps_ref):
    powers = base_flat[pl.ds(chan, 8, stride=chans), :]
    for k in range(4):
        powers = jnp.concatenate([powers, times(powers, const_of(consts, k, chan))], axis=0)
    q_high, q_rest = split(powers)
    q_ref[chan, :128, :] = q_high
    q_ref[chan, 128:, :] = q_rest
    taps = jnp.concatenate([row_of(consts, 2 * kern_slot, chan), row_of(consts, 2 * kern_slot + 1, chan)], axis=0)
    kern = nt(twice(taps.astype(BF16)), jnp.concatenate([q_high, q_rest], axis=1))
    taps_ref[pl.ds(chan, 1), :] = kern[0:1] + kern[1:2]


def shift_taps(skip, taps_ref, base):
    taps = taps_ref[...]
    taps = taps + jnp.where(iota(taps.shape, 1) == 0, skip[...], 0.0)
    for r in range(8):
        base[r] = taps if r == 7 else pltpu.roll(taps, 7 - r, 1)


def make_band(chan, chans, base_flat, t_ref):
    tile = base_flat[pl.ds(chan, 8, stride=chans), :]
    band = jnp.concatenate([pltpu.roll(tile, 120 - 8 * m, 1) if m < 15 else tile for m in range(16)], axis=0)
    band = jnp.where(iota((128, 128), 0) + iota((128, 128), 1) >= 127, band, 0.0)
    t_high, t_rest = split(band)
    t_ref[chan, :128, :] = t_high
    t_ref[chan, 128:, :] = t_rest


def scan(v, consts, first, chan, reverse):
    rows = v.shape[0]
    places = iota(v.shape, 0)

    def moved(x, d):
        if reverse:
            return jnp.where(places < rows - d, pltpu.roll(x, rows - d, 0), 0.0)
        return jnp.where(places >= d, pltpu.roll(x, d, 0), 0.0)

    v = moved(v, 1)
    d, k = 1, 0
    while d < rows:
        v = v + times(moved(v, d), const_of(consts, first + k, chan))
        d, k = 2 * d, k + 1
    return v


def wide(chan, q_ref, t_ref):
    return jnp.concatenate([q_ref[chan], t_ref[chan]], axis=1)


def far_part(lead, chan, q_ref):
    rows = lead.shape[0]
    high, rest = split(lead)
    both = twice(jnp.concatenate([high, rest], axis=0))
    out = nt(both, jnp.concatenate([q_ref[chan, :128, :], q_ref[chan, 128:, :]], axis=1))
    return out[:rows] + out[rows:]


def forward_channel(chan, chans, rows, consts, lead_slot, x_flat, q_ref, t_ref, h_ref, y_flat):
    u = x_flat[pl.ds(chan, rows, stride=chans), :]
    out = nn(twice(u.astype(BF16)), wide(chan, q_ref, t_ref))
    h = scan(out[:, :128], consts, 4, chan, False)
    h_ref[chan] = h
    far = far_part(times(h, const_of(consts, lead_slot, chan)), chan, q_ref)
    y_flat[pl.ds(chan, rows, stride=chans), :] = out[:, 128:] + far


def backward_channel(chan, chans, rows, consts, lead_slot, x_flat, dy_flat, q_ref, t_ref, h_ref, dx_flat, a_ref, b_ref, g_ref):
    u = x_flat[pl.ds(chan, rows, stride=chans), :]
    dy = dy_flat[pl.ds(chan, rows, stride=chans), :]
    places = iota((1, 128), 1).astype(F32)
    high = dy.astype(BF16).astype(F32)
    left = twice(jnp.concatenate([high, dy - high, dy * places, u * places], axis=0).astype(BF16))
    out = nn(left, wide(chan, q_ref, t_ref))
    near = out[:rows, 128:] + out[rows : 2 * rows, 128:]
    d0 = out[:rows, :128] + out[rows : 2 * rows, :128]
    d1 = out[2 * rows : 3 * rows, :128]
    s1 = out[3 * rows :, :128]
    h = h_ref[chan]
    decay = const_of(consts, 4, chan)
    h1 = scan(s1 + 128.0 * times(h, decay), consts, 4, chan, False)
    e = scan(d0, consts, 4, chan, True)
    far = far_part(times(e, const_of(consts, lead_slot, chan)), chan, q_ref)
    dx_flat[pl.ds(chan, rows, stride=chans), :] = near + far
    mask = is_left(h.shape)

    def prod(p, q):
        q_swap = swap(q)
        return p * jnp.where(mask, q, q_swap) + swap(p) * jnp.where(mask, -q_swap, q)

    a_far = jnp.sum(prod(d0, h), axis=0, keepdims=True)
    b_far = a_far + jnp.sum(prod(d1, h) + prod(d0, h1), axis=0, keepdims=True)
    pairs = tn(u.astype(BF16), dy.astype(BF16))
    skew = pltpu.roll(pairs, 1, 1, stride=1, stride_axis=0)
    skew = jnp.where(iota((128, 128), 1) <= iota((128, 128), 0), skew, 0.0)
    lags = jnp.sum(skew, axis=0, keepdims=True)
    g_ref[pl.ds(chan, 1), :] = lags
    rows4 = jnp.concatenate([lags, lags * places], axis=0)
    high, rest = split(rows4)
    near_sums = nn(jnp.concatenate([jnp.concatenate([high, rest], axis=0)] * 2, axis=1), q_ref[chan])
    a_ref[pl.ds(chan, 1), :] = near_sums[0:1] + near_sums[2:3]
    b_ref[pl.ds(chan, 1), :] = near_sums[1:2] + near_sums[3:4]
    a_ref[pl.ds(chans + chan, 1), :] = a_far
    b_ref[pl.ds(chans + chan, 1), :] = b_far


def finish(chans, refs, a_ref, b_ref, g_ref):
    ls, lr, fr, coef, skip = refs
    step, rate, z, phi, slope = pole_parts(ls[...], lr[...], fr[...])
    b = (twice(coef[0]), twice(coef[1]))

    def dup(v):
        left = is_left(v.shape)
        moved = swap(v)
        return jnp.where(left, v, moved), jnp.where(left, moved, v)

    def total(ref):
        near, far = dup(ref[:chans, :]), dup(ref[chans:, :])
        far = cmul(far, z)
        return near[0] + far[0], near[1] + far[1]

    a, bb = total(a_ref), total(b_ref)
    residue = cmul(b, (step * phi[0], step * phi[1]))
    g_res = (2.0 * a[0], -2.0 * a[1])
    rb = cmul(residue, bb)
    g_pole = (2.0 * rb[0], -2.0 * rb[1])
    conj = lambda v: (v[0], -v[1])
    g_coef = cmul(conj((step * phi[0], step * phi[1])), g_res)
    bs = cmul(b, (step * slope[0], step * slope[1]))
    more = cmul(conj(bs), g_res)
    g_pole = (g_pole[0] + more[0], g_pole[1] + more[1])
    d_rate = -rate * g_pole[0]
    d_freq = step * g_pole[1]
    by_step = cmul(conj(cmul(b, phi)), g_res)[0] + g_pole[1] * twice(fr[...])
    left = is_left(by_step.shape)
    d_step = step * jnp.sum(jnp.where(left, by_step, 0.0), axis=1, keepdims=True)
    return jnp.where(left, d_rate, d_freq), jnp.where(left, g_coef[0], g_coef[1]), d_step, g_ref[:, 0:1]


def forward_kernel(chans, rows, x_ref, ls, lr, fr, coef, skip, y_ref, q_ref, t_ref, h_ref, consts, base, taps):
    refs = (ls, lr, fr, coef, skip)
    kern_slot = ssm_setup(chans, rows, refs, consts, base, q_ref, t_ref)
    base_flat = base.reshape(8 * chans, 128)
    x_flat = x_ref.reshape(rows * chans, 128)
    y_flat = y_ref.reshape(rows * chans, 128)

    def make(chan, carry):
        make_powers(chan, chans, consts, kern_slot, base_flat, q_ref, taps)
        return carry

    lax.fori_loop(0, chans, make, 0, unroll=4)
    shift_taps(skip, taps, base)

    def band(chan, carry):
        make_band(chan, chans, base_flat, t_ref)
        return carry

    lax.fori_loop(0, chans, band, 0, unroll=4)

    def go(chan, carry):
        forward_channel(chan, chans, rows, consts, kern_slot - 1, x_flat, q_ref, t_ref, h_ref, y_flat)
        return carry

    lax.fori_loop(0, chans, go, 0, unroll=4)


def backward_kernel(chans, rows, x_ref, dy_ref, q_ref, t_ref, h_ref, consts, ls, lr, fr, coef, skip, dx_ref, rf_ref, co_ref, st_ref, sk_ref, a_ref, b_ref, g_ref):
    refs = (ls, lr, fr, coef, skip)
    x_flat = x_ref.reshape(rows * chans, 128)
    dy_flat = dy_ref.reshape(rows * chans, 128)
    dx_flat = dx_ref.reshape(rows * chans, 128)
    lead_slot = consts.shape[0] // 2 - 2

    def go(chan, carry):
        backward_channel(chan, chans, rows, consts, lead_slot, x_flat, dy_flat, q_ref, t_ref, h_ref, dx_flat, a_ref, b_ref, g_ref)
        return carry

    lax.fori_loop(0, chans, go, 0, unroll=4)
    out = finish(chans, refs, a_ref, b_ref, g_ref)
    rf_ref[...] = out[0]
    co_ref[...] = out[1]
    st_ref[...] = out[2]
    sk_ref[...] = out[3]


def n_consts(rows):
    return 2 * (4 + (rows - 1).bit_length() + 2)


def ssm_forward(x, params):
    rows, chans, _ = x.shape
    shapes = [
        jax.ShapeDtypeStruct(x.shape, F32),
        jax.ShapeDtypeStruct((chans, 256, 128), BF16),
        jax.ShapeDtypeStruct((chans, 256, 128), BF16),
        jax.ShapeDtypeStruct((chans, rows, 128), F32),
        jax.ShapeDtypeStruct((n_consts(rows), chans, 128), F32),
    ]
    return pl.pallas_call(
        functools.partial(forward_kernel, chans, rows),
        out_shape=shapes,
        in_specs=[pl.BlockSpec(memory_space=VMEM)] * 6,
        out_specs=[pl.BlockSpec(memory_space=VMEM)] * 5,
        scratch_shapes=[VMEM((8, chans, 128), F32), VMEM((chans, 128), F32)],
        compiler_params=pltpu.CompilerParams(vmem_limit_bytes=50 * 2**20),
    )(x, *params)


def ssm_backward(x, dy, saved, params):
    rows, chans, _ = x.shape
    shapes = [
        jax.ShapeDtypeStruct(x.shape, F32),
        jax.ShapeDtypeStruct((chans, 128), F32),
        jax.ShapeDtypeStruct((chans, 128), F32),
        jax.ShapeDtypeStruct((chans, 1), F32),
        jax.ShapeDtypeStruct((chans, 1), F32),
    ]
    return pl.pallas_call(
        functools.partial(backward_kernel, chans, rows),
        out_shape=shapes,
        in_specs=[pl.BlockSpec(memory_space=VMEM)] * 11,
        out_specs=[pl.BlockSpec(memory_space=VMEM)] * 5,
        scratch_shapes=[VMEM((2 * chans, 128), F32), VMEM((2 * chans, 128), F32), VMEM((chans, 128), F32)],
        compiler_params=pltpu.CompilerParams(vmem_limit_bytes=50 * 2**20),
    )(x, dy, *saved, *params)


def layer_norm(values, gain, shift):
    center = values - jnp.mean(values, axis=-1, keepdims=True)
    scale = lax.rsqrt(jnp.mean(center * center, axis=-1, keepdims=True) + NORM_EPSILON)
    normed = center * scale
    return (normed * gain + shift, normed, scale)


def norm_back(grad_out, gain, normed, scale):
    scaled = grad_out * gain
    return scale * (
        scaled
        - jnp.mean(scaled, axis=-1, keepdims=True)
        - normed * jnp.mean(scaled * normed, axis=-1, keepdims=True)
    )


def token_sum(values):
    return jnp.sum(values, axis=0)


def dot(spec, a, b):
    return jnp.einsum(spec, a, b, preferred_element_type=F32)


def to_channels(v, blocks):
    rows, width = v.shape
    parts = v.T.reshape(blocks, width // blocks, rows)
    return lax.all_to_all(parts, "blk", 0, 0)


def to_tokens(v):
    parts = lax.all_to_all(v, "blk", 0, 0)
    return parts.reshape(-1, v.shape[-1]).T


def on_device(block_in, seq_lengths, norm1_gain, norm1_bias, log_step, log_rate, frequency, out_coef, skip_gain, glu_weight, glu_bias, norm2_gain, norm2_bias, ffn_in, ffn_in_bias, ffn_out, ffn_out_bias, cotangent):
    _, block_rows, channels = block_in.shape
    blocks = lax.axis_size("blk")
    mine = channels // blocks
    start = lax.axis_index("blk") * mine
    inputs = block_in[0].astype(F32)
    places = lax.axis_index("blk") * block_rows + jnp.arange(block_rows, dtype=jnp.int32)
    live = (places < seq_lengths[0]).astype(F32)[:, None]
    normed_in, unit_in, scale_in = layer_norm(inputs, norm1_gain, norm1_bias)
    mixed = normed_in.astype(BF16).astype(F32) * live
    cut = lambda v, axis: lax.dynamic_slice_in_dim(v, start, mine, axis)
    params = (cut(log_step[:, None], 0), cut(log_rate, 0), cut(frequency, 0), cut(out_coef, 1), cut(skip_gain[:, None], 0))
    x = to_channels(mixed[::-1], blocks)
    y, *saved = ssm_forward(x, params)
    conv_out = to_tokens(y)
    gelu_out = jax.nn.gelu(conv_out).astype(BF16)
    glu_pre = dot("bd,de->be", gelu_out, glu_weight) + glu_bias
    glu_left = glu_pre[..., :channels]
    glu_gate = jax.nn.sigmoid(glu_pre[..., channels:])
    residual = inputs + live * glu_left * glu_gate
    normed_mid, unit_mid, scale_mid = layer_norm(residual, norm2_gain, norm2_bias)
    ffn_feed = normed_mid.astype(BF16)
    hidden_pre = dot("bd,df->bf", ffn_feed, ffn_in) + ffn_in_bias
    hidden = jax.nn.gelu(hidden_pre).astype(BF16)
    ffn_result = dot("bf,fd->bd", hidden, ffn_out) + ffn_out_bias
    block_out = (residual + live * ffn_result).astype(BF16)
    upstream = cotangent[0].astype(F32)
    grad_result = (live * upstream).astype(BF16)
    grad_ffn_out = dot("bf,bd->fd", hidden, grad_result)
    grad_ffn_out_bias = token_sum(grad_result.astype(F32))
    grad_hidden = dot("bd,fd->bf", grad_result, ffn_out)
    grad_pre = jax.vjp(jax.nn.gelu, hidden_pre)[1](grad_hidden)[0].astype(BF16)
    grad_ffn_in = dot("bd,bf->df", ffn_feed, grad_pre)
    grad_ffn_in_bias = token_sum(grad_pre.astype(F32))
    grad_feed = dot("bf,df->bd", grad_pre, ffn_in)
    grad_norm2_gain = token_sum(grad_feed * unit_mid)
    grad_norm2_bias = token_sum(grad_feed)
    grad_residual = upstream + norm_back(grad_feed, norm2_gain, unit_mid, scale_mid)
    grad_left = live * grad_residual
    grad_glu = jnp.concatenate([grad_left * glu_gate, grad_left * glu_left * glu_gate * (1.0 - glu_gate)], axis=-1).astype(BF16)
    grad_glu_weight = dot("bd,be->de", gelu_out, grad_glu)
    grad_glu_bias = token_sum(grad_glu.astype(F32))
    grad_gelu = dot("be,de->bd", grad_glu, glu_weight)
    grad_conv = jax.vjp(jax.nn.gelu, conv_out)[1](grad_gelu)[0]
    dx, rf, co, st, sk = ssm_backward(x, to_channels(grad_conv, blocks), saved, params)
    grad_normed_in = live * to_tokens(dx)[::-1]
    grad_norm1_gain = token_sum(grad_normed_in * unit_in)
    grad_norm1_bias = token_sum(grad_normed_in)
    grad_block_in = grad_residual + norm_back(grad_normed_in, norm1_gain, unit_in, scale_in)
    half = log_rate.shape[1]
    own = jnp.concatenate([rf, co, st, sk], axis=1)
    own = lax.all_gather(lax.psum(own, "dp"), "blk", axis=0, tiled=True)
    totals = lax.psum((grad_norm1_gain, grad_norm1_bias, grad_glu_weight, grad_glu_bias, grad_norm2_gain, grad_norm2_bias, grad_ffn_in, grad_ffn_in_bias, grad_ffn_out, grad_ffn_out_bias), ("dp", "blk"))
    return (
        block_out[None],
        grad_block_in[None],
        totals[0],
        totals[1],
        own[:, 4 * half],
        own[:, :half],
        own[:, half : 2 * half],
        jnp.stack([own[:, 2 * half : 3 * half], own[:, 3 * half : 4 * half]]),
        own[:, 4 * half + 1],
        *totals[2:],
    )


def solution(mesh):
    split_spec, whole = P("dp", "blk", None), P()
    return jax.shard_map(
        on_device,
        mesh=mesh,
        in_specs=(split_spec, P("dp")) + (whole,) * 15 + (split_spec,),
        out_specs=(split_spec, split_spec) + (whole,) * 15,
        check_vma=False,
    )
```

```python
import functools

import jax
import jax.numpy as jnp
from jax import lax
from jax.experimental import pallas as pl
from jax.experimental.pallas import tpu as pltpu
from jax.sharding import PartitionSpec as P

NORM_EPSILON = 1e-05
F32 = jnp.float32
BF16 = jnp.bfloat16
PRECISE = lax.Precision.HIGHEST
SERIES = 16
GROUP = 16
LINK_SEMS = 128
VMEM = pltpu.VMEM


def iota(shape, axis):
    return lax.broadcasted_iota(jnp.int32, shape, axis)


def is_left(shape):
    half = shape[-1] // 2
    return iota(shape, len(shape) - 1) < half


def swap(v):
    return pltpu.roll(v, v.shape[-1] // 2, v.ndim - 1)


def times(v, const):
    return v * const[0] + swap(v) * const[1]


def split(v):
    high = v.astype(BF16)
    return high, (v - high.astype(F32)).astype(BF16)


def nn(a, b):
    return lax.dot_general(a, b, (((1,), (0,)), ((), ())), preferred_element_type=F32)


def nt(a, b):
    return lax.dot_general(a, b, (((1,), (1,)), ((), ())), preferred_element_type=F32)


def tn(a, b):
    return lax.dot_general(a, b, (((0,), (0,)), ((), ())), preferred_element_type=F32)


def cmul(a, b):
    return a[0] * b[0] - a[1] * b[1], a[0] * b[1] + a[1] * b[0]


def twice(v):
    return jnp.concatenate([v, v], axis=-1)


def pole_parts(log_step, log_rate, frequency):
    step = jnp.exp(log_step)
    rate = jnp.exp(twice(log_rate))
    pole = (-rate, step * twice(frequency))
    phi = (jnp.zeros_like(rate), jnp.zeros_like(rate))
    slope = (jnp.zeros_like(rate), jnp.zeros_like(rate))
    fact = [1.0]
    for k in range(1, SERIES + 2):
        fact.append(fact[-1] * k)
    for k in range(SERIES, -1, -1):
        phi = cmul(phi, pole)
        phi = (phi[0] + 1.0 / fact[k + 1], phi[1])
    for k in range(SERIES, 0, -1):
        slope = cmul(slope, pole)
        slope = (slope[0] + k / fact[k + 1], slope[1])
    grow = cmul(pole, phi)
    z = (1.0 + grow[0], grow[1])
    return step, rate, z, phi, slope


def as_const(value):
    sign = jnp.where(is_left(value[0].shape), -1.0, 1.0)
    return value[0], value[1] * sign


def packed(value):
    return jnp.where(is_left(value[0].shape), value[0], value[1])


def ssm_setup(rows, ssm, consts, base):
    log_step, log_rate, frequency, coef = ssm
    step, rate, z, phi, slope = pole_parts(log_step, log_rate, frequency)
    b = (twice(coef[0]), twice(coef[1]))
    residue = cmul(b, (step * phi[0], step * phi[1]))
    power = (jnp.ones_like(rate), jnp.zeros_like(rate))
    for r in range(8):
        base[r] = packed(power)
        power = cmul(power, z)
    slot = 0

    def keep(value):
        nonlocal slot
        c = as_const(value)
        consts[2 * slot] = c[0]
        consts[2 * slot + 1] = c[1]
        slot += 1

    for k in range(4):
        keep(power)
        power = cmul(power, power)
    for k in range((rows - 1).bit_length()):
        keep(power)
        power = cmul(power, power)
    lead = cmul(residue, z)
    lead = (2.0 * lead[0], 2.0 * lead[1])
    sign = jnp.where(is_left(rate.shape), 1.0, -1.0)
    consts[2 * slot] = lead[0] * sign
    consts[2 * slot + 1] = -lead[1]
    slot += 1
    kern = jnp.where(is_left(rate.shape), 2.0 * residue[0], -2.0 * residue[1])
    kern_high = kern.astype(BF16).astype(F32)
    consts[2 * slot] = kern_high
    consts[2 * slot + 1] = kern - kern_high
    return slot


def row_of(ref, index, chan):
    return ref[index, pl.ds(chan, 1), :]


def const_of(consts, slot, chan):
    return row_of(consts, 2 * slot, chan), row_of(consts, 2 * slot + 1, chan)


def make_powers(group, chans, consts, kern_slot, base_flat, q_ref, taps_ref):
    every = [base_flat[pl.ds(chan, 8, stride=chans), :] for chan in group]
    for k in range(4):
        every = [
            jnp.concatenate([powers, times(powers, const_of(consts, k, chan))], axis=0)
            for chan, powers in zip(group, every)
        ]
    parts = [split(powers) for powers in every]
    for chan, (high, rest) in zip(group, parts):
        q_ref[chan, :128, :] = high
        q_ref[chan, 128:, :] = rest
    kerns = []
    for chan, (high, rest) in zip(group, parts):
        taps = [row_of(consts, 2 * kern_slot + k, chan) for k in range(2)]
        taps = jnp.concatenate([taps[0], taps[1]], axis=0).astype(BF16)
        kerns.append(nt(twice(taps), jnp.concatenate([high, rest], axis=1)))
    for chan, kern in zip(group, kerns):
        taps_ref[pl.ds(chan, 1), :] = kern[0:1] + kern[1:2]


def shift_taps(skip, taps_ref, base):
    taps = taps_ref[...]
    taps = taps + jnp.where(iota(taps.shape, 1) == 0, skip, 0.0)
    for r in range(8):
        base[r] = taps if r == 7 else pltpu.roll(taps, 7 - r, 1)


def make_band(group, chans, base_flat, t_ref):
    for chan in group:
        tile = base_flat[pl.ds(chan, 8, stride=chans), :]
        band = jnp.concatenate([pltpu.roll(tile, 120 - 8 * m, 1) if m < 15 else tile for m in range(16)], axis=0)
        band = jnp.where(iota((128, 128), 0) + iota((128, 128), 1) >= 127, band, 0.0)
        t_high, t_rest = split(band)
        t_ref[chan, :128, :] = t_high
        t_ref[chan, 128:, :] = t_rest


def scan(values, consts, first, group, reverse):
    rows = values[0].shape[0]
    places = iota(values[0].shape, 0)

    def moved(x, d):
        if reverse:
            return jnp.where(places < rows - d, pltpu.roll(x, rows - d, 0), 0.0)
        return jnp.where(places >= d, pltpu.roll(x, d, 0), 0.0)

    values = [moved(v, 1) for v in values]
    d, k = 1, 0
    while d < rows:
        values = [v + times(moved(v, d), const_of(consts, first + k, chan)) for v, chan in zip(values, group)]
        d, k = 2 * d, k + 1
    return values


def wide(chan, q_ref, t_ref):
    return jnp.concatenate([q_ref[chan], t_ref[chan]], axis=1)


def far_parts(states, consts, lead_slot, group, q_ref):
    rows = states[0].shape[0]
    outs = []
    for chan, state in zip(group, states):
        high, rest = split(times(state, const_of(consts, lead_slot, chan)))
        both = twice(jnp.concatenate([high, rest], axis=0))
        outs.append(nt(both, jnp.concatenate([q_ref[chan, :128, :], q_ref[chan, 128:, :]], axis=1)))
    return [out[:rows] + out[rows:] for out in outs]


def forward_group(group, chans, rows, consts, lead_slot, x_flat, q_ref, t_ref, h_ref, y_flat):
    outs = [
        nn(twice(x_flat[pl.ds(chan, rows, stride=chans), :].astype(BF16)), wide(chan, q_ref, t_ref))
        for chan in group
    ]
    states = scan([out[:, :128] for out in outs], consts, 4, group, False)
    for chan, state in zip(group, states):
        h_ref[chan] = state
    fars = far_parts(states, consts, lead_slot, group, q_ref)
    for chan, out, far in zip(group, outs, fars):
        y_flat[pl.ds(chan, rows, stride=chans), :] = out[:, 128:] + far


def backward_group(group, chans, rows, consts, lead_slot, x_flat, dy_flat, q_ref, t_ref, h_ref, dx_flat, a_ref, b_ref, g_ref):
    places = iota((1, 128), 1).astype(F32)
    us = [x_flat[pl.ds(chan, rows, stride=chans), :] for chan in group]
    dys = [dy_flat[pl.ds(chan, rows, stride=chans), :] for chan in group]
    outs = []
    for chan, u, dy in zip(group, us, dys):
        high = dy.astype(BF16).astype(F32)
        left = twice(jnp.concatenate([high, dy - high, dy * places, u * places], axis=0).astype(BF16))
        outs.append(nn(left, wide(chan, q_ref, t_ref)))
    pairs = [tn(u.astype(BF16), dy.astype(BF16)) for u, dy in zip(us, dys)]
    d0s = [out[:rows, :128] + out[rows : 2 * rows, :128] for out in outs]
    d1s = [out[2 * rows : 3 * rows, :128] for out in outs]
    hs = [h_ref[chan] for chan in group]
    ends = scan(d0s, consts, 4, group, True)
    fars = far_parts(ends, consts, lead_slot, group, q_ref)
    for chan, out, far in zip(group, outs, fars):
        dx_flat[pl.ds(chan, rows, stride=chans), :] = out[:rows, 128:] + out[rows : 2 * rows, 128:] + far
    h1s = scan(
        [out[3 * rows :, :128] + 128.0 * times(h, const_of(consts, 4, chan)) for chan, out, h in zip(group, outs, hs)],
        consts, 4, group, False,
    )
    mask = is_left(hs[0].shape)

    def prod(p, q):
        q_swap = swap(q)
        return p * jnp.where(mask, q, q_swap) + swap(p) * jnp.where(mask, -q_swap, q)

    for chan, d0, d1, h, h1 in zip(group, d0s, d1s, hs, h1s):
        a_far = jnp.sum(prod(d0, h), axis=0, keepdims=True)
        b_far = a_far + jnp.sum(prod(d1, h) + prod(d0, h1), axis=0, keepdims=True)
        a_ref[pl.ds(chans + chan, 1), :] = a_far
        b_ref[pl.ds(chans + chan, 1), :] = b_far
    keep = iota((128, 128), 1) <= iota((128, 128), 0)
    for chan, pair in zip(group, pairs):
        skew = jnp.where(keep, pltpu.roll(pair, 1, 1, stride=1, stride_axis=0), 0.0)
        g_ref[pl.ds(chan, 1), :] = jnp.sum(skew, axis=0, keepdims=True)


def split_lags(g_ref, base):
    lags = g_ref[...]
    weighted = lags * iota(lags.shape, 1).astype(F32)
    for k, v in enumerate((lags, weighted)):
        high = v.astype(BF16).astype(F32)
        base[k] = high
        base[2 + k] = v - high
        base[4 + k] = jnp.zeros_like(v)
        base[6 + k] = jnp.zeros_like(v)


def near_sums(group, chans, base_flat, q_ref, a_ref, b_ref):
    outs = [nn(twice(base_flat[pl.ds(chan, 8, stride=chans), :].astype(BF16)), q_ref[chan]) for chan in group]
    for chan, out in zip(group, outs):
        a_ref[pl.ds(chan, 1), :] = out[0:1] + out[2:3]
        b_ref[pl.ds(chan, 1), :] = out[1:2] + out[3:4]


def groups(chans, size, body):
    size = min(size, chans)

    def step(k, carry):
        body([k * size + i for i in range(size)])
        return carry

    lax.fori_loop(0, chans // size, step, 0)


def finish(chans, ssm, a_ref, b_ref, g_ref):
    log_step, log_rate, frequency, coef = ssm
    step, rate, z, phi, slope = pole_parts(log_step, log_rate, frequency)
    b = (twice(coef[0]), twice(coef[1]))

    def dup(v):
        left = is_left(v.shape)
        moved = swap(v)
        return jnp.where(left, v, moved), jnp.where(left, moved, v)

    def total(ref):
        near, far = dup(ref[:chans, :]), dup(ref[chans:, :])
        far = cmul(far, z)
        return near[0] + far[0], near[1] + far[1]

    a, bb = total(a_ref), total(b_ref)
    residue = cmul(b, (step * phi[0], step * phi[1]))
    g_res = (2.0 * a[0], -2.0 * a[1])
    rb = cmul(residue, bb)
    g_pole = (2.0 * rb[0], -2.0 * rb[1])
    conj = lambda v: (v[0], -v[1])
    g_coef = cmul(conj((step * phi[0], step * phi[1])), g_res)
    bs = cmul(b, (step * slope[0], step * slope[1]))
    more = cmul(conj(bs), g_res)
    g_pole = (g_pole[0] + more[0], g_pole[1] + more[1])
    d_rate = -rate * g_pole[0]
    d_freq = step * g_pole[1]
    by_step = cmul(conj(cmul(b, phi)), g_res)[0] + g_pole[1] * twice(frequency)
    left = is_left(by_step.shape)
    d_step = step * jnp.sum(jnp.where(left, by_step, 0.0), axis=1, keepdims=True)
    return jnp.where(left, d_rate, d_freq), jnp.where(left, g_coef[0], g_coef[1]), d_step, g_ref[:, 0:1]


def n_consts(rows):
    return 2 * (4 + (rows - 1).bit_length() + 2)


def gelu_parts(v):
    scale = 0.7978845608028654
    square = v * v
    bend = jnp.tanh(scale * v * (1.0 + 0.044715 * square))
    half = 0.5 + 0.5 * bend
    slope = half + 0.5 * v * (1.0 - bend * bend) * (scale * (1.0 + 0.134145 * square))
    return v * half, slope


def layer_norm(values, gain, shift):
    center = values - jnp.mean(values, axis=-1, keepdims=True)
    scale = lax.rsqrt(jnp.mean(center * center, axis=-1, keepdims=True) + NORM_EPSILON)
    normed = center * scale
    return normed * gain + shift, normed, scale


def norm_back(grad_out, gain, normed, scale):
    scaled = grad_out * gain
    return scale * (
        scaled
        - jnp.mean(scaled, axis=-1, keepdims=True)
        - normed * jnp.mean(scaled * normed, axis=-1, keepdims=True)
    )


def token_sum(values):
    return jnp.sum(values, axis=0, keepdims=True)


class Links:
    def __init__(self, send, recv, n_dp, n_blk):
        self.send, self.recv, self.used, self.open = send, recv, 0, []
        self.n_dp, self.n_blk = n_dp, n_blk
        self.dp, self.blk = lax.axis_index("dp"), lax.axis_index("blk")

    def dp_peer(self, mask):
        return jnp.bitwise_xor(self.dp, mask)

    def blk_peer(self, mask):
        return jnp.bitwise_xor(self.blk, mask)

    def copy(self, src, dst, dp_mask, blk_mask):
        copy = pltpu.make_async_remote_copy(
            src_ref=src,
            dst_ref=dst,
            send_sem=self.send.at[self.used],
            recv_sem=self.recv.at[self.used],
            device_id=(self.dp_peer(dp_mask), self.blk_peer(blk_mask)),
            device_id_type=pl.DeviceIdType.MESH,
        )
        copy.start()
        self.used += 1
        self.open.append(copy)
        return copy

    def greet(self):
        barrier = pltpu.get_barrier_semaphore()
        for mask in range(1, self.n_dp):
            pl.semaphore_signal(
                barrier, inc=1, device_id=(self.dp_peer(mask), self.blk), device_id_type=pl.DeviceIdType.MESH
            )
        for mask in range(1, self.n_blk):
            pl.semaphore_signal(
                barrier, inc=1, device_id=(self.dp, self.blk_peer(mask)), device_id_type=pl.DeviceIdType.MESH
            )

    def meet(self):
        pl.semaphore_wait(pltpu.get_barrier_semaphore(), self.n_dp + self.n_blk - 2)

    def finish(self):
        for copy in self.open:
            copy.wait_send()

    def exchange(self, src, dst):
        copies = [
            self.copy(src.at[self.blk_peer(mask)], dst.at[self.blk], 0, mask) for mask in range(1, self.n_blk)
        ]
        dst[self.blk] = src[self.blk]
        return copies


def wait_all(copies):
    for copy in copies:
        copy.wait_recv()


class Gather:
    def __init__(self, links, buf):
        self.links, self.buf, self.got = links, buf, {}
        self.bits = [1 << k for k in range(links.n_dp.bit_length() - 1)]
        self.forward(0)

    def forward(self, mask):
        low = mask & -mask if mask else self.links.n_dp
        if mask:
            self.got[mask].wait_recv()
        slot = self.buf.at[self.links.dp_peer(mask)]
        for bit in reversed(self.bits):
            if bit < low:
                self.got[mask | bit] = self.links.copy(slot, slot, bit, 0)

    def relay(self):
        for mask in sorted(range(1, self.links.n_dp), key=lambda m: bin(m).count("1")):
            self.forward(mask)


class Chunk:
    def __init__(self, links, part, landing, view, order, late):
        self.links, self.part, self.landing, self.view = links, part, landing, view
        self.order, self.late = order, late
        self.rows = part.shape[0]
        self.walk = self.steps()

    def advance(self):
        next(self.walk, None)

    def steps(self):
        links, part = self.links, self.part
        low, size, lows = 0, self.rows, []
        for k, bit in enumerate(self.order):
            half = size // 2
            mine = (links.blk // bit) % 2
            keep = pl.multiple_of(low + mine * half, 8)
            away = pl.multiple_of(low + (1 - mine) * half, 8)
            slot = self.landing.at[pl.ds(self.rows - size, half), :]
            copy = links.copy(part.at[pl.ds(away, half), :], slot, 0, bit)
            yield
            copy.wait_recv()
            lows.append(low)
            low, size = keep, half
            total = part[pl.ds(low, size), :] + slot[...]
            if k + 1 < len(self.order):
                part[pl.ds(low, size), :] = total
            else:
                self.view(0, low, size)[...] = total
        held = [0]
        dp_bits = [1 << k for k in range(1, links.n_dp.bit_length() - 1)]
        plan = [("blk", bit) for bit in reversed(self.order)]
        plan = plan[: self.late] + [("dp", bit) for bit in dp_bits] + plan[self.late :]
        if links.n_dp > 1:
            plan.append(("dp", 1))
        for axis, bit in plan:
            place = [self.view(mask, low, size) for mask in held]
            if axis == "blk":
                copies = [links.copy(v, v, 0, bit) for v in place]
                low, size = lows.pop(), size * 2
            else:
                copies = [links.copy(v, v, bit, 0) for v in place]
                held = held + [mask | bit for mask in held]
            yield
            wait_all(copies)


VEC_ROWS = 16


def whole_kernel(
    n_dp, n_blk, x_ref, lengths, cot_ref, n1g, n1b, log_step, log_rate, frequency, out_coef, skip_gain, glu_hbm, glu_b,
    n2g, n2b, in_hbm, in_b, out_hbm, out_b,
    block_out, grad_in, grad_glu_out, grad_in_out, grad_out_out, vec_out, rate_out, freq_out, coef_out,
    send_sems, recv_sems, load_sems, glu_w, ffn_in, ffn_out, rate_own, freq_own, coef_own, columns,
    a_send, x_all, y_send, y_all, dy_send, dy_all, dx_send, dx_all,
    q_ref, t_ref, h_ref, consts, base, taps, a_ref, b_ref, g_ref,
    result_all, gelu_all, feed_all, dglu, dglu_all, hidden_grad, slice_grad, hidden_s, pre_s, conv_keep, unit_keep, residual_keep, gate_keep,
    acc_out, acc_feed, residual_grad,
    part_glu, part_in0, part_in1, part_out0, part_out1, land_glu, land_in0, land_in1, land_out0, land_out1,
    sum_glu, sum_in, sum_out, own_par, dp_par, sum_par, blk_par, all_par, vec, dp_vec, sum_vec, blk_vec,
):
    rows, width = x_ref.shape
    ff = ffn_in.shape[1]
    chans = width // n_blk
    quarter = chans // n_dp
    links = Links(send_sems, recv_sems, n_dp, n_blk)
    dp, blk = links.dp, links.blk
    first = pl.multiple_of(blk * chans, 8)

    loads = [
        pltpu.make_async_copy(src, dst, load_sems.at[k])
        for k, (src, dst) in enumerate([
            (log_rate.at[pl.ds(first, chans), :], rate_own),
            (frequency.at[pl.ds(first, chans), :], freq_own),
            (out_coef.at[:, pl.ds(first, chans), :], coef_own),
            (out_hbm, ffn_out),
            (glu_hbm, glu_w),
            (in_hbm, ffn_in),
        ])
    ]
    for load in loads:
        load.start()
    links.greet()

    places = blk * rows + iota((rows, 1), 0)
    live = (places < lengths[0]).astype(F32)
    inputs = x_ref[...].astype(F32)
    normed, unit, scale1 = layer_norm(inputs, n1g[...], n1b[...])
    unit_keep[...] = unit
    mixed = normed.astype(BF16) * live.astype(BF16)
    flip = jnp.where(iota((rows, rows), 0) + iota((rows, rows), 1) == rows - 1, 1.0, 0.0).astype(BF16)
    a_send[...] = nn(flip, mixed).T
    links.meet()
    to_x = links.exchange(a_send.reshape(n_blk, chans, rows), x_all)
    cot = cot_ref[...].astype(F32)
    result = live * cot
    result_all[dp] = result
    gather_result = Gather(links, result_all)

    columns[0] = jnp.broadcast_to(log_step[...], (128, width)).T
    columns[1] = jnp.broadcast_to(skip_gain[...], (128, width)).T
    own_step = columns[0, pl.ds(first, chans), :]
    own_skip = columns[1, pl.ds(first, chans), :]
    for load in loads[:3]:
        load.wait()

    def ssm():
        return columns[0, pl.ds(first, chans), :], rate_own[...], freq_own[...], (coef_own[0], coef_own[1])

    kern_slot = ssm_setup(n_blk, ssm(), consts, base)
    lead_slot = kern_slot - 1
    base_flat = base.reshape(8 * chans, 128)
    groups(chans, GROUP, lambda group: make_powers(group, chans, consts, kern_slot, base_flat, q_ref, taps))
    shift_taps(own_skip, taps, base)
    groups(chans, GROUP, lambda group: make_band(group, chans, base_flat, t_ref))

    x_flat = x_all.reshape(n_blk * chans, 128)
    y_flat = y_send.reshape(n_blk * chans, 128)
    wait_all(to_x)
    groups(chans, GROUP, lambda group: forward_group(group, chans, n_blk, consts, lead_slot, x_flat, q_ref, t_ref, h_ref, y_flat))
    to_y = links.exchange(y_send, y_all)

    gather_result.relay()
    loads[3].wait()
    low = result.astype(BF16)
    step = ff // 4
    for k in range(4):
        hidden_grad[:, k * step : (k + 1) * step] = nt(low, ffn_out[k * step : (k + 1) * step, :])
    part_ff = ff // n_dp
    rows_s = pl.multiple_of(dp * part_ff, 128)
    out_slice = ffn_out[pl.ds(rows_s, part_ff), :]
    for k in range(n_dp):
        slice_grad[k * rows : (k + 1) * rows, :] = nt(result_all[k].astype(BF16), out_slice)
    loads[4].wait()
    loads[5].wait()

    wait_all(to_y)
    conv = y_all.reshape(width, rows)[...].T
    gelu_out, gelu_slope = gelu_parts(conv)
    conv_keep[...] = gelu_slope
    gelu_low = gelu_out.astype(BF16)
    gelu_all[dp] = gelu_low.astype(F32)
    gather_gelu = Gather(links, gelu_all)
    glu_pre = nn(gelu_low, glu_w[...]) + glu_b[...]
    left = glu_pre[:, :width]
    gate = 0.5 + 0.5 * jnp.tanh(0.5 * glu_pre[:, width:])
    gate_keep[0] = left
    gate_keep[1] = gate
    residual = x_ref[...].astype(F32) + live * left * gate
    normed_mid, unit_mid, scale_mid = layer_norm(residual, n2g[...], n2b[...])
    feed = normed_mid.astype(BF16)
    feed_all[dp] = feed.astype(F32)
    gather_feed = Gather(links, feed_all)
    residual_keep[0] = residual
    residual_keep[1] = unit_mid

    for k in range(4):
        cut = slice(k * step, (k + 1) * step)
        hidden, slope = gelu_parts(nn(feed, ffn_in[:, cut]) + in_b[:, cut])
        grad_pre = (hidden_grad[:, cut] * slope).astype(BF16)
        forward = nn(hidden.astype(BF16), ffn_out[cut, :])
        back = nt(grad_pre, ffn_in[:, cut])
        acc_out[...] = forward if k == 0 else acc_out[...] + forward
        acc_feed[...] = back if k == 0 else acc_feed[...] + back
        vec[7 + k : 8 + k, :] = token_sum(grad_pre.astype(F32))
    gather_gelu.relay()
    gather_feed.relay()

    in_slice = ffn_in[:, pl.ds(rows_s, part_ff)]
    in_b_slice = in_b[:, pl.ds(rows_s, part_ff)]
    for k in range(n_dp):
        hidden, slope = gelu_parts(nn(feed_all[k].astype(BF16), in_slice) + in_b_slice)
        cut = slice(k * rows, (k + 1) * rows)
        hidden_s[cut, :] = hidden.astype(BF16)
        pre_s[cut, :] = (slice_grad[cut, :] * slope).astype(BF16)
    half = width // 2
    results = result_all[...].reshape(n_dp * rows, width).astype(BF16)

    def out_view(piece):
        def view(mask, row, size):
            at = pl.multiple_of(links.dp_peer(mask) * part_ff + row, 8)
            return sum_out.at[pl.ds(at, size), pl.ds(piece * half, half)]
        return view

    half_ff = part_ff // 2

    def in_view(piece):
        def view(mask, row, size):
            at = pl.multiple_of(links.dp_peer(mask) * part_ff + piece * half_ff, 128)
            return sum_in.at[pl.ds(pl.multiple_of(row, 8), size), pl.ds(at, half_ff)]
        return view

    part_gl = 2 * width // n_dp

    def glu_view(mask, row, size):
        at = pl.multiple_of(links.dp_peer(mask) * part_gl, 128)
        return sum_glu.at[pl.ds(pl.multiple_of(row, 8), size), pl.ds(at, part_gl)]

    bits = [1 << k for k in range(n_blk.bit_length() - 1)]
    orders = [(bits, 2), ([bits[1], bits[0]] + bits[2:], len(bits))]

    part_out0[...] = tn(hidden_s[...], results[:, :half])
    out0 = Chunk(links, part_out0, land_out0, out_view(0), *orders[0])
    out0.advance()
    part_out1[...] = tn(hidden_s[...], results[:, half:])
    out1 = Chunk(links, part_out1, land_out1, out_view(1), *orders[1])
    out1.advance()
    feeds = feed_all[...].reshape(n_dp * rows, width).astype(BF16)
    part_in0[...] = tn(feeds, pre_s[:, :half_ff])
    in0 = Chunk(links, part_in0, land_in0, in_view(0), *orders[0])
    in0.advance()
    part_in1[...] = tn(feeds, pre_s[:, half_ff:])
    in1 = Chunk(links, part_in1, land_in1, in_view(1), *orders[1])
    in1.advance()

    grad_feed = acc_feed[...]
    unit_mid = residual_keep[1]
    vec[2:3, :] = token_sum(grad_feed * unit_mid)
    vec[3:4, :] = token_sum(grad_feed)
    vec[4:5, :] = token_sum(result)
    grad_res = cot_ref[...].astype(F32) + norm_back(grad_feed, n2g[...], unit_mid, scale_mid)
    residual_grad[...] = grad_res
    grad_left = live * grad_res
    left, gate = gate_keep[0], gate_keep[1]
    dglu[:, :width] = (grad_left * gate).astype(BF16).astype(F32)
    dglu[:, width:] = (grad_left * left * gate * (1.0 - gate)).astype(BF16).astype(F32)
    to_glu = []
    for mask in range(1, n_dp):
        at = pl.multiple_of(links.dp_peer(mask) * part_gl, 128)
        to_glu.append(links.copy(dglu.at[:, pl.ds(at, part_gl)], dglu_all.at[dp], mask, 0))
    dglu_all[dp] = dglu[:, pl.ds(pl.multiple_of(dp * part_gl, 128), part_gl)]
    vec[5:6, :] = token_sum(dglu[:, :width])
    vec[6:7, :] = token_sum(dglu[:, width:])
    grad_gelu = nt(dglu[...].astype(BF16), glu_w[...])
    dy_send[...] = (grad_gelu * conv_keep[...]).T
    to_dy = links.exchange(dy_send.reshape(n_blk, chans, rows), dy_all)
    block_out[...] = (residual_keep[0] + live * (acc_out[...] + out_b[...])).astype(BF16)

    out0.advance()
    out1.advance()
    wait_all(to_glu)
    gelus = gelu_all[...].reshape(n_dp * rows, width).astype(BF16)
    part_glu[...] = tn(gelus, dglu_all[...].reshape(n_dp * rows, part_gl).astype(BF16))
    glu = Chunk(links, part_glu, land_glu, glu_view, *orders[0])
    glu.advance()
    in0.advance()
    in1.advance()
    out0.advance()
    out1.advance()

    wait_all(to_dy)
    dy_flat = dy_all.reshape(n_blk * chans, 128)
    dx_flat = dx_send.reshape(n_blk * chans, 128)
    groups(chans, GROUP, lambda group: backward_group(group, chans, n_blk, consts, lead_slot, x_flat, dy_flat, q_ref, t_ref, h_ref, dx_flat, a_ref, b_ref, g_ref))
    to_dx = links.exchange(dx_send, dx_all)
    for chunk in (in0, in1, glu, out0, out1):
        chunk.advance()
    split_lags(g_ref, base)
    groups(chans, GROUP, lambda group: near_sums(group, chans, base_flat, q_ref, a_ref, b_ref))
    rate_freq, coefs, d_step, d_skip = finish(chans, ssm(), a_ref, b_ref, g_ref)
    own_par[:, 0, :] = rate_freq
    own_par[:, 1, :] = coefs
    pair = jnp.where(iota((chans, 128), 1) == 0, d_step, jnp.where(iota((chans, 128), 1) == 1, d_skip, 0.0))
    if chans < 128:
        pair = jnp.concatenate([pair, jnp.zeros((128 - chans, 128), F32)], axis=0)
    pair = pair.T[0:8]
    if width > 128:
        pair = jnp.concatenate([pair, jnp.zeros((8, width - 128), F32)], axis=1)
    pair = pltpu.roll(pair, blk * chans, 1)
    vec[11:13, :] = pair[0:2]
    vec[13:16, :] = jnp.zeros((3, width), F32)
    for chunk in (in0, in1, glu, out0, out1):
        chunk.advance()

    wait_all(to_dx)
    back = dx_all.reshape(width, rows)[...].T
    high, rest = split(back)
    rest, last = split(back - high.astype(F32))
    grad_normed = live * (nn(flip, high) + (nn(flip, rest) + nn(flip, last)))
    unit = unit_keep[...]
    vec[0:1, :] = token_sum(grad_normed * unit)
    vec[1:2, :] = token_sum(grad_normed)
    grad_in[...] = residual_grad[...] + norm_back(grad_normed, n1g[...], unit, scale1)

    waits = []
    for mask in range(1, n_dp):
        at = links.dp_peer(mask) * quarter
        waits.append(links.copy(own_par.at[pl.ds(at, quarter)], dp_par.at[dp], mask, 0))
        waits.append(links.copy(vec, dp_vec.at[dp], mask, 0))
    dp_par[dp] = own_par[pl.ds(dp * quarter, quarter)]
    dp_vec[dp] = vec[...]
    for chunk in (in0, in1, glu, out0, out1):
        chunk.advance()
    wait_all(waits)
    sum_par[...] = sum_slots(dp_par, n_dp)
    sum_vec[...] = sum_slots(dp_vec, n_dp)
    waits = []
    for mask in range(1, n_blk):
        waits.append(links.copy(sum_par, blk_par.at[blk], 0, mask))
        waits.append(links.copy(sum_vec, blk_vec.at[blk], 0, mask))
    blk_par[blk] = sum_par[...]
    blk_vec[blk] = sum_vec[...]
    for chunk in (in0, in1, glu, out0, out1):
        chunk.advance()
    wait_all(waits)
    all_par[dp] = blk_par[...]
    gather_par = Gather(links, all_par)
    vec_out[...] = sum_slots(blk_vec, n_blk)
    for chunk in (in0, in1, glu, out0, out1):
        chunk.advance()
    gather_par.relay()
    state = rate_out.shape[1]
    for b in range(n_blk):
        for d in range(n_dp):
            at = b * chans + d * quarter
            block = all_par[d, b]
            rate_out[at : at + quarter, :] = block[:, 0, :state]
            freq_out[at : at + quarter, :] = block[:, 0, state:]
            coef_out[0, at : at + quarter, :] = block[:, 1, :state]
            coef_out[1, at : at + quarter, :] = block[:, 1, state:]
    for _ in range(8):
        for chunk in (in0, in1, glu, out0, out1):
            chunk.advance()
    stores = [
        pltpu.make_async_copy(src, dst, load_sems.at[k])
        for k, (src, dst) in enumerate([(sum_glu, grad_glu_out), (sum_in, grad_in_out), (sum_out, grad_out_out)])
    ]
    for store in stores:
        store.start()
    links.finish()
    for store in stores:
        store.wait()


def sum_slots(ref, count):
    total = ref[0]
    for k in range(1, count):
        total = total + ref[k]
    return total


def on_device(n_dp, n_blk, block_in, seq_lengths, norm1_gain, norm1_bias, log_step, log_rate, frequency, out_coef, skip_gain, glu_weight, glu_bias, norm2_gain, norm2_bias, ffn_in, ffn_in_bias, ffn_out, ffn_out_bias, cotangent):
    _, rows, width = block_in.shape
    ff = ffn_in.shape[1]
    states = log_rate.shape[1]
    chans, quarter = width // n_blk, width // n_blk // n_dp
    row = lambda v: v.reshape(1, -1)
    vmem, anywhere = pl.BlockSpec(memory_space=VMEM), pl.BlockSpec(memory_space=pl.ANY)
    shape = jax.ShapeDtypeStruct
    outs = [
        (shape((rows, width), BF16), vmem),
        (shape((rows, width), F32), vmem),
        (shape((width, 2 * width), F32), anywhere),
        (shape((width, ff), F32), anywhere),
        (shape((ff, width), F32), anywhere),
        (shape((VEC_ROWS, width), F32), vmem),
        (shape((width, states), F32), vmem),
        (shape((width, states), F32), vmem),
        (shape((2, width, states), F32), vmem),
    ]
    part_ff, part_gl = ff // n_dp, 2 * width // n_dp
    tokens = n_dp * rows
    parts = [(width, part_gl), (width, part_ff // 2), (width, part_ff // 2), (part_ff, width // 2), (part_ff, width // 2)]
    f32 = lambda *dims: VMEM(dims, F32)
    bf16 = lambda *dims: VMEM(dims, BF16)
    dma = lambda n: pltpu.SemaphoreType.DMA((n,))
    scratch = [
        dma(LINK_SEMS), dma(LINK_SEMS), dma(8),
        bf16(width, 2 * width), bf16(width, ff), bf16(ff, width),
        f32(chans, states), f32(chans, states), f32(2, chans, states), f32(2, width, 128),
        f32(width, rows), f32(n_blk, chans, rows), f32(n_blk, chans, rows), f32(n_blk, chans, rows),
        f32(width, rows), f32(n_blk, chans, rows), f32(n_blk, chans, rows), f32(n_blk, chans, rows),
        bf16(chans, 256, 128), bf16(chans, 256, 128), f32(chans, n_blk, 128), f32(n_consts(n_blk), chans, 128),
        f32(8, chans, 128), f32(chans, 128), f32(2 * chans, 128), f32(2 * chans, 128), f32(chans, 128),
        f32(n_dp, rows, width), f32(n_dp, rows, width), f32(n_dp, rows, width),
        f32(rows, 2 * width), f32(n_dp, rows, part_gl),
        f32(rows, ff), f32(tokens, part_ff), bf16(tokens, part_ff), bf16(tokens, part_ff),
        f32(rows, width), f32(rows, width), f32(2, rows, width), f32(2, rows, width),
        f32(rows, width), f32(rows, width), f32(rows, width),
        *[f32(*p) for p in parts], *[f32(*p) for p in parts],
        f32(width, 2 * width), f32(width, ff), f32(ff, width),
        f32(chans, 2, 128), f32(n_dp, quarter, 2, 128), f32(quarter, 2, 128), f32(n_blk, quarter, 2, 128), f32(n_dp, n_blk, quarter, 2, 128),
        f32(VEC_ROWS, width), f32(n_dp, VEC_ROWS, width), f32(VEC_ROWS, width), f32(n_blk, VEC_ROWS, width),
    ]
    out = pl.pallas_call(
        functools.partial(whole_kernel, n_dp, n_blk),
        out_shape=[o[0] for o in outs],
        out_specs=[o[1] for o in outs],
        in_specs=[vmem, pl.BlockSpec(memory_space=pltpu.SMEM), vmem, vmem, vmem, vmem, anywhere, anywhere, anywhere, vmem, anywhere, vmem, vmem, vmem, anywhere, vmem, anywhere, vmem],
        scratch_shapes=scratch,
        compiler_params=pltpu.CompilerParams(collective_id=0, has_side_effects=True, vmem_limit_bytes=60 * 2**20),
    )(
        block_in[0], seq_lengths, cotangent[0], row(norm1_gain), row(norm1_bias), row(log_step), log_rate, frequency, out_coef,
        row(skip_gain), glu_weight, row(glu_bias), row(norm2_gain), row(norm2_bias), ffn_in, row(ffn_in_bias), ffn_out, row(ffn_out_bias),
    )
    block_out, grad_in, g_glu, g_in, g_out, vec, rate, freq, coef = out
    return (
        block_out[None], grad_in[None], vec[0], vec[1], vec[11], rate, freq, coef, vec[12],
        g_glu, vec[5:7].reshape(-1), vec[2], vec[3], g_in, vec[7:11].reshape(-1), g_out, vec[4],
    )


def solution(mesh):
    split_spec, whole = P("dp", "blk", None), P()
    return jax.shard_map(
        functools.partial(on_device, mesh.shape["dp"], mesh.shape["blk"]),
        mesh=mesh,
        in_specs=(split_spec, P("dp")) + (whole,) * 15 + (split_spec,),
        out_specs=(split_spec, split_spec) + (whole,) * 15,
        check_vma=False,
    )
```

```python
import functools

import jax
import jax.numpy as jnp
from jax import lax
from jax.experimental import pallas as pl
from jax.experimental.pallas import tpu as pltpu
from jax.sharding import PartitionSpec as P

NORM_EPSILON = 1e-05
F32 = jnp.float32
BF16 = jnp.bfloat16
PRECISE = lax.Precision.HIGHEST
SERIES = 16
GROUP = 16
LINK_SEMS = 256
BIG_PARTS = 4
GLU_PLANS = (
    (("c", "y", "x", "z0", "z1"), 0),
    (("c", "z0", "y", "x", "z1"), 2),
)
FFN_PLANS = (
    (("x", "z0", "z1"), 3),
    (("x", "z0", "z1"), 2),
    (("x", "z0", "z1"), 3),
    (("x", "z0", "z1"), 2),
    (("x", "z1", "z0"), 3),
    (("x", "z0", "z1"), 3),
    (("x", "z0", "z1"), 2),
    (("x", "z0", "z1"), 3),
    (("x", "z0", "z1"), 1),
    (("z0", "x", "z1"), 3),
    (("x", "z0", "z1"), 1),
    (("x", "z1", "z0"), 1),
    (("z1", "x", "z0"), 3),
    (("x", "z0", "z1"), 3),
    (("z0", "x", "z1"), 2),
    (("x", "z0", "z1"), 2),
)
ORDER = (
    "own", "glubwd", "dy", "part0", "part1", 0, 1, "slice", "part2", "part3", "part4", "part5", "part6",
    "part7", "part8", "part9", "part10", "part11", 2, "part12", 0, "part13", 3, 1, "part14", "part15",
    "part16", 4, 11, 2, "part17", 5, 3, "bwd0", 6, 1, 7, 14, 16, 4, 8, 2, 5, 3, 9, 6, 7, 10, 4, 8, 12, 2,
    "bwd1", 5, 3, 9, 6, 0, 7, 10, 4, 13, 8, 12, 15, 2, 11, 5, 3, "bwd2", 6, 9, 17, 0, 1, 7, 14, 10, 16, 3, 4,
    2, 13, 8, "bwd3", 12, 15, 11, 5, 6, "near", 3, 9, 2, 17, 4, 0, 5, 1, 7, 14, 10, 3, 2, 13, 16, 8, 4, 0, 10,
    4, 6, 8, "ln1", 12, 15, 5, "s0", 11, 9, 7, 17, 6, 12, 5, 14, 1, 13, 16, 8, 6, "s1", 11, 9, 8, 0, 10, 14,
    15, 7, 17, 13, 1, 12, 16, 7, "s2", 9, 11, 10, 9, 1, 0, 10, 16, 12, 15, 17, 14, 12, "s3", 13, 11, 0, 17,
    15, 11, 1, 0, 14, 13, 1, 16, 14, 15, 13, 17, 16, 15, 17,
)
VMEM = pltpu.VMEM


def iota(shape, axis):
    return lax.broadcasted_iota(jnp.int32, shape, axis)


def is_left(shape):
    half = shape[-1] // 2
    return iota(shape, len(shape) - 1) < half


def swap(v):
    return pltpu.roll(v, v.shape[-1] // 2, v.ndim - 1)


def times(v, const):
    return v * const[0] + swap(v) * const[1]


def split(v):
    high = v.astype(BF16)
    return high, (v - high.astype(F32)).astype(BF16)


def nn(a, b):
    return lax.dot_general(a, b, (((1,), (0,)), ((), ())), preferred_element_type=F32)


def nt(a, b):
    return lax.dot_general(a, b, (((1,), (1,)), ((), ())), preferred_element_type=F32)


def tn(a, b):
    return lax.dot_general(a, b, (((0,), (0,)), ((), ())), preferred_element_type=F32)


def cmul(a, b):
    return a[0] * b[0] - a[1] * b[1], a[0] * b[1] + a[1] * b[0]


def twice(v):
    return jnp.concatenate([v, v], axis=-1)


def pole_parts(log_step, log_rate, frequency):
    step = jnp.exp(log_step)
    rate = jnp.exp(twice(log_rate))
    pole = (-rate, step * twice(frequency))
    phi = (jnp.zeros_like(rate), jnp.zeros_like(rate))
    slope = (jnp.zeros_like(rate), jnp.zeros_like(rate))
    fact = [1.0]
    for k in range(1, SERIES + 2):
        fact.append(fact[-1] * k)
    for k in range(SERIES, -1, -1):
        phi = cmul(phi, pole)
        phi = (phi[0] + 1.0 / fact[k + 1], phi[1])
    for k in range(SERIES, 0, -1):
        slope = cmul(slope, pole)
        slope = (slope[0] + k / fact[k + 1], slope[1])
    grow = cmul(pole, phi)
    z = (1.0 + grow[0], grow[1])
    return step, rate, z, phi, slope


def as_const(value):
    sign = jnp.where(is_left(value[0].shape), -1.0, 1.0)
    return value[0], value[1] * sign


def packed(value):
    return jnp.where(is_left(value[0].shape), value[0], value[1])


def ssm_setup(rows, ssm, consts, base):
    log_step, log_rate, frequency, coef = ssm
    step, rate, z, phi, slope = pole_parts(log_step, log_rate, frequency)
    b = (twice(coef[0]), twice(coef[1]))
    residue = cmul(b, (step * phi[0], step * phi[1]))
    power = (jnp.ones_like(rate), jnp.zeros_like(rate))
    for r in range(8):
        base[r] = packed(power)
        power = cmul(power, z)
    slot = 0

    def keep(value):
        nonlocal slot
        c = as_const(value)
        consts[2 * slot] = c[0]
        consts[2 * slot + 1] = c[1]
        slot += 1

    for k in range(4):
        keep(power)
        power = cmul(power, power)
    for k in range((rows - 1).bit_length()):
        keep(power)
        power = cmul(power, power)
    lead = cmul(residue, z)
    lead = (2.0 * lead[0], 2.0 * lead[1])
    sign = jnp.where(is_left(rate.shape), 1.0, -1.0)
    consts[2 * slot] = lead[0] * sign
    consts[2 * slot + 1] = -lead[1]
    slot += 1
    kern = jnp.where(is_left(rate.shape), 2.0 * residue[0], -2.0 * residue[1])
    kern_high = kern.astype(BF16).astype(F32)
    consts[2 * slot] = kern_high
    consts[2 * slot + 1] = kern - kern_high
    return slot


def row_of(ref, index, chan):
    return ref[index, pl.ds(chan, 1), :]


def const_of(consts, slot, chan):
    return row_of(consts, 2 * slot, chan), row_of(consts, 2 * slot + 1, chan)


def make_powers(group, chans, consts, kern_slot, base_flat, q_ref, taps_ref):
    every = [base_flat[pl.ds(chan, 8, stride=chans), :] for chan in group]
    for k in range(4):
        every = [
            jnp.concatenate([powers, times(powers, const_of(consts, k, chan))], axis=0)
            for chan, powers in zip(group, every)
        ]
    parts = [split(powers) for powers in every]
    for chan, (high, rest) in zip(group, parts):
        q_ref[chan, :128, :] = high
        q_ref[chan, 128:, :] = rest
    kerns = []
    for chan, (high, rest) in zip(group, parts):
        taps = [row_of(consts, 2 * kern_slot + k, chan) for k in range(2)]
        taps = jnp.concatenate([taps[0], taps[1]], axis=0).astype(BF16)
        kerns.append(nt(twice(taps), jnp.concatenate([high, rest], axis=1)))
    for chan, kern in zip(group, kerns):
        taps_ref[pl.ds(chan, 1), :] = kern[0:1] + kern[1:2]


def shift_taps(skip, taps_ref, base):
    taps = taps_ref[...]
    taps = taps + jnp.where(iota(taps.shape, 1) == 0, skip, 0.0)
    for r in range(8):
        base[r] = taps if r == 7 else pltpu.roll(taps, 7 - r, 1)


def make_band(group, chans, base_flat, t_ref):
    for chan in group:
        tile = base_flat[pl.ds(chan, 8, stride=chans), :]
        band = jnp.concatenate([pltpu.roll(tile, 120 - 8 * m, 1) if m < 15 else tile for m in range(16)], axis=0)
        band = jnp.where(iota((128, 128), 0) + iota((128, 128), 1) >= 127, band, 0.0)
        t_high, t_rest = split(band)
        t_ref[chan, :128, :] = t_high
        t_ref[chan, 128:, :] = t_rest


def scan(values, consts, first, group, reverse):
    rows = values[0].shape[0]
    places = iota(values[0].shape, 0)

    def moved(x, d):
        if reverse:
            return jnp.where(places < rows - d, pltpu.roll(x, rows - d, 0), 0.0)
        return jnp.where(places >= d, pltpu.roll(x, d, 0), 0.0)

    values = [moved(v, 1) for v in values]
    d, k = 1, 0
    while d < rows:
        values = [v + times(moved(v, d), const_of(consts, first + k, chan)) for v, chan in zip(values, group)]
        d, k = 2 * d, k + 1
    return values


def wide(chan, q_ref, t_ref):
    return jnp.concatenate([q_ref[chan], t_ref[chan]], axis=1)


def far_parts(states, consts, lead_slot, group, q_ref):
    rows = states[0].shape[0]
    outs = []
    for chan, state in zip(group, states):
        high, rest = split(times(state, const_of(consts, lead_slot, chan)))
        both = twice(jnp.concatenate([high, rest], axis=0))
        outs.append(nt(both, jnp.concatenate([q_ref[chan, :128, :], q_ref[chan, 128:, :]], axis=1)))
    return [out[:rows] + out[rows:] for out in outs]


def forward_group(group, chans, rows, consts, lead_slot, x_flat, q_ref, t_ref, h_ref, y_flat):
    outs = [
        nn(twice(x_flat[pl.ds(chan, rows, stride=chans), :].astype(BF16)), wide(chan, q_ref, t_ref))
        for chan in group
    ]
    states = scan([out[:, :128] for out in outs], consts, 4, group, False)
    for chan, state in zip(group, states):
        h_ref[chan] = state
    fars = far_parts(states, consts, lead_slot, group, q_ref)
    for chan, out, far in zip(group, outs, fars):
        y_flat[pl.ds(chan, rows, stride=chans), :] = out[:, 128:] + far


def backward_group(group, chans, rows, consts, lead_slot, x_flat, dy_flat, q_ref, t_ref, h_ref, dx_flat, a_ref, b_ref, g_ref):
    places = iota((1, 128), 1).astype(F32)
    us = [x_flat[pl.ds(chan, rows, stride=chans), :] for chan in group]
    dys = [dy_flat[pl.ds(chan, rows, stride=chans), :] for chan in group]
    outs = []
    for chan, u, dy in zip(group, us, dys):
        high = dy.astype(BF16).astype(F32)
        left = twice(jnp.concatenate([high, dy - high, dy * places, u * places], axis=0).astype(BF16))
        outs.append(nn(left, wide(chan, q_ref, t_ref)))
    pairs = [tn(u.astype(BF16), dy.astype(BF16)) for u, dy in zip(us, dys)]
    d0s = [out[:rows, :128] + out[rows : 2 * rows, :128] for out in outs]
    d1s = [out[2 * rows : 3 * rows, :128] for out in outs]
    hs = [h_ref[chan] for chan in group]
    ends = scan(d0s, consts, 4, group, True)
    fars = far_parts(ends, consts, lead_slot, group, q_ref)
    for chan, out, far in zip(group, outs, fars):
        dx_flat[pl.ds(chan, rows, stride=chans), :] = out[:rows, 128:] + out[rows : 2 * rows, 128:] + far
    h1s = scan(
        [out[3 * rows :, :128] + 128.0 * times(h, const_of(consts, 4, chan)) for chan, out, h in zip(group, outs, hs)],
        consts, 4, group, False,
    )
    mask = is_left(hs[0].shape)

    def prod(p, q):
        q_swap = swap(q)
        return p * jnp.where(mask, q, q_swap) + swap(p) * jnp.where(mask, -q_swap, q)

    for chan, d0, d1, h, h1 in zip(group, d0s, d1s, hs, h1s):
        a_far = jnp.sum(prod(d0, h), axis=0, keepdims=True)
        b_far = a_far + jnp.sum(prod(d1, h) + prod(d0, h1), axis=0, keepdims=True)
        a_ref[pl.ds(chans + chan, 1), :] = a_far
        b_ref[pl.ds(chans + chan, 1), :] = b_far
    keep = iota((128, 128), 1) <= iota((128, 128), 0)
    for chan, pair in zip(group, pairs):
        skew = jnp.where(keep, pltpu.roll(pair, 1, 1, stride=1, stride_axis=0), 0.0)
        g_ref[pl.ds(chan, 1), :] = jnp.sum(skew, axis=0, keepdims=True)


def split_lags(g_ref, base):
    lags = g_ref[...]
    weighted = lags * iota(lags.shape, 1).astype(F32)
    for k, v in enumerate((lags, weighted)):
        high = v.astype(BF16).astype(F32)
        base[k] = high
        base[2 + k] = v - high
        base[4 + k] = jnp.zeros_like(v)
        base[6 + k] = jnp.zeros_like(v)


def near_sums(group, chans, base_flat, q_ref, a_ref, b_ref):
    outs = [nn(twice(base_flat[pl.ds(chan, 8, stride=chans), :].astype(BF16)), q_ref[chan]) for chan in group]
    for chan, out in zip(group, outs):
        a_ref[pl.ds(chan, 1), :] = out[0:1] + out[2:3]
        b_ref[pl.ds(chan, 1), :] = out[1:2] + out[3:4]


def groups(first, count, body):
    size = min(GROUP, count)

    def step(k, carry):
        body([first + k * size + i for i in range(size)])
        return carry

    if count > 0:
        lax.fori_loop(0, count // size, step, 0)


def finish(chans, ssm, a_ref, b_ref, g_ref):
    log_step, log_rate, frequency, coef = ssm
    step, rate, z, phi, slope = pole_parts(log_step, log_rate, frequency)
    b = (twice(coef[0]), twice(coef[1]))

    def dup(v):
        left = is_left(v.shape)
        moved = swap(v)
        return jnp.where(left, v, moved), jnp.where(left, moved, v)

    def total(ref):
        near, far = dup(ref[:chans, :]), dup(ref[chans:, :])
        far = cmul(far, z)
        return near[0] + far[0], near[1] + far[1]

    a, bb = total(a_ref), total(b_ref)
    residue = cmul(b, (step * phi[0], step * phi[1]))
    g_res = (2.0 * a[0], -2.0 * a[1])
    rb = cmul(residue, bb)
    g_pole = (2.0 * rb[0], -2.0 * rb[1])
    conj = lambda v: (v[0], -v[1])
    g_coef = cmul(conj((step * phi[0], step * phi[1])), g_res)
    bs = cmul(b, (step * slope[0], step * slope[1]))
    more = cmul(conj(bs), g_res)
    g_pole = (g_pole[0] + more[0], g_pole[1] + more[1])
    d_rate = -rate * g_pole[0]
    d_freq = step * g_pole[1]
    by_step = cmul(conj(cmul(b, phi)), g_res)[0] + g_pole[1] * twice(frequency)
    left = is_left(by_step.shape)
    d_step = step * jnp.sum(jnp.where(left, by_step, 0.0), axis=1, keepdims=True)
    return jnp.where(left, d_rate, d_freq), jnp.where(left, g_coef[0], g_coef[1]), d_step, g_ref[:, 0:1]


def n_consts(rows):
    return 2 * (4 + (rows - 1).bit_length() + 2)


def gelu_parts(v):
    scale = 0.7978845608028654
    square = v * v
    bend = jnp.tanh(scale * v * (1.0 + 0.044715 * square))
    half = 0.5 + 0.5 * bend
    slope = half + 0.5 * v * (1.0 - bend * bend) * (scale * (1.0 + 0.134145 * square))
    return v * half, slope


def layer_norm(values, gain, shift):
    center = values - jnp.mean(values, axis=-1, keepdims=True)
    scale = lax.rsqrt(jnp.mean(center * center, axis=-1, keepdims=True) + NORM_EPSILON)
    normed = center * scale
    return normed * gain + shift, normed, scale


def norm_back(grad_out, gain, normed, scale):
    scaled = grad_out * gain
    return scale * (
        scaled
        - jnp.mean(scaled, axis=-1, keepdims=True)
        - normed * jnp.mean(scaled * normed, axis=-1, keepdims=True)
    )


def token_sum(values):
    return jnp.sum(values, axis=0, keepdims=True)


class Transfer:
    def __init__(self, copy):
        self.copy, self.arrived = copy, False

    def wait_recv(self):
        self.arrived = True
        self.copy.wait_recv()


class Load:
    def __init__(self, src, dst, sem):
        self.copy, self.done = pltpu.make_async_copy(src, dst, sem), False
        self.copy.start()

    def wait(self):
        if not self.done:
            self.done = True
            self.copy.wait()


class Links:
    def __init__(self, send, recv, n_dp, n_blk):
        self.send, self.recv, self.used, self.open = send, recv, 0, []
        self.n_dp, self.n_blk = n_dp, n_blk
        self.dp, self.blk = lax.axis_index("dp"), lax.axis_index("blk")

    def dp_peer(self, mask):
        return jnp.bitwise_xor(self.dp, mask)

    def blk_peer(self, mask):
        return jnp.bitwise_xor(self.blk, mask)

    def copy(self, src, dst, dp_mask, blk_mask):
        copy = pltpu.make_async_remote_copy(
            src_ref=src,
            dst_ref=dst,
            send_sem=self.send.at[self.used],
            recv_sem=self.recv.at[self.used],
            device_id=(self.dp_peer(dp_mask), self.blk_peer(blk_mask)),
            device_id_type=pl.DeviceIdType.MESH,
        )
        copy.start()
        self.used += 1
        copy = Transfer(copy)
        self.open.append(copy)
        return copy

    def greet(self):
        barrier = pltpu.get_barrier_semaphore()
        for mask in range(1, self.n_dp):
            pl.semaphore_signal(
                barrier, inc=1, device_id=(self.dp_peer(mask), self.blk), device_id_type=pl.DeviceIdType.MESH
            )
        for mask in range(1, self.n_blk):
            pl.semaphore_signal(
                barrier, inc=1, device_id=(self.dp, self.blk_peer(mask)), device_id_type=pl.DeviceIdType.MESH
            )

    def meet(self):
        pl.semaphore_wait(pltpu.get_barrier_semaphore(), self.n_dp + self.n_blk - 2)

    def finish(self):
        for transfer in self.open:
            transfer.copy.wait_send()

    def stop(self):
        for transfer in self.open:
            if not transfer.arrived:
                transfer.wait_recv()
        for load in self.loads:
            load.wait()
        self.finish()

    def exchange(self, src, dst, first, size):
        part = pl.ds(first, size)
        copies = [
            self.copy(src.at[self.blk_peer(mask), part], dst.at[self.blk, part], 0, mask)
            for mask in range(1, self.n_blk)
        ]
        dst[self.blk, part] = src[self.blk, part]
        return copies


def wait_all(copies):
    for copy in copies:
        copy.wait_recv()


class Gather:
    def __init__(self, links, buf):
        self.links, self.buf, self.got = links, buf, {}
        self.bits = [1 << k for k in range(links.n_dp.bit_length() - 1)]
        self.forward(0)

    def forward(self, mask):
        low = mask & -mask if mask else self.links.n_dp
        if mask:
            self.got[mask].wait_recv()
        slot = self.buf.at[self.links.dp_peer(mask)]
        for bit in reversed(self.bits):
            if bit < low:
                self.got[mask | bit] = self.links.copy(slot, slot, bit, 0)

    def relay(self):
        for mask in sorted(range(1, self.links.n_dp), key=lambda m: bin(m).count("1")):
            self.forward(mask)


def bit_names(n_dp, n_blk):
    blk = [("blk", 1 << k) for k in range(n_blk.bit_length() - 1)]
    dp = [("dp", 1 << k) for k in range(n_dp.bit_length() - 1)]
    return {"x": blk[:1], "z0": blk[1:2], "z1": blk[2:], "c": dp[:1], "y": dp[1:]}


class Chunk:
    def __init__(self, links, rows, part, out, landing, every, plan):
        names = bit_names(links.n_dp, links.n_blk)
        order, late = plan
        spread = lambda tokens: [bit for token in tokens for bit in names[token]]
        self.links, self.rows, self.part, self.out, self.landing = links, rows, part, out, landing
        self.halving = spread(order)
        back = [token for token in reversed(order) if token not in "cy"]
        back = back[:late] + ["y"] + back[late:] + ["c"]
        self.doubling = []
        for token in back:
            bits = names[token]
            self.doubling += bits if token in "cy" else bits[::-1]
        self.held = list(range(links.n_dp)) if every else [0]
        self.walk = self.steps()
        self.live = True

    def advance(self):
        self.live = next(self.walk, "end") != "end"

    def steps(self):
        links = self.links
        held, low, size, lows, at = self.held, 0, self.rows, [], 0
        for k, (axis, bit) in enumerate(self.halving):
            last = k + 1 == len(self.halving)
            if axis == "blk":
                half = size // 2
                mine = (links.blk // bit) % 2
                keep = pl.multiple_of(low + mine * half, 8)
                away = pl.multiple_of(low + (1 - mine) * half, 8)
                moves = [(mask, mask, away) for mask in held]
                lows.append(low)
                low, size = keep, half
            else:
                moves = [(mask, mask ^ bit, low) for mask in held if mask & bit]
                held = [mask for mask in held if not mask & bit]
            slots, copies = {}, []
            for mask, there, row in moves:
                slots[there] = self.landing.at[pl.ds(at, size), :]
                at += size
                dp_mask, blk_mask = (0, bit) if axis == "blk" else (bit, 0)
                copies.append(links.copy(self.part(mask, row, size), slots[there], dp_mask, blk_mask))
            yield
            wait_all(copies)
            for mask in held:
                own = self.part(mask, low, size)
                goal = self.out(mask, low, size) if last else own
                goal[...] = own[...] + slots[mask][...]
        for axis, bit in self.doubling:
            place = [self.out(mask, low, size) for mask in held]
            if axis == "blk":
                copies = [links.copy(v, v, 0, bit) for v in place]
                low, size = lows.pop(), size * 2
            else:
                copies = [links.copy(v, v, bit, 0) for v in place]
                held = held + [mask | bit for mask in held]
            yield
            wait_all(copies)


def landing_rows(rows, order, n_dp, n_blk, every):
    names, held, total = bit_names(n_dp, n_blk), n_dp if every else 1, 0
    for token in order:
        for axis, _ in names[token]:
            if axis == "blk":
                rows //= 2
            else:
                held //= 2
            total += held * rows
    return total


VEC_ROWS = 16


def whole_kernel(
    n_dp, n_blk, x_ref, lengths, cot_ref, n1g, n1b, log_step, log_rate, frequency, out_coef, skip_gain, glu_hbm, glu_b,
    n2g, n2b, in_hbm, in_b, out_hbm, out_b,
    block_out, grad_in, sum_glu, sum_in, sum_out, vec_out, par_out,
    send_sems, recv_sems, load_sems, glu_w, ffn_in, ffn_out, windows, rate_own, freq_own, coef_own, columns,
    a_send, x_all, y_send, y_all, dy_send, dy_all, dx_send, dx_all,
    q_ref, t_ref, h_ref, consts, base, taps, a_ref, b_ref, g_ref,
    result_all, feed_all, dglu, hidden_grad, slice_grad, hidden_s, pre_s, slope_keep, unit_keep, residual_keep, gate_keep,
    gelu_keep, acc_out, acc_feed, residual_grad, part_glu, part_in, part_out,
    own_par, dp_par, sum_par, blk_par, all_par, flat_par, vec, dp_vec, sum_vec, blk_vec, *landings,
):
    rows, width = x_ref.shape
    ff = ffn_in.shape[1]
    chans = width // n_blk
    quarter = chans // n_dp
    half = max(chans // 2, 8)
    halves = [(first, half) for first in range(0, chans, half)]
    links = Links(send_sems, recv_sems, n_dp, n_blk)
    dp, blk = links.dp, links.blk
    first = pl.multiple_of(blk * chans, 8)
    lanes_at = pl.multiple_of(blk * chans // 128 * 128, 128)

    loads = [
        Load(src, dst, load_sems.at[k])
        for k, (src, dst) in enumerate([
            (log_rate.at[:, pl.ds(lanes_at, 128)], windows.at[0]),
            (frequency.at[:, pl.ds(lanes_at, 128)], windows.at[1]),
            (out_coef.at[:, :, pl.ds(lanes_at, 128)], windows.at[pl.ds(2, 2)]),
            (out_hbm, ffn_out),
            (glu_hbm, glu_w),
            (in_hbm, ffn_in),
        ])
    ]
    links.loads = loads
    links.greet()

    places = blk * rows + iota((rows, 1), 0)
    live = (places < lengths[0]).astype(F32)
    inputs = x_ref[...].astype(F32)
    normed, unit, scale1 = layer_norm(inputs, n1g[...], n1b[...])
    unit_keep[...] = unit
    mixed = normed.astype(BF16) * live.astype(BF16)
    flip = jnp.where(iota((rows, rows), 0) + iota((rows, rows), 1) == rows - 1, 1.0, 0.0).astype(BF16)
    a_send[...] = nn(flip, mixed).T
    links.meet()
    to_x = [links.exchange(a_send.reshape(n_blk, chans, rows), x_all, *part) for part in halves]
    cot = cot_ref[...].astype(F32)
    result = live * cot
    result_all[dp] = result
    gather_result = Gather(links, result_all)

    columns[0] = jnp.broadcast_to(log_step[...], (128, width)).T
    columns[1] = jnp.broadcast_to(skip_gain[...], (128, width)).T
    own_skip = columns[1, pl.ds(first, chans), :]
    for load in loads[:3]:
        load.wait()
    turn = (128 - blk * chans % 128) % 128
    own = [pltpu.roll(windows[k], turn, 1).T[:chans] for k in range(4)]
    rate_own[...], freq_own[...], coef_own[0], coef_own[1] = own

    def ssm():
        return columns[0, pl.ds(first, chans), :], rate_own[...], freq_own[...], (coef_own[0], coef_own[1])

    kern_slot = ssm_setup(n_blk, ssm(), consts, base)
    lead_slot = kern_slot - 1
    base_flat = base.reshape(8 * chans, 128)
    groups(0, chans, lambda group: make_powers(group, chans, consts, kern_slot, base_flat, q_ref, taps))
    shift_taps(own_skip, taps, base)
    groups(0, chans, lambda group: make_band(group, chans, base_flat, t_ref))

    x_flat = x_all.reshape(n_blk * chans, 128)
    y_flat = y_send.reshape(n_blk * chans, 128)
    to_y = []
    for part, arriving in zip(halves, to_x):
        wait_all(arriving)
        groups(*part, lambda group: forward_group(group, chans, n_blk, consts, lead_slot, x_flat, q_ref, t_ref, h_ref, y_flat))
        to_y += links.exchange(y_send, y_all, *part)

    gather_result.relay()
    loads[3].wait()
    low = result.astype(BF16)
    step = ff // 4
    for k in range(4):
        hidden_grad[:, k * step : (k + 1) * step] = nt(low, ffn_out[k * step : (k + 1) * step, :])
    part_ff = ff // n_dp
    rows_s = pl.multiple_of(dp * part_ff, 128)
    out_slice = ffn_out[pl.ds(rows_s, part_ff), :]
    for k in range(n_dp):
        slice_grad[k * rows : (k + 1) * rows, :] = nt(result_all[k].astype(BF16), out_slice)
    loads[4].wait()
    loads[5].wait()

    wait_all(to_y)
    conv = y_all.reshape(width, rows)[...].T
    gelu_out, gelu_slope = gelu_parts(conv)
    slope_keep[...] = gelu_slope
    gelu_low = gelu_out.astype(BF16)
    gelu_keep[...] = gelu_low
    glu_pre = nn(gelu_low, glu_w[...]) + glu_b[...]
    left = glu_pre[:, :width]
    gate = 0.5 + 0.5 * jnp.tanh(0.5 * glu_pre[:, width:])
    gate_keep[0] = left
    gate_keep[1] = gate
    residual = x_ref[...].astype(F32) + live * left * gate
    normed_mid, unit_mid, scale_mid = layer_norm(residual, n2g[...], n2b[...])
    feed = normed_mid.astype(BF16)
    feed_all[dp] = feed.astype(F32)
    gather_feed = Gather(links, feed_all)
    residual_keep[0] = residual
    residual_keep[1] = unit_mid

    pieces, arrivals = {}, {}

    def piece(work):
        pieces[work.__name__] = work

    @piece
    def own():
        for k in range(4):
            cut = slice(k * step, (k + 1) * step)
            hidden, slope = gelu_parts(nn(feed, ffn_in[:, cut]) + in_b[:, cut])
            grad_pre = (hidden_grad[:, cut] * slope).astype(BF16)
            forward = nn(hidden.astype(BF16), ffn_out[cut, :])
            back = nt(grad_pre, ffn_in[:, cut])
            acc_out[...] = forward if k == 0 else acc_out[...] + forward
            acc_feed[...] = back if k == 0 else acc_feed[...] + back
            vec[7 + k : 8 + k, :] = token_sum(grad_pre.astype(F32))
        block_out[...] = (residual_keep[0] + live * (acc_out[...] + out_b[...])).astype(BF16)

    @piece
    def glubwd():
        grad_feed = acc_feed[...]
        unit_mid = residual_keep[1]
        vec[2:3, :] = token_sum(grad_feed * unit_mid)
        vec[3:4, :] = token_sum(grad_feed)
        vec[4:5, :] = token_sum(result_all[dp])
        grad_res = cot_ref[...].astype(F32) + norm_back(grad_feed, n2g[...], unit_mid, scale_mid)
        residual_grad[...] = grad_res
        grad_left = live * grad_res
        left, gate = gate_keep[0], gate_keep[1]
        to_left = (grad_left * gate).astype(BF16)
        to_gate = (grad_left * left * gate * (1.0 - gate)).astype(BF16)
        dglu[:, :width] = to_left
        dglu[:, width:] = to_gate
        vec[5:6, :] = token_sum(to_left.astype(F32))
        vec[6:7, :] = token_sum(to_gate.astype(F32))

    @piece
    def dy():
        dy_send[...] = (nt(dglu[...], glu_w[...]) * slope_keep[...]).T
        arrivals["dy"] = links.exchange(dy_send.reshape(n_blk, chans, rows), dy_all, 0, chans)

    @piece
    def slice_all():
        gather_feed.relay()
        in_slice = ffn_in[:, pl.ds(rows_s, part_ff)]
        in_b_slice = in_b[:, pl.ds(rows_s, part_ff)]
        for k in range(n_dp):
            hidden, slope = gelu_parts(nn(feed_all[k].astype(BF16), in_slice) + in_b_slice)
            cut = slice(k * rows, (k + 1) * rows)
            hidden_s[cut, :] = hidden.astype(BF16)
            pre_s[cut, :] = (slice_grad[cut, :] * slope).astype(BF16)

    part_gl = 2 * width // n_dp
    shapes = piece_shapes(n_dp, n_blk, width, ff)
    chunks = {}

    def window(ref, row0, col0, rows_at, cols):
        def view(mask, row, size):
            slot = links.dp_peer(mask)
            row_at = pl.multiple_of(slot * rows_at[0] + row0 + row, 8)
            col_at = pl.multiple_of(slot * rows_at[1] + col0, 128) if rows_at[1] else col0
            return ref.at[pl.ds(row_at, size), pl.ds(col_at, cols)]
        return view

    def start_chunk(k):
        if k not in shapes:
            return
        kind, row0, col0, rows_k, cols_k, plan = shapes[k]
        rows_cut, cols_cut = slice(row0, row0 + rows_k), slice(col0, col0 + cols_k)
        if kind == "glu":
            part_glu[rows_cut, :] = tn(gelu_keep[:, rows_cut], dglu[...])
            part = window(part_glu, row0, 0, (0, part_gl), part_gl)
            total = window(sum_glu, row0, 0, (0, part_gl), part_gl)
        elif kind == "out":
            results = result_all[:, :, cols_cut].reshape(n_dp * rows, cols_k).astype(BF16)
            part_out[rows_cut, cols_cut] = tn(hidden_s[:, rows_cut], results)
            part = window(part_out, row0, col0, (0, 0), cols_k)
            total = window(sum_out, row0, col0, (part_ff, 0), cols_k)
        else:
            feeds = feed_all[:, :, rows_cut].reshape(n_dp * rows, rows_k).astype(BF16)
            part_in[rows_cut, cols_cut] = tn(feeds, pre_s[:, cols_cut])
            part = window(part_in, row0, col0, (0, 0), cols_k)
            total = window(sum_in, row0, col0, (0, part_ff), cols_k)
        chunks[k] = Chunk(links, rows_k, part, total, landings[k], kind == "glu", plan)
        chunks[k].advance()

    dy_flat = dy_all.reshape(n_blk * chans, 128)
    dx_flat = dx_send.reshape(n_blk * chans, 128)

    def backward(k):
        if k == 0:
            wait_all(arrivals["dy"])
        size = min(GROUP, chans)
        if k * size < chans:
            backward_group([k * size + i for i in range(size)], chans, n_blk, consts, lead_slot, x_flat, dy_flat, q_ref, t_ref, h_ref, dx_flat, a_ref, b_ref, g_ref)
        if k == 3:
            groups(4 * size, chans - 4 * size, lambda group: backward_group(group, chans, n_blk, consts, lead_slot, x_flat, dy_flat, q_ref, t_ref, h_ref, dx_flat, a_ref, b_ref, g_ref))
            arrivals["dx"] = links.exchange(dx_send, dx_all, 0, chans)

    @piece
    def near():
        split_lags(g_ref, base)
        groups(0, chans, lambda group: near_sums(group, chans, base_flat, q_ref, a_ref, b_ref))
        rate_freq, coefs, d_step, d_skip = finish(chans, ssm(), a_ref, b_ref, g_ref)
        own_par[:, 0, :] = rate_freq
        own_par[:, 1, :] = coefs
        lane = iota((chans, 128), 1)
        pair = jnp.where(lane == 0, d_step, jnp.where(lane == 1, d_skip, 0.0))
        if chans < 128:
            pair = jnp.concatenate([pair, jnp.zeros((128 - chans, 128), F32)], axis=0)
        pair = pair.T[0:8]
        if width > 128:
            pair = jnp.concatenate([pair, jnp.zeros((8, width - 128), F32)], axis=1)
        pair = pltpu.roll(pair, blk * chans, 1)
        vec[11:13, :] = pair[0:2]
        vec[13:16, :] = jnp.zeros((3, width), F32)

    @piece
    def ln1():
        wait_all(arrivals["dx"])
        back = dx_all.reshape(width, rows)[...].T
        high, rest = split(back)
        rest, last = split(back - high.astype(F32))
        grad_normed = live * (nn(flip, high) + (nn(flip, rest) + nn(flip, last)))
        unit = unit_keep[...]
        vec[0:1, :] = token_sum(grad_normed * unit)
        vec[1:2, :] = token_sum(grad_normed)
        grad_in[...] = residual_grad[...] + norm_back(grad_normed, n1g[...], unit, scale1)

    @piece
    def s0():
        waits = arrivals["s0"] = []
        for mask in range(1, n_dp):
            at = links.dp_peer(mask) * quarter
            waits.append(links.copy(own_par.at[pl.ds(at, quarter)], dp_par.at[dp], mask, 0))
            waits.append(links.copy(vec, dp_vec.at[dp], mask, 0))
        dp_par[dp] = own_par[pl.ds(dp * quarter, quarter)]
        dp_vec[dp] = vec[...]

    @piece
    def s1():
        wait_all(arrivals["s0"])
        sum_par[...] = sum_slots(dp_par, n_dp)
        sum_vec[...] = sum_slots(dp_vec, n_dp)
        waits = arrivals["s1"] = []
        for mask in range(1, n_blk):
            waits.append(links.copy(sum_par, blk_par.at[blk], 0, mask))
            waits.append(links.copy(sum_vec, blk_vec.at[blk], 0, mask))
        blk_par[blk] = sum_par[...]
        blk_vec[blk] = sum_vec[...]

    @piece
    def s2():
        wait_all(arrivals["s1"])
        all_par[dp] = blk_par[...]
        arrivals["s2"] = Gather(links, all_par)
        vec_out[...] = sum_slots(blk_vec, n_blk)

    @piece
    def s3():
        arrivals["s2"].relay()
        state = par_out.shape[0] // 4
        for b in range(n_blk):
            for d in range(n_dp):
                at = b * chans + d * quarter
                block = all_par[d, b]
                flat_par[0, at : at + quarter, :] = block[:, 0, :]
                flat_par[1, at : at + quarter, :] = block[:, 1, :]
        par_out[: 2 * state, :] = flat_par[0].T
        par_out[2 * state :, :] = flat_par[1].T

    for token in ORDER:
        if isinstance(token, int):
            if token in chunks:
                chunks[token].advance()
        elif token.startswith("part"):
            start_chunk(int(token[4:]))
        elif token.startswith("bwd"):
            backward(int(token[3:]))
        else:
            pieces["slice_all" if token == "slice" else token]()
    while any(chunk.live for chunk in chunks.values()):
        for chunk in chunks.values():
            chunk.advance()
    links.finish()


def piece_shapes(n_dp, n_blk, width, ff):
    shapes = {}
    n_glu, n_ffn = len(GLU_PLANS), len(FFN_PLANS) // 2
    size = width // n_glu
    for k, plan in enumerate(GLU_PLANS):
        shapes[k] = ("glu", k * size, 0, size, 2 * width // n_dp, plan)
    for kind, at, height, breadth in (("out", n_glu, ff // n_dp, width), ("in", n_glu + n_ffn, width, ff // n_dp)):
        cols = min(n_ffn, breadth // 128)
        cuts = min(n_ffn // cols, height // (8 * n_blk))
        high, wide = height // cuts, breadth // cols
        for k in range(cols * cuts):
            shapes[at + k] = (kind, k % cuts * high, k // cuts * wide, high, wide, FFN_PLANS[at - n_glu + k])
    return shapes


def sum_slots(ref, count):
    total = ref[0]
    for k in range(1, count):
        total = total + ref[k]
    return total


def deliver_kernel(big_in, vec, par, others, big_out, rows_out, rate, freq, coef, others_out, sems):
    states = rate.shape[0]
    moves = []
    for src, dst in zip(big_in, big_out):
        part = src.shape[0] // BIG_PARTS
        moves += [(src.at[pl.ds(k * part, part)], dst.at[pl.ds(k * part, part)]) for k in range(BIG_PARTS)]
    moves += list(zip(others, others_out))
    moves += [(par.at[pl.ds(0, states)], rate), (par.at[pl.ds(states, states)], freq)]
    moves += [(par.at[pl.ds((2 + k) * states, states)], coef.at[k]) for k in range(2)]
    copies = [pltpu.make_async_copy(src, dst, sems.at[k]) for k, (src, dst) in enumerate(moves)]
    for copy in copies:
        copy.start()
    row = 0
    for out in rows_out:
        count = out.shape[1] // vec.shape[1]
        for k in range(count):
            out[:, k * vec.shape[1] : (k + 1) * vec.shape[1]] = vec[row : row + 1, :]
            row += 1
    for copy in copies:
        copy.wait()


def on_device(n_dp, n_blk, block_in, seq_lengths, norm1_gain, norm1_bias, log_step, log_rate, frequency, out_coef, skip_gain, glu_weight, glu_bias, norm2_gain, norm2_bias, ffn_in, ffn_in_bias, ffn_out, ffn_out_bias, cotangent):
    _, rows, width = block_in.shape
    ff = ffn_in.shape[1]
    states = log_rate.shape[1]
    chans, quarter = width // n_blk, width // n_blk // n_dp
    row = lambda v: v.reshape(1, -1)
    vmem, anywhere = pl.BlockSpec(memory_space=VMEM), pl.BlockSpec(memory_space=pl.ANY)
    shape = jax.ShapeDtypeStruct
    outs = [
        shape((rows, width), BF16), shape((rows, width), F32),
        shape((width, 2 * width), F32), shape((width, ff), F32), shape((ff, width), F32),
        shape((VEC_ROWS, width), F32), shape((4 * states, width), F32),
    ]
    part_ff, part_gl = ff // n_dp, 2 * width // n_dp
    tokens = n_dp * rows
    f32 = lambda *dims: VMEM(dims, F32)
    bf16 = lambda *dims: VMEM(dims, BF16)
    dma = lambda n: pltpu.SemaphoreType.DMA((n,))
    shapes = piece_shapes(n_dp, n_blk, width, ff)
    landings = []
    for k in range(len(GLU_PLANS) + len(FFN_PLANS)):
        kind, _, _, rows_k, cols_k, plan = shapes.get(k, ("out", 0, 0, 8 * n_blk, 128, FFN_PLANS[0]))
        landings.append(f32(landing_rows(rows_k, plan[0], n_dp, n_blk, kind == "glu"), cols_k))
    scratch = [
        dma(LINK_SEMS), dma(LINK_SEMS), dma(8),
        bf16(width, 2 * width), bf16(width, ff), bf16(ff, width),
        f32(4, states, 128), f32(chans, states), f32(chans, states), f32(2, chans, states), f32(2, width, 128),
        f32(width, rows), f32(n_blk, chans, rows), f32(n_blk, chans, rows), f32(n_blk, chans, rows),
        f32(width, rows), f32(n_blk, chans, rows), f32(n_blk, chans, rows), f32(n_blk, chans, rows),
        bf16(chans, 256, 128), bf16(chans, 256, 128), f32(chans, n_blk, 128), f32(n_consts(n_blk), chans, 128),
        f32(8, chans, 128), f32(chans, 128), f32(2 * chans, 128), f32(2 * chans, 128), f32(chans, 128),
        f32(n_dp, rows, width), f32(n_dp, rows, width),
        bf16(rows, 2 * width),
        f32(rows, ff), f32(tokens, part_ff), bf16(tokens, part_ff), bf16(tokens, part_ff),
        f32(rows, width), f32(rows, width), f32(2, rows, width), f32(2, rows, width),
        bf16(rows, width), f32(rows, width), f32(rows, width), f32(rows, width),
        f32(width, 2 * width), f32(width, part_ff), f32(part_ff, width),
        f32(chans, 2, 128), f32(n_dp, quarter, 2, 128), f32(quarter, 2, 128), f32(n_blk, quarter, 2, 128),
        f32(n_dp, n_blk, quarter, 2, 128), f32(2, width, 128),
        f32(VEC_ROWS, width), f32(n_dp, VEC_ROWS, width), f32(VEC_ROWS, width), f32(n_blk, VEC_ROWS, width),
        *landings,
    ]
    out = pl.pallas_call(
        functools.partial(whole_kernel, n_dp, n_blk),
        out_shape=[VMEM(v.shape, v.dtype) for v in outs],
        out_specs=[vmem] * len(outs),
        in_specs=[vmem, pl.BlockSpec(memory_space=pltpu.SMEM), vmem, vmem, vmem, vmem, anywhere, anywhere, anywhere, vmem, anywhere, vmem, vmem, vmem, anywhere, vmem, anywhere, vmem],
        scratch_shapes=scratch,
        compiler_params=pltpu.CompilerParams(collective_id=0, has_side_effects=True, vmem_limit_bytes=44 * 2**20),
    )(
        block_in[0], seq_lengths, cotangent[0], row(norm1_gain), row(norm1_bias), row(log_step), log_rate.T, frequency.T,
        out_coef.swapaxes(1, 2), row(skip_gain), glu_weight, row(glu_bias), row(norm2_gain), row(norm2_bias), ffn_in,
        row(ffn_in_bias), ffn_out, row(ffn_out_bias),
    )
    block_out, grad_in, g_glu, g_in, g_out, vec, par = out
    widths = [width, width, width, width, width, 2 * width, ff, width, width]
    made = [shape((rows, width), BF16), shape((rows, width), F32)]
    big = [shape(v.shape, F32) for v in (g_glu, g_in, g_out)]
    small = [shape((1, w), F32) for w in widths]
    params = [shape((states, width), F32), shape((states, width), F32), shape((2, states, width), F32)]
    out_shapes = made + big + small + params

    def deliver(block_out, grad_in, g_glu, g_in, g_out, vec, par, *rest):
        outs, sems = rest[:-1], rest[-1]
        deliver_kernel([g_glu, g_in, g_out], vec, par, [block_out, grad_in], outs[2:5], outs[5:14], *outs[14:], outs[:2], sems)

    done = pl.pallas_call(
        deliver,
        out_shape=out_shapes,
        in_specs=[vmem] * 7,
        out_specs=[anywhere] * 5 + [vmem] * 9 + [anywhere] * 3,
        scratch_shapes=[dma(32)],
        compiler_params=pltpu.CompilerParams(vmem_limit_bytes=8 * 2**20),
    )(*out)
    flat = [v.reshape(-1) for v in done[5:14]]
    n1_gain, n1_bias, n2_gain, n2_bias, ffn_out_b, glu_b, ffn_in_b, d_step, d_skip = flat
    return (
        done[0][None], done[1][None], n1_gain, n1_bias, d_step, done[14].T, done[15].T, done[16].swapaxes(1, 2), d_skip,
        done[2], glu_b, n2_gain, n2_bias, done[3], ffn_in_b, done[4], ffn_out_b,
    )


def solution(mesh):
    split_spec, whole = P("dp", "blk", None), P()
    return jax.shard_map(
        functools.partial(on_device, mesh.shape["dp"], mesh.shape["blk"]),
        mesh=mesh,
        in_specs=(split_spec, P("dp")) + (whole,) * 15 + (split_spec,),
        out_specs=(split_spec, split_spec) + (whole,) * 15,
        check_vma=False,
    )
```

```python
import functools

import jax
import jax.numpy as jnp
from jax import lax
from jax.experimental import pallas as pl
from jax.experimental.pallas import tpu as pltpu
from jax.sharding import PartitionSpec as P

NORM_EPSILON = 1e-05
F32 = jnp.float32
BF16 = jnp.bfloat16
PRECISE = lax.Precision.HIGHEST
SERIES = 16
GROUP = 16
SEND_SEMS = 43
RECV_SEMS = 191
BIG_PARTS = 1
FIRST_WHOLE = False
GLU_PLANS = (
    (("c", "x", "z0", "y", "z1"), 3),
    (("c", "y", "x", "z0", "z1"), 3),
    (("c", "z0", "x", "y", "z1"), 2),
    (("c", "y", "x", "z0", "z1"), 3),
)
FFN_PLANS = (
    (("x", "z0", "z1"), 2),
    (("x", "z1", "z0"), 2),
    (("z1", "x", "z0"), 3),
    (("x", "z0", "z1"), 2),
    (("x", "z0", "z1"), 2),
    (("z0", "x", "z1"), 2),
    (("x", "z0", "z1"), 2),
    (("x", "z0", "z1"), 2),
    (("z1", "x", "z0"), 1),
    (("x", "z0", "z1"), 3),
    (("x", "z0", "z1"), 3),
    (("z0", "x", "z1"), 0),
    (("x", "z1", "z0"), 2),
    (("x", "z0", "z1"), 3),
    (("x", "z0", "z1"), 1),
    (("x", "z0", "z1"), 0),
)
ORDER = (
    "own", "glubwd", "dy", "part0", "part1", "part2", "part3", 0, 1, 2, 3, "slice", "part4", "part5", "part6",
    0, "part7", 1, "part8", "part9", "part10", 2, "part11", "part12", "part13", "part14", 4, "part15",
    "part16", 3, "part17", "part18", 5, "part19", 0, 6, "bwd0", 7, 9, 1, 0, 8, 4, 12, "bwd1", 7, 5, 1, 10, 0,
    11, 8, 15, 2, 4, "bwd2", 7, 5, 1, 14, 8, 11, 13, 10, 0, 16, 3, 2, 7, 5, 4, "bwd3", 1, 8, 14, 11, 17, 13,
    19, 10, 0, 18, 6, "near", 9, 7, 12, 5, 3, 16, 2, 15, 4, 7, 0, 5, 1, 8, "ln1", 14, 11, 17, 7, 4, "s0", 13,
    19, 0, 10, 18, 6, 7, 8, 5, 9, 12, 0, 3, 16, 1, 2, "s1", 5, 15, 14, 11, 17, 4, 13, 19, 10, 1, 6, 18, 15, 4,
    8, 9, 12, 2, 11, 3, 16, 19, 1, "s2", 8, 14, 10, 9, 12, 17, 13, 6, 18, 2, 3, 15, 11, 16, 14, "s3", 11, 19,
    17, 9, 18, 10, 16, 6, 12, 10, 2, 13, 14, 19, 3, 2, 15, 14, 6, 9, 17, 18, 6, 9, 13, 16, 13, 16, 3, 19, 12,
    15, 3, 17, 19, 18, 12, 15, 17, 18,
)
VMEM = pltpu.VMEM


def iota(shape, axis):
    return lax.broadcasted_iota(jnp.int32, shape, axis)


def is_left(shape):
    half = shape[-1] // 2
    return iota(shape, len(shape) - 1) < half


def swap(v):
    return pltpu.roll(v, v.shape[-1] // 2, v.ndim - 1)


def times(v, const):
    return v * const[0] + swap(v) * const[1]


def split(v):
    high = v.astype(BF16)
    return high, (v - high.astype(F32)).astype(BF16)


def nn(a, b):
    return lax.dot_general(a, b, (((1,), (0,)), ((), ())), preferred_element_type=F32)


def nt(a, b):
    return lax.dot_general(a, b, (((1,), (1,)), ((), ())), preferred_element_type=F32)


def tn(a, b):
    return lax.dot_general(a, b, (((0,), (0,)), ((), ())), preferred_element_type=F32)


def cmul(a, b):
    return a[0] * b[0] - a[1] * b[1], a[0] * b[1] + a[1] * b[0]


def twice(v):
    return jnp.concatenate([v, v], axis=-1)


def pole_parts(log_step, log_rate, frequency):
    step = jnp.exp(log_step)
    rate = jnp.exp(twice(log_rate))
    pole = (-rate, step * twice(frequency))
    phi = (jnp.zeros_like(rate), jnp.zeros_like(rate))
    slope = (jnp.zeros_like(rate), jnp.zeros_like(rate))
    fact = [1.0]
    for k in range(1, SERIES + 2):
        fact.append(fact[-1] * k)
    for k in range(SERIES, -1, -1):
        phi = cmul(phi, pole)
        phi = (phi[0] + 1.0 / fact[k + 1], phi[1])
    for k in range(SERIES, 0, -1):
        slope = cmul(slope, pole)
        slope = (slope[0] + k / fact[k + 1], slope[1])
    grow = cmul(pole, phi)
    z = (1.0 + grow[0], grow[1])
    return step, rate, z, phi, slope


def as_const(value):
    sign = jnp.where(is_left(value[0].shape), -1.0, 1.0)
    return value[0], value[1] * sign


def packed(value):
    return jnp.where(is_left(value[0].shape), value[0], value[1])


def ssm_setup(rows, ssm, consts, base):
    log_step, log_rate, frequency, coef = ssm
    step, rate, z, phi, slope = pole_parts(log_step, log_rate, frequency)
    b = (twice(coef[0]), twice(coef[1]))
    residue = cmul(b, (step * phi[0], step * phi[1]))
    power = (jnp.ones_like(rate), jnp.zeros_like(rate))
    for r in range(8):
        base[r] = packed(power)
        power = cmul(power, z)
    slot = 0

    def keep(value):
        nonlocal slot
        c = as_const(value)
        consts[2 * slot] = c[0]
        consts[2 * slot + 1] = c[1]
        slot += 1

    for k in range(4):
        keep(power)
        power = cmul(power, power)
    for k in range((rows - 1).bit_length()):
        keep(power)
        power = cmul(power, power)
    lead = cmul(residue, z)
    lead = (2.0 * lead[0], 2.0 * lead[1])
    sign = jnp.where(is_left(rate.shape), 1.0, -1.0)
    consts[2 * slot] = lead[0] * sign
    consts[2 * slot + 1] = -lead[1]
    slot += 1
    kern = jnp.where(is_left(rate.shape), 2.0 * residue[0], -2.0 * residue[1])
    kern_high = kern.astype(BF16).astype(F32)
    consts[2 * slot] = kern_high
    consts[2 * slot + 1] = kern - kern_high
    return slot


def row_of(ref, index, chan):
    return ref[index, pl.ds(chan, 1), :]


def const_of(consts, slot, chan):
    return row_of(consts, 2 * slot, chan), row_of(consts, 2 * slot + 1, chan)


def make_powers(group, chans, consts, kern_slot, base_flat, q_ref, taps_ref):
    every = [base_flat[pl.ds(chan, 8, stride=chans), :] for chan in group]
    for k in range(4):
        every = [
            jnp.concatenate([powers, times(powers, const_of(consts, k, chan))], axis=0)
            for chan, powers in zip(group, every)
        ]
    parts = [split(powers) for powers in every]
    for chan, (high, rest) in zip(group, parts):
        q_ref[chan, :128, :] = high
        q_ref[chan, 128:, :] = rest
    kerns = []
    for chan, (high, rest) in zip(group, parts):
        taps = [row_of(consts, 2 * kern_slot + k, chan) for k in range(2)]
        taps = jnp.concatenate([taps[0], taps[1]], axis=0).astype(BF16)
        kerns.append(nt(twice(taps), jnp.concatenate([high, rest], axis=1)))
    for chan, kern in zip(group, kerns):
        taps_ref[pl.ds(chan, 1), :] = kern[0:1] + kern[1:2]


def shift_taps(skip, taps_ref, base):
    taps = taps_ref[...]
    taps = taps + jnp.where(iota(taps.shape, 1) == 0, skip, 0.0)
    for r in range(8):
        base[r] = taps if r == 7 else pltpu.roll(taps, 7 - r, 1)


def make_band(group, chans, base_flat, t_ref):
    for chan in group:
        tile = base_flat[pl.ds(chan, 8, stride=chans), :]
        band = jnp.concatenate([pltpu.roll(tile, 120 - 8 * m, 1) if m < 15 else tile for m in range(16)], axis=0)
        band = jnp.where(iota((128, 128), 0) + iota((128, 128), 1) >= 127, band, 0.0)
        t_high, t_rest = split(band)
        t_ref[chan, :128, :] = t_high
        t_ref[chan, 128:, :] = t_rest


def scan(values, consts, first, group, reverse):
    rows = values[0].shape[0]
    places = iota(values[0].shape, 0)

    def moved(x, d):
        if reverse:
            return jnp.where(places < rows - d, pltpu.roll(x, rows - d, 0), 0.0)
        return jnp.where(places >= d, pltpu.roll(x, d, 0), 0.0)

    values = [moved(v, 1) for v in values]
    d, k = 1, 0
    while d < rows:
        values = [v + times(moved(v, d), const_of(consts, first + k, chan)) for v, chan in zip(values, group)]
        d, k = 2 * d, k + 1
    return values


def wide(chan, q_ref, t_ref):
    return jnp.concatenate([q_ref[chan], t_ref[chan]], axis=1)


def far_parts(states, consts, lead_slot, group, q_ref):
    rows = states[0].shape[0]
    outs = []
    for chan, state in zip(group, states):
        high, rest = split(times(state, const_of(consts, lead_slot, chan)))
        both = twice(jnp.concatenate([high, rest], axis=0))
        outs.append(nt(both, jnp.concatenate([q_ref[chan, :128, :], q_ref[chan, 128:, :]], axis=1)))
    return [out[:rows] + out[rows:] for out in outs]


def forward_group(group, chans, rows, consts, lead_slot, x_flat, q_ref, t_ref, h_ref, y_flat):
    outs = [
        nn(twice(x_flat[pl.ds(chan, rows, stride=chans), :].astype(BF16)), wide(chan, q_ref, t_ref))
        for chan in group
    ]
    states = scan([out[:, :128] for out in outs], consts, 4, group, False)
    for chan, state in zip(group, states):
        h_ref[chan] = state
    fars = far_parts(states, consts, lead_slot, group, q_ref)
    for chan, out, far in zip(group, outs, fars):
        y_flat[pl.ds(chan, rows, stride=chans), :] = out[:, 128:] + far


def backward_group(group, chans, rows, consts, lead_slot, x_flat, dy_flat, q_ref, t_ref, h_ref, dx_flat, a_ref, b_ref, g_ref):
    places = iota((1, 128), 1).astype(F32)
    us = [x_flat[pl.ds(chan, rows, stride=chans), :] for chan in group]
    dys = [dy_flat[pl.ds(chan, rows, stride=chans), :] for chan in group]
    outs = []
    for chan, u, dy in zip(group, us, dys):
        high = dy.astype(BF16).astype(F32)
        left = twice(jnp.concatenate([high, dy - high, dy * places, u * places], axis=0).astype(BF16))
        outs.append(nn(left, wide(chan, q_ref, t_ref)))
    pairs = [tn(u.astype(BF16), dy.astype(BF16)) for u, dy in zip(us, dys)]
    d0s = [out[:rows, :128] + out[rows : 2 * rows, :128] for out in outs]
    d1s = [out[2 * rows : 3 * rows, :128] for out in outs]
    hs = [h_ref[chan] for chan in group]
    ends = scan(d0s, consts, 4, group, True)
    fars = far_parts(ends, consts, lead_slot, group, q_ref)
    for chan, out, far in zip(group, outs, fars):
        dx_flat[pl.ds(chan, rows, stride=chans), :] = out[:rows, 128:] + out[rows : 2 * rows, 128:] + far
    h1s = scan(
        [out[3 * rows :, :128] + 128.0 * times(h, const_of(consts, 4, chan)) for chan, out, h in zip(group, outs, hs)],
        consts, 4, group, False,
    )
    mask = is_left(hs[0].shape)

    def prod(p, q):
        q_swap = swap(q)
        return p * jnp.where(mask, q, q_swap) + swap(p) * jnp.where(mask, -q_swap, q)

    for chan, d0, d1, h, h1 in zip(group, d0s, d1s, hs, h1s):
        a_far = jnp.sum(prod(d0, h), axis=0, keepdims=True)
        b_far = a_far + jnp.sum(prod(d1, h) + prod(d0, h1), axis=0, keepdims=True)
        a_ref[pl.ds(chans + chan, 1), :] = a_far
        b_ref[pl.ds(chans + chan, 1), :] = b_far
    keep = iota((128, 128), 1) <= iota((128, 128), 0)
    for chan, pair in zip(group, pairs):
        skew = jnp.where(keep, pltpu.roll(pair, 1, 1, stride=1, stride_axis=0), 0.0)
        g_ref[pl.ds(chan, 1), :] = jnp.sum(skew, axis=0, keepdims=True)


def split_lags(g_ref, base):
    lags = g_ref[...]
    weighted = lags * iota(lags.shape, 1).astype(F32)
    for k, v in enumerate((lags, weighted)):
        high = v.astype(BF16).astype(F32)
        base[k] = high
        base[2 + k] = v - high
        base[4 + k] = jnp.zeros_like(v)
        base[6 + k] = jnp.zeros_like(v)


def near_sums(group, chans, base_flat, q_ref, a_ref, b_ref):
    outs = [nn(twice(base_flat[pl.ds(chan, 8, stride=chans), :].astype(BF16)), q_ref[chan]) for chan in group]
    for chan, out in zip(group, outs):
        a_ref[pl.ds(chan, 1), :] = out[0:1] + out[2:3]
        b_ref[pl.ds(chan, 1), :] = out[1:2] + out[3:4]


def groups(first, count, body):
    size = min(GROUP, count)

    def step(k, carry):
        body([first + k * size + i for i in range(size)])
        return carry

    if count > 0:
        lax.fori_loop(0, count // size, step, 0)


def finish(chans, ssm, a_ref, b_ref, g_ref):
    log_step, log_rate, frequency, coef = ssm
    step, rate, z, phi, slope = pole_parts(log_step, log_rate, frequency)
    b = (twice(coef[0]), twice(coef[1]))

    def dup(v):
        left = is_left(v.shape)
        moved = swap(v)
        return jnp.where(left, v, moved), jnp.where(left, moved, v)

    def total(ref):
        near, far = dup(ref[:chans, :]), dup(ref[chans:, :])
        far = cmul(far, z)
        return near[0] + far[0], near[1] + far[1]

    a, bb = total(a_ref), total(b_ref)
    residue = cmul(b, (step * phi[0], step * phi[1]))
    g_res = (2.0 * a[0], -2.0 * a[1])
    rb = cmul(residue, bb)
    g_pole = (2.0 * rb[0], -2.0 * rb[1])
    conj = lambda v: (v[0], -v[1])
    g_coef = cmul(conj((step * phi[0], step * phi[1])), g_res)
    bs = cmul(b, (step * slope[0], step * slope[1]))
    more = cmul(conj(bs), g_res)
    g_pole = (g_pole[0] + more[0], g_pole[1] + more[1])
    d_rate = -rate * g_pole[0]
    d_freq = step * g_pole[1]
    by_step = cmul(conj(cmul(b, phi)), g_res)[0] + g_pole[1] * twice(frequency)
    left = is_left(by_step.shape)
    d_step = step * jnp.sum(jnp.where(left, by_step, 0.0), axis=1, keepdims=True)
    return jnp.where(left, d_rate, d_freq), jnp.where(left, g_coef[0], g_coef[1]), d_step, g_ref[:, 0:1]


def n_consts(rows):
    return 2 * (4 + (rows - 1).bit_length() + 2)


def gelu_parts(v):
    scale = 0.7978845608028654
    square = v * v
    bend = jnp.tanh(scale * v * (1.0 + 0.044715 * square))
    half = 0.5 + 0.5 * bend
    slope = half + 0.5 * v * (1.0 - bend * bend) * (scale * (1.0 + 0.134145 * square))
    return v * half, slope


def layer_norm(values, gain, shift):
    center = values - jnp.mean(values, axis=-1, keepdims=True)
    scale = lax.rsqrt(jnp.mean(center * center, axis=-1, keepdims=True) + NORM_EPSILON)
    normed = center * scale
    return normed * gain + shift, normed, scale


def norm_back(grad_out, gain, normed, scale):
    scaled = grad_out * gain
    return scale * (
        scaled
        - jnp.mean(scaled, axis=-1, keepdims=True)
        - normed * jnp.mean(scaled * normed, axis=-1, keepdims=True)
    )


def token_sum(values):
    return jnp.sum(values, axis=0, keepdims=True)


class Load:
    def __init__(self, src, dst, sem):
        self.copy, self.done = pltpu.make_async_copy(src, dst, sem), False
        self.copy.start()

    def wait(self):
        if not self.done:
            self.done = True
            self.copy.wait()


class Batch:
    def __init__(self, links, moves, total, send=None):
        self.total, self.recv, self.arrived, self.left = total, links.recv.at[links.used_recv], False, False
        links.used_recv += 1
        if send is None:
            send = links.send.at[links.used_send]
            links.used_send += 1
        self.send = send
        links.open.append(self)
        self.copies = []
        for src, dst, dp_mask, blk_mask in moves:
            copy = pltpu.make_async_remote_copy(
                src_ref=src,
                dst_ref=dst,
                send_sem=self.send,
                recv_sem=self.recv,
                device_id=(links.dp_peer(dp_mask), links.blk_peer(blk_mask)),
                device_id_type=pl.DeviceIdType.MESH,
            )
            copy.start()
            self.copies.append(copy)

    def wait_recv(self):
        if not self.arrived:
            self.arrived = True
            if len(self.copies) == 1:
                self.copies[0].wait_recv()
            else:
                pltpu.make_async_copy(self.total, self.total, self.recv).wait()

    def wait_send(self):
        if not self.left:
            self.left = True
            if len(self.copies) == 1:
                self.copies[0].wait_send()
            else:
                pltpu.make_async_copy(self.total, self.total, self.send).wait()


class Links:
    def __init__(self, send, recv, n_dp, n_blk):
        self.send, self.recv, self.used_send, self.used_recv, self.open = send, recv, 0, 0, []
        self.n_dp, self.n_blk = n_dp, n_blk
        self.dp, self.blk = lax.axis_index("dp"), lax.axis_index("blk")

    def dp_peer(self, mask):
        return jnp.bitwise_xor(self.dp, mask)

    def blk_peer(self, mask):
        return jnp.bitwise_xor(self.blk, mask)

    def greet(self):
        barrier = pltpu.get_barrier_semaphore()
        for mask in range(1, self.n_dp):
            pl.semaphore_signal(
                barrier, inc=1, device_id=(self.dp_peer(mask), self.blk), device_id_type=pl.DeviceIdType.MESH
            )
        for mask in range(1, self.n_blk):
            pl.semaphore_signal(
                barrier, inc=1, device_id=(self.dp, self.blk_peer(mask)), device_id_type=pl.DeviceIdType.MESH
            )

    def meet(self):
        pl.semaphore_wait(pltpu.get_barrier_semaphore(), self.n_dp + self.n_blk - 2)

    def finish(self):
        for batch in self.open:
            batch.wait_send()

    def stop(self):
        for batch in self.open:
            batch.wait_recv()
        for load in self.loads:
            load.wait()
        self.finish()

    def exchange(self, src, dst, first, size):
        part = pl.ds(first, size)
        moves = [(src.at[self.blk_peer(mask), part], dst.at[self.blk, part], 0, mask) for mask in range(1, self.n_blk)]
        batch = Batch(self, moves, dst.at[pl.ds(0, self.n_blk - 1), part])
        dst[self.blk, part] = src[self.blk, part]
        return batch


class Gather:
    def __init__(self, links, buf):
        self.links, self.buf, self.got = links, buf, {}
        self.bits = [1 << k for k in range(links.n_dp.bit_length() - 1)]
        self.forward(0)

    def forward(self, mask):
        low = mask & -mask if mask else self.links.n_dp
        if mask:
            self.got[mask].wait_recv()
        slot = self.buf.at[self.links.dp_peer(mask)]
        for bit in reversed(self.bits):
            if bit < low:
                self.got[mask | bit] = Batch(self.links, [(slot, slot, bit, 0)], slot)

    def relay(self):
        for mask in sorted(range(1, self.links.n_dp), key=lambda m: bin(m).count("1")):
            self.forward(mask)


def bit_names(n_dp, n_blk):
    blk = [("blk", 1 << k) for k in range(n_blk.bit_length() - 1)]
    dp = [("dp", 1 << k) for k in range(n_dp.bit_length() - 1)]
    return {"x": blk[:1], "z0": blk[1:2], "z1": blk[2:], "c": dp[:1], "y": dp[1:]}


class Chunk:
    def __init__(self, links, rows, part, out, landing, every, plan, measure):
        self.measure = measure
        names = bit_names(links.n_dp, links.n_blk)
        order, late = plan
        spread = lambda tokens: [bit for token in tokens for bit in names[token]]
        self.links, self.rows, self.part, self.out, self.landing = links, rows, part, out, landing
        self.halving = spread(order)
        back = [token for token in reversed(order) if token not in "cy"]
        back = back[:late] + ["y"] + back[late:] + ["c"]
        self.doubling = []
        for token in back:
            bits = names[token]
            self.doubling += bits if token in "cy" else bits[::-1]
        self.held = list(range(links.n_dp)) if every else [0]
        self.walk = self.steps()
        self.live = True

    def advance(self):
        self.live = next(self.walk, "end") != "end"

    def steps(self):
        links = self.links
        held, low, size, lows, at, last_batch = self.held, 0, self.rows, [], 0, None
        send = links.send.at[links.used_send]
        links.used_send += 1

        def move(moves, total):
            if last_batch is not None:
                last_batch.wait_send()
            return Batch(links, moves, total, send)

        for k, (axis, bit) in enumerate(self.halving):
            last = k + 1 == len(self.halving)
            if axis == "blk":
                half = size // 2
                mine = (links.blk // bit) % 2
                keep = pl.multiple_of(low + mine * half, 8)
                away = pl.multiple_of(low + (1 - mine) * half, 8)
                moves = [(mask, mask, away) for mask in held]
                lows.append(low)
                low, size = keep, half
            else:
                moves = [(mask, mask ^ bit, low) for mask in held if mask & bit]
                held = [mask for mask in held if not mask & bit]
            slots, copies, start = {}, [], at
            dp_mask, blk_mask = (0, bit) if axis == "blk" else (bit, 0)
            for mask, there, row in moves:
                slots[there] = self.landing.at[pl.ds(at, size), :]
                at += size
                copies.append((self.part(mask, row, size), slots[there], dp_mask, blk_mask))
            last_batch = move(copies, self.landing.at[pl.ds(start, at - start), :])
            yield
            last_batch.wait_recv()
            for mask in held:
                own = self.part(mask, low, size)
                goal = self.out(mask, low, size) if last else own
                goal[...] = own[...] + slots[mask][...]
        for axis, bit in self.doubling:
            place = [self.out(mask, low, size) for mask in held]
            dp_mask, blk_mask = (0, bit) if axis == "blk" else (bit, 0)
            total = self.measure.at[pl.ds(0, size * len(held)), pl.ds(0, place[0].shape[1])]
            last_batch = move([(v, v, dp_mask, blk_mask) for v in place], total)
            if axis == "blk":
                low, size = lows.pop(), size * 2
            else:
                held = held + [mask | bit for mask in held]
            yield
            last_batch.wait_recv()


def landing_rows(rows, order, n_dp, n_blk, every):
    names, held, total = bit_names(n_dp, n_blk), n_dp if every else 1, 0
    for token in order:
        for axis, _ in names[token]:
            if axis == "blk":
                rows //= 2
            else:
                held //= 2
            total += held * rows
    return total


VEC_ROWS = 16


def whole_kernel(
    n_dp, n_blk, x_hbm, lengths, cot_hbm, log_rate, frequency, out_coef, glu_hbm, in_hbm, out_hbm,
    n1g_hbm, n1b_hbm, log_step_hbm, skip_hbm, glu_b_hbm, n2g_hbm, n2b_hbm, in_b_hbm, out_b_hbm,
    block_out, grad_in, sum_glu, sum_in, sum_out, vec_out, par_out,
    send_sems, recv_sems, load_sems, x_ref, cot_ref, n1g, n1b, log_step, skip_gain, glu_b, n2g, n2b, in_b, out_b, glu_w, ffn_in, ffn_out, windows, rate_own, freq_own, coef_own, columns,
    a_send, x_all, y_send, y_all, dy_send, dy_all, dx_send, dx_all,
    q_ref, t_ref, h_ref, consts, base, taps, a_ref, b_ref, g_ref,
    result_all, feed_all, dglu, hidden_grad, slice_grad, hidden_s, pre_s, slope_keep, unit_keep, residual_keep, gate_keep,
    gelu_keep, acc_out, acc_feed, residual_grad, part_glu, part_in, part_out,
    own_par, dp_par, sum_par, blk_par, all_par, flat_par, vec, dp_vec, sum_vec, blk_vec, *landings,
):
    rows, width = x_ref.shape
    ff = ffn_in.shape[1]
    chans = width // n_blk
    quarter = chans // n_dp
    size = min(GROUP, chans)
    parts = [(first, size) for first in range(0, chans, size)]
    first_parts = [(0, chans)] if FIRST_WHOLE else parts
    links = Links(send_sems, recv_sems, n_dp, n_blk)
    dp, blk = links.dp, links.blk
    first = pl.multiple_of(blk * chans, 8)
    lanes_at = pl.multiple_of(blk * chans // 128 * 128, 128)

    links.loads = []
    sources = {
        "x": (x_hbm, x_ref), "n1g": (n1g_hbm, n1g), "n1b": (n1b_hbm, n1b), "cot": (cot_hbm, cot_ref),
        "rate": (log_rate.at[:, pl.ds(lanes_at, 128)], windows.at[0]),
        "freq": (frequency.at[:, pl.ds(lanes_at, 128)], windows.at[1]),
        "coef": (out_coef.at[:, :, pl.ds(lanes_at, 128)], windows.at[pl.ds(2, 2)]),
        "step": (log_step_hbm, log_step), "skip": (skip_hbm, skip_gain), "out": (out_hbm, ffn_out),
        "glu": (glu_hbm, glu_w), "glu_b": (glu_b_hbm, glu_b), "n2g": (n2g_hbm, n2g), "n2b": (n2b_hbm, n2b),
        "in": (in_hbm, ffn_in), "in_b": (in_b_hbm, in_b), "out_b": (out_b_hbm, out_b),
    }
    loads = {}

    def fetch(names):
        for name in names:
            loads[name] = Load(*sources[name], load_sems.at[len(loads)])
            links.loads.append(loads[name])

    def need(*names):
        for name in names:
            loads[name].wait()

    links.greet()
    fetch(list(sources))
    need("x", "n1g", "n1b")

    places = blk * rows + iota((rows, 1), 0)
    live = (places < lengths[0]).astype(F32)
    inputs = x_ref[...].astype(F32)
    normed, unit, scale1 = layer_norm(inputs, n1g[...], n1b[...])
    unit_keep[...] = unit
    mixed = normed.astype(BF16) * live.astype(BF16)
    flip = jnp.where(iota((rows, rows), 0) + iota((rows, rows), 1) == rows - 1, 1.0, 0.0).astype(BF16)
    a_send[...] = nn(flip, mixed).T
    links.meet()
    to_x = [links.exchange(a_send.reshape(n_blk, chans, rows), x_all, *part) for part in first_parts]
    need("cot")
    cot = cot_ref[...].astype(F32)
    result = live * cot
    result_all[dp] = result
    gather_result = Gather(links, result_all)

    need("step", "skip", "rate", "freq", "coef")
    columns[0] = jnp.broadcast_to(log_step[...], (128, width)).T
    columns[1] = jnp.broadcast_to(skip_gain[...], (128, width)).T
    own_skip = columns[1, pl.ds(first, chans), :]
    turn = (128 - blk * chans % 128) % 128
    own = [pltpu.roll(windows[k], turn, 1).T[:chans] for k in range(4)]
    rate_own[...], freq_own[...], coef_own[0], coef_own[1] = own

    def ssm():
        return columns[0, pl.ds(first, chans), :], rate_own[...], freq_own[...], (coef_own[0], coef_own[1])

    kern_slot = ssm_setup(n_blk, ssm(), consts, base)
    lead_slot = kern_slot - 1
    base_flat = base.reshape(8 * chans, 128)
    groups(0, chans, lambda group: make_powers(group, chans, consts, kern_slot, base_flat, q_ref, taps))
    shift_taps(own_skip, taps, base)

    x_flat = x_all.reshape(n_blk * chans, 128)
    y_flat = y_send.reshape(n_blk * chans, 128)
    to_y = []
    for k, part in enumerate(parts):
        groups(*part, lambda group: make_band(group, chans, base_flat, t_ref))
        if k < len(to_x):
            to_x[k].wait_recv()
        groups(*part, lambda group: forward_group(group, chans, n_blk, consts, lead_slot, x_flat, q_ref, t_ref, h_ref, y_flat))
        to_y.append(links.exchange(y_send, y_all, *part))

    gather_result.relay()
    need("out")
    low = result.astype(BF16)
    step = ff // 4
    for k in range(4):
        hidden_grad[:, k * step : (k + 1) * step] = nt(low, ffn_out[k * step : (k + 1) * step, :])
    part_ff = ff // n_dp
    rows_s = pl.multiple_of(dp * part_ff, 128)
    out_slice = ffn_out[pl.ds(rows_s, part_ff), :]
    for k in range(n_dp):
        slice_grad[k * rows : (k + 1) * rows, :] = nt(result_all[k].astype(BF16), out_slice)
    need("glu", "glu_b", "n2g", "n2b", "in", "in_b", "out_b")

    for batch in to_y:
        batch.wait_recv()
    conv = y_all.reshape(width, rows)[...].T
    gelu_out, gelu_slope = gelu_parts(conv)
    slope_keep[...] = gelu_slope
    gelu_low = gelu_out.astype(BF16)
    gelu_keep[...] = gelu_low
    glu_pre = nn(gelu_low, glu_w[...]) + glu_b[...]
    left = glu_pre[:, :width]
    gate = 0.5 + 0.5 * jnp.tanh(0.5 * glu_pre[:, width:])
    gate_keep[0] = left
    gate_keep[1] = gate
    residual = x_ref[...].astype(F32) + live * left * gate
    normed_mid, unit_mid, scale_mid = layer_norm(residual, n2g[...], n2b[...])
    feed = normed_mid.astype(BF16)
    feed_all[dp] = feed.astype(F32)
    gather_feed = Gather(links, feed_all)
    residual_keep[0] = residual
    residual_keep[1] = unit_mid

    pieces, arrivals = {}, {}

    def piece(work):
        pieces[work.__name__] = work

    @piece
    def own():
        for k in range(4):
            cut = slice(k * step, (k + 1) * step)
            hidden, slope = gelu_parts(nn(feed, ffn_in[:, cut]) + in_b[:, cut])
            grad_pre = (hidden_grad[:, cut] * slope).astype(BF16)
            forward = nn(hidden.astype(BF16), ffn_out[cut, :])
            back = nt(grad_pre, ffn_in[:, cut])
            acc_out[...] = forward if k == 0 else acc_out[...] + forward
            acc_feed[...] = back if k == 0 else acc_feed[...] + back
            vec[7 + k : 8 + k, :] = token_sum(grad_pre.astype(F32))
        block_out[...] = (residual_keep[0] + live * (acc_out[...] + out_b[...])).astype(BF16)

    @piece
    def glubwd():
        grad_feed = acc_feed[...]
        unit_mid = residual_keep[1]
        vec[2:3, :] = token_sum(grad_feed * unit_mid)
        vec[3:4, :] = token_sum(grad_feed)
        vec[4:5, :] = token_sum(result_all[dp])
        grad_res = cot_ref[...].astype(F32) + norm_back(grad_feed, n2g[...], unit_mid, scale_mid)
        residual_grad[...] = grad_res
        grad_left = live * grad_res
        left, gate = gate_keep[0], gate_keep[1]
        to_left = (grad_left * gate).astype(BF16)
        to_gate = (grad_left * left * gate * (1.0 - gate)).astype(BF16)
        dglu[:, :width] = to_left
        dglu[:, width:] = to_gate
        vec[5:6, :] = token_sum(to_left.astype(F32))
        vec[6:7, :] = token_sum(to_gate.astype(F32))

    @piece
    def dy():
        dy_send[...] = (nt(dglu[...], glu_w[...]) * slope_keep[...]).T
        arrivals["dy"] = links.exchange(dy_send.reshape(n_blk, chans, rows), dy_all, 0, chans)

    @piece
    def slice_all():
        gather_feed.relay()
        in_slice = ffn_in[:, pl.ds(rows_s, part_ff)]
        in_b_slice = in_b[:, pl.ds(rows_s, part_ff)]
        for k in range(n_dp):
            hidden, slope = gelu_parts(nn(feed_all[k].astype(BF16), in_slice) + in_b_slice)
            cut = slice(k * rows, (k + 1) * rows)
            hidden_s[cut, :] = hidden.astype(BF16)
            pre_s[cut, :] = (slice_grad[cut, :] * slope).astype(BF16)

    part_gl = 2 * width // n_dp
    shapes = piece_shapes(n_dp, n_blk, width, ff)
    chunks = {}

    def window(ref, row0, col0, rows_at, cols):
        def view(mask, row, size):
            slot = links.dp_peer(mask)
            row_at = pl.multiple_of(slot * rows_at[0] + row0 + row, 8)
            col_at = pl.multiple_of(slot * rows_at[1] + col0, 128) if rows_at[1] else col0
            return ref.at[pl.ds(row_at, size), pl.ds(col_at, cols)]
        return view

    def start_chunk(k):
        if k not in shapes:
            return
        kind, row0, col0, rows_k, cols_k, plan = shapes[k]
        rows_cut, cols_cut = slice(row0, row0 + rows_k), slice(col0, col0 + cols_k)
        if kind == "glu":
            part_glu[rows_cut, :] = tn(gelu_keep[:, rows_cut], dglu[...])
            part = window(part_glu, row0, 0, (0, part_gl), part_gl)
            total = window(sum_glu, row0, 0, (0, part_gl), part_gl)
        elif kind == "out":
            results = result_all[:, :, cols_cut].reshape(n_dp * rows, cols_k).astype(BF16)
            part_out[rows_cut, cols_cut] = tn(hidden_s[:, rows_cut], results)
            part = window(part_out, row0, col0, (0, 0), cols_k)
            total = window(sum_out, row0, col0, (part_ff, 0), cols_k)
        else:
            feeds = feed_all[:, :, rows_cut].reshape(n_dp * rows, rows_k).astype(BF16)
            part_in[rows_cut, cols_cut] = tn(feeds, pre_s[:, cols_cut])
            part = window(part_in, row0, col0, (0, 0), cols_k)
            total = window(sum_in, row0, col0, (0, part_ff), cols_k)
        chunks[k] = Chunk(links, rows_k, part, total, landings[k], kind == "glu", plan, sum_out)
        chunks[k].advance()

    dy_flat = dy_all.reshape(n_blk * chans, 128)
    dx_flat = dx_send.reshape(n_blk * chans, 128)

    def backward(k):
        if k == 0:
            arrivals["dy"].wait_recv()
        size = min(GROUP, chans)
        if k * size < chans:
            backward_group([k * size + i for i in range(size)], chans, n_blk, consts, lead_slot, x_flat, dy_flat, q_ref, t_ref, h_ref, dx_flat, a_ref, b_ref, g_ref)
        if k == 3:
            groups(4 * size, chans - 4 * size, lambda group: backward_group(group, chans, n_blk, consts, lead_slot, x_flat, dy_flat, q_ref, t_ref, h_ref, dx_flat, a_ref, b_ref, g_ref))
            arrivals["dx"] = links.exchange(dx_send, dx_all, 0, chans)

    @piece
    def near():
        split_lags(g_ref, base)
        groups(0, chans, lambda group: near_sums(group, chans, base_flat, q_ref, a_ref, b_ref))
        rate_freq, coefs, d_step, d_skip = finish(chans, ssm(), a_ref, b_ref, g_ref)
        own_par[:, 0, :] = rate_freq
        own_par[:, 1, :] = coefs
        lane = iota((chans, 128), 1)
        pair = jnp.where(lane == 0, d_step, jnp.where(lane == 1, d_skip, 0.0))
        if chans < 128:
            pair = jnp.concatenate([pair, jnp.zeros((128 - chans, 128), F32)], axis=0)
        pair = pair.T[0:8]
        if width > 128:
            pair = jnp.concatenate([pair, jnp.zeros((8, width - 128), F32)], axis=1)
        pair = pltpu.roll(pair, blk * chans, 1)
        vec[11:13, :] = pair[0:2]
        vec[13:16, :] = jnp.zeros((3, width), F32)

    @piece
    def ln1():
        arrivals["dx"].wait_recv()
        back = dx_all.reshape(width, rows)[...].T
        high, rest = split(back)
        rest, last = split(back - high.astype(F32))
        grad_normed = live * (nn(flip, high) + (nn(flip, rest) + nn(flip, last)))
        unit = unit_keep[...]
        vec[0:1, :] = token_sum(grad_normed * unit)
        vec[1:2, :] = token_sum(grad_normed)
        grad_in[...] = residual_grad[...] + norm_back(grad_normed, n1g[...], unit, scale1)

    @piece
    def s0():
        moves = [
            (own_par.at[pl.ds(links.dp_peer(mask) * quarter, quarter)], dp_par.at[dp], mask, 0) for mask in range(1, n_dp)
        ]
        arrivals["s0"] = [
            Batch(links, moves, dp_par.at[pl.ds(0, n_dp - 1)]),
            Batch(links, [(vec, dp_vec.at[dp], mask, 0) for mask in range(1, n_dp)], dp_vec.at[pl.ds(0, n_dp - 1)]),
        ]
        dp_par[dp] = own_par[pl.ds(dp * quarter, quarter)]
        dp_vec[dp] = vec[...]

    @piece
    def s1():
        for batch in arrivals["s0"]:
            batch.wait_recv()
        sum_par[...] = sum_slots(dp_par, n_dp)
        sum_vec[...] = sum_slots(dp_vec, n_dp)
        arrivals["s1"] = [
            Batch(links, [(src, dst.at[blk], 0, mask) for mask in range(1, n_blk)], dst.at[pl.ds(0, n_blk - 1)])
            for src, dst in ((sum_par, blk_par), (sum_vec, blk_vec))
        ]
        blk_par[blk] = sum_par[...]
        blk_vec[blk] = sum_vec[...]

    @piece
    def s2():
        for batch in arrivals["s1"]:
            batch.wait_recv()
        all_par[dp] = blk_par[...]
        arrivals["s2"] = Gather(links, all_par)
        vec_out[...] = sum_slots(blk_vec, n_blk)

    @piece
    def s3():
        arrivals["s2"].relay()
        state = par_out.shape[0] // 4
        for b in range(n_blk):
            for d in range(n_dp):
                at = b * chans + d * quarter
                block = all_par[d, b]
                flat_par[0, at : at + quarter, :] = block[:, 0, :]
                flat_par[1, at : at + quarter, :] = block[:, 1, :]
        par_out[: 2 * state, :] = flat_par[0].T
        par_out[2 * state :, :] = flat_par[1].T

    for token in ORDER:
        if isinstance(token, int):
            if token in chunks:
                chunks[token].advance()
        elif token.startswith("part"):
            start_chunk(int(token[4:]))
        elif token.startswith("bwd"):
            backward(int(token[3:]))
        else:
            pieces["slice_all" if token == "slice" else token]()
    while any(chunk.live for chunk in chunks.values()):
        for chunk in chunks.values():
            chunk.advance()
    links.finish()


def piece_shapes(n_dp, n_blk, width, ff):
    shapes = {}
    n_glu, n_ffn = len(GLU_PLANS), len(FFN_PLANS) // 2
    cuts = min(n_glu, width // (8 * n_blk))
    size = width // cuts
    for k, plan in enumerate(GLU_PLANS[:cuts]):
        shapes[k] = ("glu", k * size, 0, size, 2 * width // n_dp, plan)
    for kind, at, height, breadth in (("out", n_glu, ff // n_dp, width), ("in", n_glu + n_ffn, width, ff // n_dp)):
        cols = min(n_ffn, breadth // 128)
        cuts = min(n_ffn // cols, height // (8 * n_blk))
        high, wide = height // cuts, breadth // cols
        for k in range(cols * cuts):
            shapes[at + k] = (kind, k % cuts * high, k // cuts * wide, high, wide, FFN_PLANS[at - n_glu + k])
    return shapes


def sum_slots(ref, count):
    total = ref[0]
    for k in range(1, count):
        total = total + ref[k]
    return total


def deliver_kernel(big_in, vec, par, others, big_out, rows_out, rate, freq, coef, others_out, sems):
    states = rate.shape[0]
    moves = []
    for src, dst in zip(big_in, big_out):
        part = src.shape[0] // BIG_PARTS
        moves += [(src.at[pl.ds(k * part, part)], dst.at[pl.ds(k * part, part)]) for k in range(BIG_PARTS)]
    moves += list(zip(others, others_out))
    moves += [(par.at[pl.ds(0, states)], rate), (par.at[pl.ds(states, states)], freq)]
    moves += [(par.at[pl.ds((2 + k) * states, states)], coef.at[k]) for k in range(2)]
    copies = [pltpu.make_async_copy(src, dst, sems.at[k]) for k, (src, dst) in enumerate(moves)]
    for copy in copies:
        copy.start()
    row = 0
    for out in rows_out:
        count = out.shape[1] // vec.shape[1]
        for k in range(count):
            out[:, k * vec.shape[1] : (k + 1) * vec.shape[1]] = vec[row : row + 1, :]
            row += 1
    for copy in copies:
        copy.wait()


def on_device(n_dp, n_blk, block_in, seq_lengths, norm1_gain, norm1_bias, log_step, log_rate, frequency, out_coef, skip_gain, glu_weight, glu_bias, norm2_gain, norm2_bias, ffn_in, ffn_in_bias, ffn_out, ffn_out_bias, cotangent):
    _, rows, width = block_in.shape
    ff = ffn_in.shape[1]
    states = log_rate.shape[1]
    chans, quarter = width // n_blk, width // n_blk // n_dp
    row = lambda v: v.reshape(1, -1)
    vmem, anywhere = pl.BlockSpec(memory_space=VMEM), pl.BlockSpec(memory_space=pl.ANY)
    shape = jax.ShapeDtypeStruct
    outs = [
        shape((rows, width), BF16), shape((rows, width), F32),
        shape((width, 2 * width), F32), shape((width, ff), F32), shape((ff, width), F32),
        shape((VEC_ROWS, width), F32), shape((4 * states, width), F32),
    ]
    part_ff, part_gl = ff // n_dp, 2 * width // n_dp
    tokens = n_dp * rows
    f32 = lambda *dims: VMEM(dims, F32)
    bf16 = lambda *dims: VMEM(dims, BF16)
    dma = lambda n: pltpu.SemaphoreType.DMA((n,))
    shapes = piece_shapes(n_dp, n_blk, width, ff)
    landings = []
    for k in range(len(GLU_PLANS) + len(FFN_PLANS)):
        kind, _, _, rows_k, cols_k, plan = shapes.get(k, ("out", 0, 0, 8 * n_blk, 128, FFN_PLANS[0]))
        landings.append(f32(landing_rows(rows_k, plan[0], n_dp, n_blk, kind == "glu"), cols_k))
    scratch = [
        dma(SEND_SEMS), dma(RECV_SEMS), dma(20),
        bf16(rows, width), bf16(rows, width), f32(1, width), f32(1, width), f32(1, width), f32(1, width), f32(1, 2 * width),
        f32(1, width), f32(1, width), f32(1, ff), f32(1, width),
        bf16(width, 2 * width), bf16(width, ff), bf16(ff, width),
        f32(4, states, 128), f32(chans, states), f32(chans, states), f32(2, chans, states), f32(2, width, 128),
        f32(width, rows), f32(n_blk, chans, rows), f32(n_blk, chans, rows), f32(n_blk, chans, rows),
        f32(width, rows), f32(n_blk, chans, rows), f32(n_blk, chans, rows), f32(n_blk, chans, rows),
        bf16(chans, 256, 128), bf16(chans, 256, 128), f32(chans, n_blk, 128), f32(n_consts(n_blk), chans, 128),
        f32(8, chans, 128), f32(chans, 128), f32(2 * chans, 128), f32(2 * chans, 128), f32(chans, 128),
        f32(n_dp, rows, width), f32(n_dp, rows, width),
        bf16(rows, 2 * width),
        f32(rows, ff), f32(tokens, part_ff), bf16(tokens, part_ff), bf16(tokens, part_ff),
        f32(rows, width), f32(rows, width), f32(2, rows, width), f32(2, rows, width),
        bf16(rows, width), f32(rows, width), f32(rows, width), f32(rows, width),
        f32(width, 2 * width), f32(width, part_ff), f32(part_ff, width),
        f32(chans, 2, 128), f32(n_dp, quarter, 2, 128), f32(quarter, 2, 128), f32(n_blk, quarter, 2, 128),
        f32(n_dp, n_blk, quarter, 2, 128), f32(2, width, 128),
        f32(VEC_ROWS, width), f32(n_dp, VEC_ROWS, width), f32(VEC_ROWS, width), f32(n_blk, VEC_ROWS, width),
        *landings,
    ]
    out = pl.pallas_call(
        functools.partial(whole_kernel, n_dp, n_blk),
        out_shape=[VMEM(v.shape, v.dtype) for v in outs],
        out_specs=[vmem] * len(outs),
        in_specs=[anywhere, pl.BlockSpec(memory_space=pltpu.SMEM)] + [anywhere] * 16,
        scratch_shapes=scratch,
        compiler_params=pltpu.CompilerParams(collective_id=0, has_side_effects=True, vmem_limit_bytes=44 * 2**20),
    )(
        block_in[0], seq_lengths, cotangent[0], log_rate.T, frequency.T, out_coef.swapaxes(1, 2), glu_weight, ffn_in, ffn_out,
        row(norm1_gain), row(norm1_bias), row(log_step), row(skip_gain), row(glu_bias), row(norm2_gain), row(norm2_bias),
        row(ffn_in_bias), row(ffn_out_bias),
    )
    block_out, grad_in, g_glu, g_in, g_out, vec, par = out
    widths = [width, width, width, width, width, 2 * width, ff, width, width]
    made = [shape((rows, width), BF16), shape((rows, width), F32)]
    big = [shape(v.shape, F32) for v in (g_glu, g_in, g_out)]
    small = [shape((1, w), F32) for w in widths]
    params = [shape((states, width), F32), shape((states, width), F32), shape((2, states, width), F32)]
    out_shapes = made + big + small + params

    def deliver(block_out, grad_in, g_glu, g_in, g_out, vec, par, *rest):
        outs, sems = rest[:-1], rest[-1]
        deliver_kernel([g_glu, g_in, g_out], vec, par, [block_out, grad_in], outs[2:5], outs[5:14], *outs[14:], outs[:2], sems)

    done = pl.pallas_call(
        deliver,
        out_shape=out_shapes,
        in_specs=[vmem] * 7,
        out_specs=[anywhere] * 5 + [vmem] * 9 + [anywhere] * 3,
        scratch_shapes=[dma(32)],
        compiler_params=pltpu.CompilerParams(vmem_limit_bytes=8 * 2**20),
    )(*out)
    flat = [v.reshape(-1) for v in done[5:14]]
    n1_gain, n1_bias, n2_gain, n2_bias, ffn_out_b, glu_b, ffn_in_b, d_step, d_skip = flat
    return (
        done[0][None], done[1][None], n1_gain, n1_bias, d_step, done[14].T, done[15].T, done[16].swapaxes(1, 2), d_skip,
        done[2], glu_b, n2_gain, n2_bias, done[3], ffn_in_b, done[4], ffn_out_b,
    )


def solution(mesh):
    split_spec, whole = P("dp", "blk", None), P()
    return jax.shard_map(
        functools.partial(on_device, mesh.shape["dp"], mesh.shape["blk"]),
        mesh=mesh,
        in_specs=(split_spec, P("dp")) + (whole,) * 15 + (split_spec,),
        out_specs=(split_spec, split_spec) + (whole,) * 15,
        check_vma=False,
    )
```

```python
import functools

import jax
import jax.numpy as jnp
from jax import lax
from jax.experimental import pallas as pl
from jax.experimental.pallas import tpu as pltpu
from jax.sharding import PartitionSpec as P

NORM_EPSILON = 1e-05
F32 = jnp.float32
BF16 = jnp.bfloat16
PRECISE = lax.Precision.HIGHEST
SERIES = 16
GROUP = 16
SEND_SEMS = 43
RECV_SEMS = 191
BIG_PARTS = 1
FIRST_WHOLE = False
GLU_PLANS = (
    (("c", "x", "z0", "y", "z1"), 3),
    (("c", "y", "x", "z0", "z1"), 3),
    (("c", "z0", "x", "y", "z1"), 2),
    (("c", "y", "x", "z0", "z1"), 3),
)
FFN_PLANS = (
    (("x", "z0", "z1"), 2),
    (("x", "z1", "z0"), 2),
    (("z1", "x", "z0"), 3),
    (("x", "z0", "z1"), 2),
    (("x", "z0", "z1"), 2),
    (("z0", "x", "z1"), 2),
    (("x", "z0", "z1"), 2),
    (("x", "z0", "z1"), 2),
    (("z1", "x", "z0"), 1),
    (("x", "z0", "z1"), 3),
    (("x", "z0", "z1"), 3),
    (("z0", "x", "z1"), 0),
    (("x", "z1", "z0"), 2),
    (("x", "z0", "z1"), 3),
    (("x", "z0", "z1"), 1),
    (("x", "z0", "z1"), 0),
)
ORDER = (
    "own", "glubwd", "dy", "part0", "part1", "part2", "part3", 0, 1, 2, 3, "slice", "part4", "part5", "part6",
    0, "part7", 1, "part8", "part9", "part10", 2, "part11", "part12", "part13", "part14", 4, "part15",
    "part16", 3, "part17", "part18", 5, "part19", 0, 6, "bwd0", 7, 9, 1, 0, 8, 4, 12, "bwd1", 7, 5, 1, 10, 0,
    11, 8, 15, 2, 4, "bwd2", 7, 5, 1, 14, 8, 11, 13, 10, 0, 16, 3, 2, 7, 5, 4, "bwd3", 1, 8, 14, 11, 17, 13,
    19, 10, 0, 18, 6, "late", "near", 9, 7, 12, 5, 3, 16, 2, 15, 4, 7, 0, 5, 1, 8, "ln1", 14, 11, 17, 7, 4, "s0", 13,
    19, 0, 10, 18, 6, 7, 8, 5, 9, 12, 0, 3, 16, 1, 2, "s1", 5, 15, 14, 11, 17, 4, 13, 19, 10, 1, 6, 18, 15, 4,
    8, 9, 12, 2, 11, 3, 16, 19, 1, "s2", 8, 14, 10, 9, 12, 17, 13, 6, 18, 2, 3, 15, 11, 16, 14, "s3", 11, 19,
    17, 9, 18, 10, 16, 6, 12, 10, 2, 13, 14, 19, 3, 2, 15, 14, 6, 9, 17, 18, 6, 9, 13, 16, 13, 16, 3, 19, 12,
    15, 3, 17, 19, 18, 12, 15, 17, 18,
)
VMEM = pltpu.VMEM


def iota(shape, axis):
    return lax.broadcasted_iota(jnp.int32, shape, axis)


def is_left(shape):
    half = shape[-1] // 2
    return iota(shape, len(shape) - 1) < half


def swap(v):
    return pltpu.roll(v, v.shape[-1] // 2, v.ndim - 1)


def times(v, const):
    return v * const[0] + swap(v) * const[1]


def split(v):
    high = v.astype(BF16)
    return high, (v - high.astype(F32)).astype(BF16)


def nn(a, b):
    return lax.dot_general(a, b, (((1,), (0,)), ((), ())), preferred_element_type=F32)


def nt(a, b):
    return lax.dot_general(a, b, (((1,), (1,)), ((), ())), preferred_element_type=F32)


def tn(a, b):
    return lax.dot_general(a, b, (((0,), (0,)), ((), ())), preferred_element_type=F32)


def cmul(a, b):
    return a[0] * b[0] - a[1] * b[1], a[0] * b[1] + a[1] * b[0]


def twice(v):
    return jnp.concatenate([v, v], axis=-1)


def pole_parts(log_step, log_rate, frequency):
    step = jnp.exp(log_step)
    rate = jnp.exp(twice(log_rate))
    pole = (-rate, step * twice(frequency))
    phi = (jnp.zeros_like(rate), jnp.zeros_like(rate))
    slope = (jnp.zeros_like(rate), jnp.zeros_like(rate))
    fact = [1.0]
    for k in range(1, SERIES + 2):
        fact.append(fact[-1] * k)
    for k in range(SERIES, -1, -1):
        phi = cmul(phi, pole)
        phi = (phi[0] + 1.0 / fact[k + 1], phi[1])
    for k in range(SERIES, 0, -1):
        slope = cmul(slope, pole)
        slope = (slope[0] + k / fact[k + 1], slope[1])
    grow = cmul(pole, phi)
    z = (1.0 + grow[0], grow[1])
    return step, rate, z, phi, slope


def as_const(value):
    sign = jnp.where(is_left(value[0].shape), -1.0, 1.0)
    return value[0], value[1] * sign


def packed(value):
    return jnp.where(is_left(value[0].shape), value[0], value[1])


def ssm_setup(rows, ssm, consts, base):
    log_step, log_rate, frequency, coef = ssm
    step, rate, z, phi, slope = pole_parts(log_step, log_rate, frequency)
    b = (twice(coef[0]), twice(coef[1]))
    residue = cmul(b, (step * phi[0], step * phi[1]))
    power = (jnp.ones_like(rate), jnp.zeros_like(rate))
    for r in range(8):
        base[r] = packed(power)
        power = cmul(power, z)
    slot = 0

    def keep(value):
        nonlocal slot
        c = as_const(value)
        consts[2 * slot] = c[0]
        consts[2 * slot + 1] = c[1]
        slot += 1

    for k in range(4):
        keep(power)
        power = cmul(power, power)
    for k in range((rows - 1).bit_length()):
        keep(power)
        power = cmul(power, power)
    lead = cmul(residue, z)
    lead = (2.0 * lead[0], 2.0 * lead[1])
    sign = jnp.where(is_left(rate.shape), 1.0, -1.0)
    consts[2 * slot] = lead[0] * sign
    consts[2 * slot + 1] = -lead[1]
    slot += 1
    kern = jnp.where(is_left(rate.shape), 2.0 * residue[0], -2.0 * residue[1])
    kern_high = kern.astype(BF16).astype(F32)
    consts[2 * slot] = kern_high
    consts[2 * slot + 1] = kern - kern_high
    return slot


def row_of(ref, index, chan):
    return ref[index, pl.ds(chan, 1), :]


def const_of(consts, slot, chan):
    return row_of(consts, 2 * slot, chan), row_of(consts, 2 * slot + 1, chan)


def make_powers(group, chans, consts, kern_slot, base_flat, q_ref, taps_ref):
    every = [base_flat[pl.ds(chan, 8, stride=chans), :] for chan in group]
    for k in range(4):
        every = [
            jnp.concatenate([powers, times(powers, const_of(consts, k, chan))], axis=0)
            for chan, powers in zip(group, every)
        ]
    parts = [split(powers) for powers in every]
    for chan, (high, rest) in zip(group, parts):
        q_ref[chan, :128, :] = high
        q_ref[chan, 128:, :] = rest
    kerns = []
    for chan, (high, rest) in zip(group, parts):
        taps = [row_of(consts, 2 * kern_slot + k, chan) for k in range(2)]
        taps = jnp.concatenate([taps[0], taps[1]], axis=0).astype(BF16)
        kerns.append(nt(twice(taps), jnp.concatenate([high, rest], axis=1)))
    for chan, kern in zip(group, kerns):
        taps_ref[pl.ds(chan, 1), :] = kern[0:1] + kern[1:2]


def shift_taps(skip, taps_ref, base):
    taps = taps_ref[...]
    taps = taps + jnp.where(iota(taps.shape, 1) == 0, skip, 0.0)
    for r in range(8):
        base[r] = taps if r == 7 else pltpu.roll(taps, 7 - r, 1)


def make_band(group, chans, base_flat, t_ref):
    for chan in group:
        tile = base_flat[pl.ds(chan, 8, stride=chans), :]
        band = jnp.concatenate([pltpu.roll(tile, 120 - 8 * m, 1) if m < 15 else tile for m in range(16)], axis=0)
        band = jnp.where(iota((128, 128), 0) + iota((128, 128), 1) >= 127, band, 0.0)
        t_high, t_rest = split(band)
        t_ref[chan, :128, :] = t_high
        t_ref[chan, 128:, :] = t_rest


def scan(values, consts, first, group, reverse):
    rows = values[0].shape[0]
    places = iota(values[0].shape, 0)

    def moved(x, d):
        if reverse:
            return jnp.where(places < rows - d, pltpu.roll(x, rows - d, 0), 0.0)
        return jnp.where(places >= d, pltpu.roll(x, d, 0), 0.0)

    values = [moved(v, 1) for v in values]
    d, k = 1, 0
    while d < rows:
        values = [v + times(moved(v, d), const_of(consts, first + k, chan)) for v, chan in zip(values, group)]
        d, k = 2 * d, k + 1
    return values


def wide(chan, q_ref, t_ref):
    return jnp.concatenate([q_ref[chan], t_ref[chan]], axis=1)


def far_parts(states, consts, lead_slot, group, q_ref):
    rows = states[0].shape[0]
    outs = []
    for chan, state in zip(group, states):
        high, rest = split(times(state, const_of(consts, lead_slot, chan)))
        both = twice(jnp.concatenate([high, rest], axis=0))
        outs.append(nt(both, jnp.concatenate([q_ref[chan, :128, :], q_ref[chan, 128:, :]], axis=1)))
    return [out[:rows] + out[rows:] for out in outs]


def forward_group(group, chans, rows, consts, lead_slot, x_flat, q_ref, t_ref, h_ref, y_flat):
    outs = [
        nn(twice(x_flat[pl.ds(chan, rows, stride=chans), :].astype(BF16)), wide(chan, q_ref, t_ref))
        for chan in group
    ]
    states = scan([out[:, :128] for out in outs], consts, 4, group, False)
    for chan, state in zip(group, states):
        h_ref[chan] = state
    fars = far_parts(states, consts, lead_slot, group, q_ref)
    for chan, out, far in zip(group, outs, fars):
        y_flat[pl.ds(chan, rows, stride=chans), :] = out[:, 128:] + far


def backward_group(group, chans, rows, consts, lead_slot, x_flat, dy_flat, q_ref, t_ref, h_ref, dx_flat, a_ref, b_ref, g_ref):
    places = iota((1, 128), 1).astype(F32)
    us = [x_flat[pl.ds(chan, rows, stride=chans), :] for chan in group]
    dys = [dy_flat[pl.ds(chan, rows, stride=chans), :] for chan in group]
    outs = []
    for chan, u, dy in zip(group, us, dys):
        high = dy.astype(BF16).astype(F32)
        left = twice(jnp.concatenate([high, dy - high, dy * places, u * places], axis=0).astype(BF16))
        outs.append(nn(left, wide(chan, q_ref, t_ref)))
    pairs = [tn(u.astype(BF16), dy.astype(BF16)) for u, dy in zip(us, dys)]
    d0s = [out[:rows, :128] + out[rows : 2 * rows, :128] for out in outs]
    d1s = [out[2 * rows : 3 * rows, :128] for out in outs]
    hs = [h_ref[chan] for chan in group]
    ends = scan(d0s, consts, 4, group, True)
    fars = far_parts(ends, consts, lead_slot, group, q_ref)
    for chan, out, far in zip(group, outs, fars):
        dx_flat[pl.ds(chan, rows, stride=chans), :] = out[:rows, 128:] + out[rows : 2 * rows, 128:] + far
    h1s = scan(
        [out[3 * rows :, :128] + 128.0 * times(h, const_of(consts, 4, chan)) for chan, out, h in zip(group, outs, hs)],
        consts, 4, group, False,
    )
    mask = is_left(hs[0].shape)

    def prod(p, q):
        q_swap = swap(q)
        return p * jnp.where(mask, q, q_swap) + swap(p) * jnp.where(mask, -q_swap, q)

    for chan, d0, d1, h, h1 in zip(group, d0s, d1s, hs, h1s):
        a_far = jnp.sum(prod(d0, h), axis=0, keepdims=True)
        b_far = a_far + jnp.sum(prod(d1, h) + prod(d0, h1), axis=0, keepdims=True)
        a_ref[pl.ds(chans + chan, 1), :] = a_far
        b_ref[pl.ds(chans + chan, 1), :] = b_far
    keep = iota((128, 128), 1) <= iota((128, 128), 0)
    for chan, pair in zip(group, pairs):
        skew = jnp.where(keep, pltpu.roll(pair, 1, 1, stride=1, stride_axis=0), 0.0)
        g_ref[pl.ds(chan, 1), :] = jnp.sum(skew, axis=0, keepdims=True)


def split_lags(g_ref, base):
    lags = g_ref[...]
    weighted = lags * iota(lags.shape, 1).astype(F32)
    for k, v in enumerate((lags, weighted)):
        high = v.astype(BF16).astype(F32)
        base[k] = high
        base[2 + k] = v - high
        base[4 + k] = jnp.zeros_like(v)
        base[6 + k] = jnp.zeros_like(v)


def near_sums(group, chans, base_flat, q_ref, a_ref, b_ref):
    outs = [nn(twice(base_flat[pl.ds(chan, 8, stride=chans), :].astype(BF16)), q_ref[chan]) for chan in group]
    for chan, out in zip(group, outs):
        a_ref[pl.ds(chan, 1), :] = out[0:1] + out[2:3]
        b_ref[pl.ds(chan, 1), :] = out[1:2] + out[3:4]


def groups(first, count, body, size=GROUP):
    size = min(size, count)

    def step(k, carry):
        body([first + k * size + i for i in range(size)])
        return carry

    if count > 0:
        lax.fori_loop(0, count // size, step, 0)


def finish(chans, ssm, a_ref, b_ref, g_ref):
    log_step, log_rate, frequency, coef = ssm
    step, rate, z, phi, slope = pole_parts(log_step, log_rate, frequency)
    b = (twice(coef[0]), twice(coef[1]))

    def dup(v):
        left = is_left(v.shape)
        moved = swap(v)
        return jnp.where(left, v, moved), jnp.where(left, moved, v)

    def total(ref):
        near, far = dup(ref[:chans, :]), dup(ref[chans:, :])
        far = cmul(far, z)
        return near[0] + far[0], near[1] + far[1]

    a, bb = total(a_ref), total(b_ref)
    residue = cmul(b, (step * phi[0], step * phi[1]))
    g_res = (2.0 * a[0], -2.0 * a[1])
    rb = cmul(residue, bb)
    g_pole = (2.0 * rb[0], -2.0 * rb[1])
    conj = lambda v: (v[0], -v[1])
    g_coef = cmul(conj((step * phi[0], step * phi[1])), g_res)
    bs = cmul(b, (step * slope[0], step * slope[1]))
    more = cmul(conj(bs), g_res)
    g_pole = (g_pole[0] + more[0], g_pole[1] + more[1])
    d_rate = -rate * g_pole[0]
    d_freq = step * g_pole[1]
    by_step = cmul(conj(cmul(b, phi)), g_res)[0] + g_pole[1] * twice(frequency)
    left = is_left(by_step.shape)
    d_step = step * jnp.sum(jnp.where(left, by_step, 0.0), axis=1, keepdims=True)
    return jnp.where(left, d_rate, d_freq), jnp.where(left, g_coef[0], g_coef[1]), d_step, g_ref[:, 0:1]


def n_consts(rows):
    return 2 * (4 + (rows - 1).bit_length() + 2)


def gelu_parts(v):
    scale = 0.7978845608028654
    square = v * v
    bend = jnp.tanh(scale * v * (1.0 + 0.044715 * square))
    half = 0.5 + 0.5 * bend
    slope = half + 0.5 * v * (1.0 - bend * bend) * (scale * (1.0 + 0.134145 * square))
    return v * half, slope


def layer_norm(values, gain, shift):
    center = values - jnp.mean(values, axis=-1, keepdims=True)
    scale = lax.rsqrt(jnp.mean(center * center, axis=-1, keepdims=True) + NORM_EPSILON)
    normed = center * scale
    return normed * gain + shift, normed, scale


def norm_back(grad_out, gain, normed, scale):
    scaled = grad_out * gain
    return scale * (
        scaled
        - jnp.mean(scaled, axis=-1, keepdims=True)
        - normed * jnp.mean(scaled * normed, axis=-1, keepdims=True)
    )


def token_sum(values):
    return jnp.sum(values, axis=0, keepdims=True)


class Load:
    def __init__(self, src, dst, sem):
        self.copy, self.done = pltpu.make_async_copy(src, dst, sem), False
        self.copy.start()

    def wait(self):
        if not self.done:
            self.done = True
            self.copy.wait()


class Batch:
    def __init__(self, links, moves, total, send=None):
        self.total, self.recv, self.arrived, self.left = total, links.recv.at[links.used_recv], False, False
        links.used_recv += 1
        if send is None:
            send = links.send.at[links.used_send]
            links.used_send += 1
        self.send = send
        links.open.append(self)
        self.copies = []
        for src, dst, dp_mask, blk_mask in moves:
            copy = pltpu.make_async_remote_copy(
                src_ref=src,
                dst_ref=dst,
                send_sem=self.send,
                recv_sem=self.recv,
                device_id=(links.dp_peer(dp_mask), links.blk_peer(blk_mask)),
                device_id_type=pl.DeviceIdType.MESH,
            )
            copy.start()
            self.copies.append(copy)

    def wait_recv(self):
        if not self.arrived:
            self.arrived = True
            if len(self.copies) == 1:
                self.copies[0].wait_recv()
            else:
                pltpu.make_async_copy(self.total, self.total, self.recv).wait()

    def wait_send(self):
        if not self.left:
            self.left = True
            if len(self.copies) == 1:
                self.copies[0].wait_send()
            else:
                pltpu.make_async_copy(self.total, self.total, self.send).wait()


class Links:
    def __init__(self, send, recv, n_dp, n_blk):
        self.send, self.recv, self.used_send, self.used_recv, self.open = send, recv, 0, 0, []
        self.n_dp, self.n_blk = n_dp, n_blk
        self.dp, self.blk = lax.axis_index("dp"), lax.axis_index("blk")

    def dp_peer(self, mask):
        return jnp.bitwise_xor(self.dp, mask)

    def blk_peer(self, mask):
        return jnp.bitwise_xor(self.blk, mask)

    def greet(self):
        barrier = pltpu.get_barrier_semaphore()
        for mask in range(1, self.n_dp):
            pl.semaphore_signal(
                barrier, inc=1, device_id=(self.dp_peer(mask), self.blk), device_id_type=pl.DeviceIdType.MESH
            )
        for mask in range(1, self.n_blk):
            pl.semaphore_signal(
                barrier, inc=1, device_id=(self.dp, self.blk_peer(mask)), device_id_type=pl.DeviceIdType.MESH
            )

    def meet(self):
        pl.semaphore_wait(pltpu.get_barrier_semaphore(), self.n_dp + self.n_blk - 2)

    def finish(self):
        for batch in self.open:
            batch.wait_send()

    def stop(self):
        for batch in self.open:
            batch.wait_recv()
        for load in self.loads:
            load.wait()
        self.finish()

    def exchange(self, src, dst, first, size):
        part = pl.ds(first, size)
        moves = [(src.at[self.blk_peer(mask), part], dst.at[self.blk, part], 0, mask) for mask in range(1, self.n_blk)]
        batch = Batch(self, moves, dst.at[pl.ds(0, self.n_blk - 1), part])
        dst[self.blk, part] = src[self.blk, part]
        return batch


class Gather:
    def __init__(self, links, buf):
        self.links, self.buf, self.got = links, buf, {}
        self.bits = [1 << k for k in range(links.n_dp.bit_length() - 1)]
        self.forward(0)

    def forward(self, mask):
        low = mask & -mask if mask else self.links.n_dp
        if mask:
            self.got[mask].wait_recv()
        slot = self.buf.at[self.links.dp_peer(mask)]
        for bit in reversed(self.bits):
            if bit < low:
                self.got[mask | bit] = Batch(self.links, [(slot, slot, bit, 0)], slot)

    def relay(self):
        for mask in sorted(range(1, self.links.n_dp), key=lambda m: bin(m).count("1")):
            self.forward(mask)


def bit_names(n_dp, n_blk):
    blk = [("blk", 1 << k) for k in range(n_blk.bit_length() - 1)]
    dp = [("dp", 1 << k) for k in range(n_dp.bit_length() - 1)]
    return {"x": blk[:1], "z0": blk[1:2], "z1": blk[2:], "c": dp[:1], "y": dp[1:]}


class Chunk:
    def __init__(self, links, rows, part, out, landing, every, plan, measure):
        self.measure = measure
        names = bit_names(links.n_dp, links.n_blk)
        order, late = plan
        spread = lambda tokens: [bit for token in tokens for bit in names[token]]
        self.links, self.rows, self.part, self.out, self.landing = links, rows, part, out, landing
        self.halving = spread(order)
        back = [token for token in reversed(order) if token not in "cy"]
        back = back[:late] + ["y"] + back[late:] + ["c"]
        self.doubling = []
        for token in back:
            bits = names[token]
            self.doubling += bits if token in "cy" else bits[::-1]
        self.held = list(range(links.n_dp)) if every else [0]
        self.walk = self.steps()
        self.live = True

    def advance(self):
        self.live = next(self.walk, "end") != "end"

    def steps(self):
        links = self.links
        held, low, size, lows, at, last_batch = self.held, 0, self.rows, [], 0, None
        send = links.send.at[links.used_send]
        links.used_send += 1

        def move(moves, total):
            if last_batch is not None:
                last_batch.wait_send()
            return Batch(links, moves, total, send)

        for k, (axis, bit) in enumerate(self.halving):
            last = k + 1 == len(self.halving)
            if axis == "blk":
                half = size // 2
                mine = (links.blk // bit) % 2
                keep = pl.multiple_of(low + mine * half, 8)
                away = pl.multiple_of(low + (1 - mine) * half, 8)
                moves = [(mask, mask, away) for mask in held]
                lows.append(low)
                low, size = keep, half
            else:
                moves = [(mask, mask ^ bit, low) for mask in held if mask & bit]
                held = [mask for mask in held if not mask & bit]
            slots, copies, start = {}, [], at
            dp_mask, blk_mask = (0, bit) if axis == "blk" else (bit, 0)
            for mask, there, row in moves:
                slots[there] = self.landing.at[pl.ds(at, size), :]
                at += size
                copies.append((self.part(mask, row, size), slots[there], dp_mask, blk_mask))
            last_batch = move(copies, self.landing.at[pl.ds(start, at - start), :])
            yield
            last_batch.wait_recv()
            for mask in held:
                own = self.part(mask, low, size)
                goal = self.out(mask, low, size) if last else own
                goal[...] = own[...] + slots[mask][...]
        for axis, bit in self.doubling:
            place = [self.out(mask, low, size) for mask in held]
            dp_mask, blk_mask = (0, bit) if axis == "blk" else (bit, 0)
            total = self.measure.at[pl.ds(0, size * len(held)), pl.ds(0, place[0].shape[1])]
            last_batch = move([(v, v, dp_mask, blk_mask) for v in place], total)
            if axis == "blk":
                low, size = lows.pop(), size * 2
            else:
                held = held + [mask | bit for mask in held]
            yield
            last_batch.wait_recv()


def landing_rows(rows, order, n_dp, n_blk, every):
    names, held, total = bit_names(n_dp, n_blk), n_dp if every else 1, 0
    for token in order:
        for axis, _ in names[token]:
            if axis == "blk":
                rows //= 2
            else:
                held //= 2
            total += held * rows
    return total


VEC_ROWS = 16


def whole_kernel(
    n_dp, n_blk, x_hbm, lengths, cot_hbm, log_rate, frequency, out_coef, glu_hbm, in_hbm, out_hbm,
    n1g_hbm, n1b_hbm, log_step_hbm, skip_hbm, glu_b_hbm, n2g_hbm, n2b_hbm, in_b_hbm, out_b_hbm,
    block_out, grad_in, sum_glu, sum_in, sum_out, vec_out, par_out,
    send_sems, recv_sems, load_sems, x_ref, cot_ref, n1g, n1b, log_step, skip_gain, glu_b, n2g, n2b, in_b, out_b, glu_w, ffn_in, ffn_out, windows, rate_own, freq_own, coef_own, columns,
    a_send, x_all, y_send, y_all, dy_send, dy_all, dx_send, dx_all,
    q_ref, t_ref, h_ref, consts, base, taps, a_ref, b_ref, g_ref,
    result_all, feed_all, dglu, hidden_grad, slice_grad, hidden_s, pre_s, hidden_own, pre_own, slope_keep, unit_keep, residual_keep, gate_keep,
    gelu_keep, acc_out, acc_feed, residual_grad, part_glu, part_in, part_out,
    own_par, dp_par, sum_par, blk_par, all_par, flat_par, vec, dp_vec, sum_vec, blk_vec, *landings,
):
    rows, width = x_ref.shape
    ff = ffn_in.shape[1]
    chans = width // n_blk
    quarter = chans // n_dp
    size = min(GROUP, chans)
    parts = [(first, size) for first in range(0, chans, size)]
    first_parts = [(0, chans)] if FIRST_WHOLE else parts
    links = Links(send_sems, recv_sems, n_dp, n_blk)
    dp, blk = links.dp, links.blk
    first = pl.multiple_of(blk * chans, 8)
    lanes_at = pl.multiple_of(blk * chans // 128 * 128, 128)

    links.loads = []
    sources = {
        "x": (x_hbm, x_ref), "n1g": (n1g_hbm, n1g), "n1b": (n1b_hbm, n1b), "cot": (cot_hbm, cot_ref),
        "rate": (log_rate.at[:, pl.ds(lanes_at, 128)], windows.at[0]),
        "freq": (frequency.at[:, pl.ds(lanes_at, 128)], windows.at[1]),
        "coef": (out_coef.at[:, :, pl.ds(lanes_at, 128)], windows.at[pl.ds(2, 2)]),
        "step": (log_step_hbm, log_step), "skip": (skip_hbm, skip_gain), "out": (out_hbm, ffn_out),
        "glu": (glu_hbm, glu_w), "glu_b": (glu_b_hbm, glu_b), "n2g": (n2g_hbm, n2g), "n2b": (n2b_hbm, n2b),
        "in": (in_hbm, ffn_in), "in_b": (in_b_hbm, in_b), "out_b": (out_b_hbm, out_b),
    }
    loads = {}

    def fetch(names):
        for name in names:
            loads[name] = Load(*sources[name], load_sems.at[len(loads)])
            links.loads.append(loads[name])

    def need(*names):
        for name in names:
            loads[name].wait()

    links.greet()
    fetch(list(sources))
    need("x", "n1g", "n1b")

    places = blk * rows + iota((rows, 1), 0)
    live = (places < lengths[0]).astype(F32)
    inputs = x_ref[...].astype(F32)
    normed, unit, scale1 = layer_norm(inputs, n1g[...], n1b[...])
    unit_keep[...] = unit
    mixed = normed.astype(BF16) * live.astype(BF16)
    flip = jnp.where(iota((rows, rows), 0) + iota((rows, rows), 1) == rows - 1, 1.0, 0.0).astype(BF16)
    a_send[...] = nn(flip, mixed).T
    links.meet()
    to_x = [links.exchange(a_send.reshape(n_blk, chans, rows), x_all, *part) for part in first_parts]
    need("cot")
    cot = cot_ref[...].astype(F32)
    result = live * cot
    result_all[dp] = result
    gather_result = Gather(links, result_all)

    need("step", "skip", "rate", "freq", "coef")
    columns[0] = jnp.broadcast_to(log_step[...], (128, width)).T
    columns[1] = jnp.broadcast_to(skip_gain[...], (128, width)).T
    own_skip = columns[1, pl.ds(first, chans), :]
    turn = (128 - blk * chans % 128) % 128
    own = [pltpu.roll(windows[k], turn, 1).T[:chans] for k in range(4)]
    rate_own[...], freq_own[...], coef_own[0], coef_own[1] = own

    def ssm():
        return columns[0, pl.ds(first, chans), :], rate_own[...], freq_own[...], (coef_own[0], coef_own[1])

    kern_slot = ssm_setup(n_blk, ssm(), consts, base)
    lead_slot = kern_slot - 1
    base_flat = base.reshape(8 * chans, 128)
    groups(0, chans, lambda group: make_powers(group, chans, consts, kern_slot, base_flat, q_ref, taps), 2 * GROUP)
    shift_taps(own_skip, taps, base)

    x_flat = x_all.reshape(n_blk * chans, 128)
    y_flat = y_send.reshape(n_blk * chans, 128)
    to_y = []
    for k, part in enumerate(parts):
        groups(*part, lambda group: make_band(group, chans, base_flat, t_ref))
        if k < len(to_x):
            to_x[k].wait_recv()
        groups(*part, lambda group: forward_group(group, chans, n_blk, consts, lead_slot, x_flat, q_ref, t_ref, h_ref, y_flat))
        to_y.append(links.exchange(y_send, y_all, *part))

    gather_result.relay()
    need("out")
    low = result.astype(BF16)
    step = ff // 4
    for k in range(4):
        hidden_grad[:, k * step : (k + 1) * step] = nt(low, ffn_out[k * step : (k + 1) * step, :])
    part_ff = ff // n_dp
    rows_s = pl.multiple_of(dp * part_ff, 128)
    out_slice = ffn_out[pl.ds(rows_s, part_ff), :]
    for k in range(n_dp):
        slice_grad[k * rows : (k + 1) * rows, :] = nt(result_all[k].astype(BF16), out_slice)
    need("glu", "glu_b", "n2g", "n2b", "in", "in_b", "out_b")

    for batch in to_y:
        batch.wait_recv()
    conv = y_all.reshape(width, rows)[...].T
    gelu_out, gelu_slope = gelu_parts(conv)
    slope_keep[...] = gelu_slope
    gelu_low = gelu_out.astype(BF16)
    gelu_keep[...] = gelu_low
    glu_pre = nn(gelu_low, glu_w[...]) + glu_b[...]
    left = glu_pre[:, :width]
    gate = 0.5 + 0.5 * jnp.tanh(0.5 * glu_pre[:, width:])
    gate_keep[0] = left
    gate_keep[1] = gate
    residual = x_ref[...].astype(F32) + live * left * gate
    normed_mid, unit_mid, scale_mid = layer_norm(residual, n2g[...], n2b[...])
    feed = normed_mid.astype(BF16)
    feed_all[dp] = feed.astype(F32)
    gather_feed = Gather(links, feed_all)
    residual_keep[0] = residual
    residual_keep[1] = unit_mid

    pieces, arrivals = {}, {}

    def piece(work):
        pieces[work.__name__] = work

    @piece
    def own():
        for k in range(4):
            cut = slice(k * step, (k + 1) * step)
            hidden, slope = gelu_parts(nn(feed, ffn_in[:, cut]) + in_b[:, cut])
            grad_pre = (hidden_grad[:, cut] * slope).astype(BF16)
            hidden_own[:, cut] = hidden.astype(BF16)
            pre_own[:, cut] = grad_pre
            back = nt(grad_pre, ffn_in[:, cut])
            acc_feed[...] = back if k == 0 else acc_feed[...] + back

    @piece
    def glubwd():
        unit_mid = residual_keep[1]
        grad_res = cot_ref[...].astype(F32) + norm_back(acc_feed[...], n2g[...], unit_mid, scale_mid)
        residual_grad[...] = grad_res
        grad_left = live * grad_res
        left, gate = gate_keep[0], gate_keep[1]
        dglu[:, :width] = (grad_left * gate).astype(BF16)
        dglu[:, width:] = (grad_left * left * gate * (1.0 - gate)).astype(BF16)

    @piece
    def late():
        for k in range(4):
            cut = slice(k * step, (k + 1) * step)
            forward = nn(hidden_own[:, cut], ffn_out[cut, :])
            acc_out[...] = forward if k == 0 else acc_out[...] + forward
            vec[7 + k : 8 + k, :] = token_sum(pre_own[:, cut].astype(F32))
        block_out[...] = (residual_keep[0] + live * (acc_out[...] + out_b[...])).astype(BF16)
        grad_feed = acc_feed[...]
        vec[2:3, :] = token_sum(grad_feed * residual_keep[1])
        vec[3:4, :] = token_sum(grad_feed)
        vec[4:5, :] = token_sum(result_all[dp])
        vec[5:6, :] = token_sum(dglu[:, :width].astype(F32))
        vec[6:7, :] = token_sum(dglu[:, width:].astype(F32))

    @piece
    def dy():
        dy_send[...] = (nt(dglu[...], glu_w[...]) * slope_keep[...]).T
        arrivals["dy"] = links.exchange(dy_send.reshape(n_blk, chans, rows), dy_all, 0, chans)

    @piece
    def slice_all():
        gather_feed.relay()
        in_slice = ffn_in[:, pl.ds(rows_s, part_ff)]
        in_b_slice = in_b[:, pl.ds(rows_s, part_ff)]
        for k in range(n_dp):
            hidden, slope = gelu_parts(nn(feed_all[k].astype(BF16), in_slice) + in_b_slice)
            cut = slice(k * rows, (k + 1) * rows)
            hidden_s[cut, :] = hidden.astype(BF16)
            pre_s[cut, :] = (slice_grad[cut, :] * slope).astype(BF16)

    part_gl = 2 * width // n_dp
    shapes = piece_shapes(n_dp, n_blk, width, ff)
    chunks = {}

    def window(ref, row0, col0, rows_at, cols):
        def view(mask, row, size):
            slot = links.dp_peer(mask)
            row_at = pl.multiple_of(slot * rows_at[0] + row0 + row, 8)
            col_at = pl.multiple_of(slot * rows_at[1] + col0, 128) if rows_at[1] else col0
            return ref.at[pl.ds(row_at, size), pl.ds(col_at, cols)]
        return view

    def start_chunk(k):
        if k not in shapes:
            return
        kind, row0, col0, rows_k, cols_k, plan = shapes[k]
        rows_cut, cols_cut = slice(row0, row0 + rows_k), slice(col0, col0 + cols_k)
        if kind == "glu":
            part_glu[rows_cut, :] = tn(gelu_keep[:, rows_cut], dglu[...])
            part = window(part_glu, row0, 0, (0, part_gl), part_gl)
            total = window(sum_glu, row0, 0, (0, part_gl), part_gl)
        elif kind == "out":
            results = result_all[:, :, cols_cut].reshape(n_dp * rows, cols_k).astype(BF16)
            part_out[rows_cut, cols_cut] = tn(hidden_s[:, rows_cut], results)
            part = window(part_out, row0, col0, (0, 0), cols_k)
            total = window(sum_out, row0, col0, (part_ff, 0), cols_k)
        else:
            feeds = feed_all[:, :, rows_cut].reshape(n_dp * rows, rows_k).astype(BF16)
            part_in[rows_cut, cols_cut] = tn(feeds, pre_s[:, cols_cut])
            part = window(part_in, row0, col0, (0, 0), cols_k)
            total = window(sum_in, row0, col0, (0, part_ff), cols_k)
        chunks[k] = Chunk(links, rows_k, part, total, landings[k], kind == "glu", plan, sum_out)
        chunks[k].advance()

    dy_flat = dy_all.reshape(n_blk * chans, 128)
    dx_flat = dx_send.reshape(n_blk * chans, 128)

    def backward(k):
        if k == 0:
            arrivals["dy"].wait_recv()
        size = min(GROUP, chans)
        if k * size < chans:
            backward_group([k * size + i for i in range(size)], chans, n_blk, consts, lead_slot, x_flat, dy_flat, q_ref, t_ref, h_ref, dx_flat, a_ref, b_ref, g_ref)
        if k == 3:
            groups(4 * size, chans - 4 * size, lambda group: backward_group(group, chans, n_blk, consts, lead_slot, x_flat, dy_flat, q_ref, t_ref, h_ref, dx_flat, a_ref, b_ref, g_ref))
            arrivals["dx"] = links.exchange(dx_send, dx_all, 0, chans)

    @piece
    def near():
        split_lags(g_ref, base)
        groups(0, chans, lambda group: near_sums(group, chans, base_flat, q_ref, a_ref, b_ref))
        rate_freq, coefs, d_step, d_skip = finish(chans, ssm(), a_ref, b_ref, g_ref)
        own_par[:, 0, :] = rate_freq
        own_par[:, 1, :] = coefs
        lane = iota((chans, 128), 1)
        pair = jnp.where(lane == 0, d_step, jnp.where(lane == 1, d_skip, 0.0))
        if chans < 128:
            pair = jnp.concatenate([pair, jnp.zeros((128 - chans, 128), F32)], axis=0)
        pair = pair.T[0:8]
        if width > 128:
            pair = jnp.concatenate([pair, jnp.zeros((8, width - 128), F32)], axis=1)
        pair = pltpu.roll(pair, blk * chans, 1)
        vec[11:13, :] = pair[0:2]
        vec[13:16, :] = jnp.zeros((3, width), F32)

    @piece
    def ln1():
        arrivals["dx"].wait_recv()
        back = dx_all.reshape(width, rows)[...].T
        high, rest = split(back)
        rest, last = split(back - high.astype(F32))
        grad_normed = live * (nn(flip, high) + (nn(flip, rest) + nn(flip, last)))
        unit = unit_keep[...]
        vec[0:1, :] = token_sum(grad_normed * unit)
        vec[1:2, :] = token_sum(grad_normed)
        grad_in[...] = residual_grad[...] + norm_back(grad_normed, n1g[...], unit, scale1)

    @piece
    def s0():
        moves = [
            (own_par.at[pl.ds(links.dp_peer(mask) * quarter, quarter)], dp_par.at[dp], mask, 0) for mask in range(1, n_dp)
        ]
        arrivals["s0"] = [
            Batch(links, moves, dp_par.at[pl.ds(0, n_dp - 1)]),
            Batch(links, [(vec, dp_vec.at[dp], mask, 0) for mask in range(1, n_dp)], dp_vec.at[pl.ds(0, n_dp - 1)]),
        ]
        dp_par[dp] = own_par[pl.ds(dp * quarter, quarter)]
        dp_vec[dp] = vec[...]

    @piece
    def s1():
        for batch in arrivals["s0"]:
            batch.wait_recv()
        sum_par[...] = sum_slots(dp_par, n_dp)
        sum_vec[...] = sum_slots(dp_vec, n_dp)
        arrivals["s1"] = [
            Batch(links, [(src, dst.at[blk], 0, mask) for mask in range(1, n_blk)], dst.at[pl.ds(0, n_blk - 1)])
            for src, dst in ((sum_par, blk_par), (sum_vec, blk_vec))
        ]
        blk_par[blk] = sum_par[...]
        blk_vec[blk] = sum_vec[...]

    @piece
    def s2():
        for batch in arrivals["s1"]:
            batch.wait_recv()
        all_par[dp] = blk_par[...]
        arrivals["s2"] = Gather(links, all_par)
        vec_out[...] = sum_slots(blk_vec, n_blk)

    @piece
    def s3():
        arrivals["s2"].relay()
        state = par_out.shape[0] // 4
        for b in range(n_blk):
            for d in range(n_dp):
                at = b * chans + d * quarter
                block = all_par[d, b]
                flat_par[0, at : at + quarter, :] = block[:, 0, :]
                flat_par[1, at : at + quarter, :] = block[:, 1, :]
        par_out[: 2 * state, :] = flat_par[0].T
        par_out[2 * state :, :] = flat_par[1].T

    for token in ORDER:
        if isinstance(token, int):
            if token in chunks:
                chunks[token].advance()
        elif token.startswith("part"):
            start_chunk(int(token[4:]))
        elif token.startswith("bwd"):
            backward(int(token[3:]))
        else:
            pieces["slice_all" if token == "slice" else token]()
    while any(chunk.live for chunk in chunks.values()):
        for chunk in chunks.values():
            chunk.advance()
    links.finish()


def piece_shapes(n_dp, n_blk, width, ff):
    shapes = {}
    n_glu, n_ffn = len(GLU_PLANS), len(FFN_PLANS) // 2
    cuts = min(n_glu, width // (8 * n_blk))
    size = width // cuts
    for k, plan in enumerate(GLU_PLANS[:cuts]):
        shapes[k] = ("glu", k * size, 0, size, 2 * width // n_dp, plan)
    for kind, at, height, breadth in (("out", n_glu, ff // n_dp, width), ("in", n_glu + n_ffn, width, ff // n_dp)):
        cols = min(n_ffn, breadth // 128)
        cuts = min(n_ffn // cols, height // (8 * n_blk))
        high, wide = height // cuts, breadth // cols
        for k in range(cols * cuts):
            shapes[at + k] = (kind, k % cuts * high, k // cuts * wide, high, wide, FFN_PLANS[at - n_glu + k])
    return shapes


def sum_slots(ref, count):
    total = ref[0]
    for k in range(1, count):
        total = total + ref[k]
    return total


def deliver_kernel(big_in, vec, par, rows_out, big_out, rate, freq, coef, rows_buf, sems):
    states = rate.shape[0]
    moves = list(zip(big_in, big_out))
    moves += [(par.at[pl.ds(0, states)], rate), (par.at[pl.ds(states, states)], freq)]
    moves += [(par.at[pl.ds((2 + k) * states, states)], coef.at[k]) for k in range(2)]
    copies = [pltpu.make_async_copy(src, dst, sems.at[k]) for k, (src, dst) in enumerate(moves)]
    for copy in copies:
        copy.start()
    row = 0
    for k, (buf, out) in enumerate(zip(rows_buf, rows_out)):
        for part in range(out.shape[1] // vec.shape[1]):
            buf[:, part * vec.shape[1] : (part + 1) * vec.shape[1]] = vec[row : row + 1, :]
            row += 1
        copies.append(pltpu.make_async_copy(buf, out, sems.at[len(moves) + k]))
        copies[-1].start()
    for copy in copies:
        copy.wait()


def on_device(n_dp, n_blk, block_in, seq_lengths, norm1_gain, norm1_bias, log_step, log_rate, frequency, out_coef, skip_gain, glu_weight, glu_bias, norm2_gain, norm2_bias, ffn_in, ffn_in_bias, ffn_out, ffn_out_bias, cotangent):
    _, rows, width = block_in.shape
    ff = ffn_in.shape[1]
    states = log_rate.shape[1]
    chans, quarter = width // n_blk, width // n_blk // n_dp
    row = lambda v: v.reshape(1, -1)
    vmem, anywhere = pl.BlockSpec(memory_space=VMEM), pl.BlockSpec(memory_space=pl.ANY)
    shape = jax.ShapeDtypeStruct
    outs = [
        shape((rows, width), BF16), shape((rows, width), F32),
        shape((width, 2 * width), F32), shape((width, ff), F32), shape((ff, width), F32),
        shape((VEC_ROWS, width), F32), shape((4 * states, width), F32),
    ]
    part_ff, part_gl = ff // n_dp, 2 * width // n_dp
    tokens = n_dp * rows
    f32 = lambda *dims: VMEM(dims, F32)
    bf16 = lambda *dims: VMEM(dims, BF16)
    dma = lambda n: pltpu.SemaphoreType.DMA((n,))
    shapes = piece_shapes(n_dp, n_blk, width, ff)
    landings = []
    for k in range(len(GLU_PLANS) + len(FFN_PLANS)):
        kind, _, _, rows_k, cols_k, plan = shapes.get(k, ("out", 0, 0, 8 * n_blk, 128, FFN_PLANS[0]))
        landings.append(f32(landing_rows(rows_k, plan[0], n_dp, n_blk, kind == "glu"), cols_k))
    scratch = [
        dma(SEND_SEMS), dma(RECV_SEMS), dma(20),
        bf16(rows, width), bf16(rows, width), f32(1, width), f32(1, width), f32(1, width), f32(1, width), f32(1, 2 * width),
        f32(1, width), f32(1, width), f32(1, ff), f32(1, width),
        bf16(width, 2 * width), bf16(width, ff), bf16(ff, width),
        f32(4, states, 128), f32(chans, states), f32(chans, states), f32(2, chans, states), f32(2, width, 128),
        f32(width, rows), f32(n_blk, chans, rows), f32(n_blk, chans, rows), f32(n_blk, chans, rows),
        f32(width, rows), f32(n_blk, chans, rows), f32(n_blk, chans, rows), f32(n_blk, chans, rows),
        bf16(chans, 256, 128), bf16(chans, 256, 128), f32(chans, n_blk, 128), f32(n_consts(n_blk), chans, 128),
        f32(8, chans, 128), f32(chans, 128), f32(2 * chans, 128), f32(2 * chans, 128), f32(chans, 128),
        f32(n_dp, rows, width), f32(n_dp, rows, width),
        bf16(rows, 2 * width),
        f32(rows, ff), f32(tokens, part_ff), bf16(tokens, part_ff), bf16(tokens, part_ff), bf16(rows, ff), bf16(rows, ff),
        f32(rows, width), f32(rows, width), f32(2, rows, width), f32(2, rows, width),
        bf16(rows, width), f32(rows, width), f32(rows, width), f32(rows, width),
        f32(width, 2 * width), f32(width, part_ff), f32(part_ff, width),
        f32(chans, 2, 128), f32(n_dp, quarter, 2, 128), f32(quarter, 2, 128), f32(n_blk, quarter, 2, 128),
        f32(n_dp, n_blk, quarter, 2, 128), f32(2, width, 128),
        f32(VEC_ROWS, width), f32(n_dp, VEC_ROWS, width), f32(VEC_ROWS, width), f32(n_blk, VEC_ROWS, width),
        *landings,
    ]
    out = pl.pallas_call(
        functools.partial(whole_kernel, n_dp, n_blk),
        out_shape=[VMEM(v.shape, v.dtype) for v in outs],
        out_specs=[vmem] * len(outs),
        in_specs=[anywhere, pl.BlockSpec(memory_space=pltpu.SMEM)] + [anywhere] * 16,
        scratch_shapes=scratch,
        compiler_params=pltpu.CompilerParams(collective_id=0, has_side_effects=True, vmem_limit_bytes=44 * 2**20),
    )(
        block_in[0], seq_lengths, cotangent[0], log_rate.T, frequency.T, out_coef.swapaxes(1, 2), glu_weight, ffn_in, ffn_out,
        row(norm1_gain), row(norm1_bias), row(log_step), row(skip_gain), row(glu_bias), row(norm2_gain), row(norm2_bias),
        row(ffn_in_bias), row(ffn_out_bias),
    )
    block_out, grad_in, g_glu, g_in, g_out, vec, par = out
    widths = [width, width, width, width, width, 2 * width, ff, width, width]
    made = [shape((rows, width), BF16), shape((rows, width), F32)]
    big = [shape(v.shape, F32) for v in (g_glu, g_in, g_out)]
    small = [shape((1, w), F32) for w in widths]
    params = [shape((states, width), F32), shape((states, width), F32), shape((2, states, width), F32)]
    out_shapes = made + big + small + params

    def deliver(block_out, grad_in, g_glu, g_in, g_out, vec, par, *rest):
        outs, rows_buf, sems = rest[:17], rest[17:-1], rest[-1]
        big = [g_out, g_in, g_glu, grad_in, block_out]
        deliver_kernel(big, vec, par, outs[5:14], [outs[4], outs[3], outs[2], outs[1], outs[0]], *outs[14:], rows_buf, sems)

    done = pl.pallas_call(
        deliver,
        out_shape=out_shapes,
        in_specs=[vmem] * 7,
        out_specs=[anywhere] * 17,
        scratch_shapes=[f32(1, w) for w in widths] + [dma(18)],
        compiler_params=pltpu.CompilerParams(vmem_limit_bytes=8 * 2**20),
    )(*out)
    flat = [v.reshape(-1) for v in done[5:14]]
    n1_gain, n1_bias, n2_gain, n2_bias, ffn_out_b, glu_b, ffn_in_b, d_step, d_skip = flat
    return (
        done[0][None], done[1][None], n1_gain, n1_bias, d_step, done[14].T, done[15].T, done[16].swapaxes(1, 2), d_skip,
        done[2], glu_b, n2_gain, n2_bias, done[3], ffn_in_b, done[4], ffn_out_b,
    )


def solution(mesh):
    split_spec, whole = P("dp", "blk", None), P()
    return jax.shard_map(
        functools.partial(on_device, mesh.shape["dp"], mesh.shape["blk"]),
        mesh=mesh,
        in_specs=(split_spec, P("dp")) + (whole,) * 15 + (split_spec,),
        out_specs=(split_spec, split_spec) + (whole,) * 15,
        check_vma=False,
    )
```

```python
import functools

import jax
import jax.numpy as jnp
from jax import lax
from jax.experimental import pallas as pl
from jax.experimental.pallas import tpu as pltpu
from jax.sharding import PartitionSpec as P

NORM_EPSILON = 1e-05
F32 = jnp.float32
BF16 = jnp.bfloat16
PRECISE = lax.Precision.HIGHEST
SERIES = 16
GROUP = 16
SEND_SEMS = 43
RECV_SEMS = 191
BIG_PARTS = 1
FIRST_WHOLE = False
GLU_PLANS = (
    (("c", "x", "z0", "y", "z1"), 3),
    (("c", "y", "x", "z0", "z1"), 3),
    (("c", "z0", "x", "y", "z1"), 2),
    (("c", "y", "x", "z0", "z1"), 3),
)
FFN_PLANS = (
    (("x", "z0", "z1"), 2),
    (("x", "z1", "z0"), 2),
    (("z1", "x", "z0"), 3),
    (("x", "z0", "z1"), 2),
    (("x", "z0", "z1"), 2),
    (("z0", "x", "z1"), 2),
    (("x", "z0", "z1"), 2),
    (("x", "z0", "z1"), 2),
    (("z1", "x", "z0"), 1),
    (("x", "z0", "z1"), 3),
    (("x", "z0", "z1"), 3),
    (("z0", "x", "z1"), 0),
    (("x", "z1", "z0"), 2),
    (("x", "z0", "z1"), 3),
    (("x", "z0", "z1"), 1),
    (("x", "z0", "z1"), 0),
)
ORDER = (
    "own", "glubwd", "dy", "part0", "part1", "part2", "part3", 0, 1, 2, 3, "slice", "part4", "part5", "part6",
    0, "part7", 1, "part8", "part9", "part10", 2, "part11", "part12", "part13", "part14", 4, "part15",
    "part16", 3, "part17", "part18", 5, "part19", 0, 6, "bwd0", 7, 9, 1, 0, 8, 4, 12, "bwd1", 7, 5, 1, 10, 0,
    11, 8, 15, 2, 4, "bwd2", 7, 5, 1, 14, 8, 11, 13, 10, 0, 16, 3, 2, 7, 5, 4, "bwd3", 1, 8, 14, 11, 17, 13,
    19, 10, 0, 18, 6, "late", "near", 9, 7, 12, 5, 3, 16, 2, 15, 4, 7, 0, 5, 1, 8, "ln1", 14, 11, 17, 7, 4, "s0", 13,
    19, 0, 10, 18, 6, 7, 8, 5, 9, 12, 0, 3, 16, 1, 2, "s1", 5, 15, 14, 11, 17, 4, 13, 19, 10, 1, 6, 18, 15, 4,
    8, 9, 12, 2, 11, 3, 16, 19, 1, "s2", 8, 14, 10, 9, 12, 17, 13, 6, 18, 2, 3, 15, 11, 16, 14, "s3", 11, 19,
    17, 9, 18, 10, 16, 6, 12, 10, 2, 13, 14, 19, 3, 2, 15, 14, 6, 9, 17, 18, 6, 9, 13, 16, 13, 16, 3, 19, 12,
    15, 3, 17, 19, 18, 12, 15, 17, 18,
)
VMEM = pltpu.VMEM


def iota(shape, axis):
    return lax.broadcasted_iota(jnp.int32, shape, axis)


def is_left(shape):
    half = shape[-1] // 2
    return iota(shape, len(shape) - 1) < half


def swap(v):
    return pltpu.roll(v, v.shape[-1] // 2, v.ndim - 1)


def times(v, const):
    return v * const[0] + swap(v) * const[1]


def split(v):
    high = v.astype(BF16)
    return high, (v - high.astype(F32)).astype(BF16)


def nn(a, b):
    return lax.dot_general(a, b, (((1,), (0,)), ((), ())), preferred_element_type=F32)


def nt(a, b):
    return lax.dot_general(a, b, (((1,), (1,)), ((), ())), preferred_element_type=F32)


def tn(a, b):
    return lax.dot_general(a, b, (((0,), (0,)), ((), ())), preferred_element_type=F32)


def cmul(a, b):
    return a[0] * b[0] - a[1] * b[1], a[0] * b[1] + a[1] * b[0]


def twice(v):
    return jnp.concatenate([v, v], axis=-1)


def pole_parts(log_step, log_rate, frequency):
    step = jnp.exp(log_step)
    rate = jnp.exp(twice(log_rate))
    pole = (-rate, step * twice(frequency))
    phi = (jnp.zeros_like(rate), jnp.zeros_like(rate))
    slope = (jnp.zeros_like(rate), jnp.zeros_like(rate))
    fact = [1.0]
    for k in range(1, SERIES + 2):
        fact.append(fact[-1] * k)
    for k in range(SERIES, -1, -1):
        phi = cmul(phi, pole)
        phi = (phi[0] + 1.0 / fact[k + 1], phi[1])
    for k in range(SERIES, 0, -1):
        slope = cmul(slope, pole)
        slope = (slope[0] + k / fact[k + 1], slope[1])
    grow = cmul(pole, phi)
    z = (1.0 + grow[0], grow[1])
    return step, rate, z, phi, slope


def as_const(value):
    sign = jnp.where(is_left(value[0].shape), -1.0, 1.0)
    return value[0], value[1] * sign


def packed(value):
    return jnp.where(is_left(value[0].shape), value[0], value[1])


def ssm_setup(rows, ssm, consts, base):
    log_step, log_rate, frequency, coef = ssm
    step, rate, z, phi, slope = pole_parts(log_step, log_rate, frequency)
    b = (twice(coef[0]), twice(coef[1]))
    residue = cmul(b, (step * phi[0], step * phi[1]))
    power = (jnp.ones_like(rate), jnp.zeros_like(rate))
    for r in range(8):
        base[r] = packed(power)
        power = cmul(power, z)
    slot = 0

    def keep(value):
        nonlocal slot
        c = as_const(value)
        consts[2 * slot] = c[0]
        consts[2 * slot + 1] = c[1]
        slot += 1

    for k in range(4):
        keep(power)
        power = cmul(power, power)
    for k in range((rows - 1).bit_length()):
        keep(power)
        power = cmul(power, power)
    lead = cmul(residue, z)
    lead = (2.0 * lead[0], 2.0 * lead[1])
    sign = jnp.where(is_left(rate.shape), 1.0, -1.0)
    consts[2 * slot] = lead[0] * sign
    consts[2 * slot + 1] = -lead[1]
    slot += 1
    kern = jnp.where(is_left(rate.shape), 2.0 * residue[0], -2.0 * residue[1])
    kern_high = kern.astype(BF16).astype(F32)
    consts[2 * slot] = kern_high
    consts[2 * slot + 1] = kern - kern_high
    return slot


def row_of(ref, index, chan):
    return ref[index, pl.ds(chan, 1), :]


def const_of(consts, slot, chan):
    return row_of(consts, 2 * slot, chan), row_of(consts, 2 * slot + 1, chan)


def make_powers(group, chans, consts, kern_slot, base_flat, q_ref, taps_ref):
    every = [base_flat[pl.ds(chan, 8, stride=chans), :] for chan in group]
    for k in range(4):
        every = [
            jnp.concatenate([powers, times(powers, const_of(consts, k, chan))], axis=0)
            for chan, powers in zip(group, every)
        ]
    parts = [split(powers) for powers in every]
    for chan, (high, rest) in zip(group, parts):
        q_ref[chan, :128, :] = high
        q_ref[chan, 128:, :] = rest
    kerns = []
    for chan, (high, rest) in zip(group, parts):
        taps = [row_of(consts, 2 * kern_slot + k, chan) for k in range(2)]
        taps = jnp.concatenate([taps[0], taps[1]], axis=0).astype(BF16)
        kerns.append(nt(twice(taps), jnp.concatenate([high, rest], axis=1)))
    for chan, kern in zip(group, kerns):
        taps_ref[pl.ds(chan, 1), :] = kern[0:1] + kern[1:2]


def shift_taps(skip, taps_ref, base):
    taps = taps_ref[...]
    taps = taps + jnp.where(iota(taps.shape, 1) == 0, skip, 0.0)
    for r in range(8):
        base[r] = taps if r == 7 else pltpu.roll(taps, 7 - r, 1)


def make_band(group, chans, base_flat, t_ref):
    for chan in group:
        tile = base_flat[pl.ds(chan, 8, stride=chans), :]
        band = jnp.concatenate([pltpu.roll(tile, 120 - 8 * m, 1) if m < 15 else tile for m in range(16)], axis=0)
        band = jnp.where(iota((128, 128), 0) + iota((128, 128), 1) >= 127, band, 0.0)
        t_high, t_rest = split(band)
        t_ref[chan, :128, :] = t_high
        t_ref[chan, 128:, :] = t_rest


def scan(values, consts, first, group, reverse):
    rows = values[0].shape[0]
    places = iota(values[0].shape, 0)

    def moved(x, d):
        if reverse:
            return jnp.where(places < rows - d, pltpu.roll(x, rows - d, 0), 0.0)
        return jnp.where(places >= d, pltpu.roll(x, d, 0), 0.0)

    values = [moved(v, 1) for v in values]
    d, k = 1, 0
    while d < rows:
        values = [v + times(moved(v, d), const_of(consts, first + k, chan)) for v, chan in zip(values, group)]
        d, k = 2 * d, k + 1
    return values


def wide(chan, q_ref, t_ref):
    return jnp.concatenate([q_ref[chan], t_ref[chan]], axis=1)


def far_parts(states, consts, lead_slot, group, q_ref):
    rows = states[0].shape[0]
    outs = []
    for chan, state in zip(group, states):
        high, rest = split(times(state, const_of(consts, lead_slot, chan)))
        both = twice(jnp.concatenate([high, rest], axis=0))
        outs.append(nt(both, jnp.concatenate([q_ref[chan, :128, :], q_ref[chan, 128:, :]], axis=1)))
    return [out[:rows] + out[rows:] for out in outs]


def forward_group(group, chans, rows, consts, lead_slot, x_flat, q_ref, t_ref, h_ref, y_flat):
    outs = [
        nn(twice(x_flat[pl.ds(chan, rows, stride=chans), :].astype(BF16)), wide(chan, q_ref, t_ref))
        for chan in group
    ]
    states = scan([out[:, :128] for out in outs], consts, 4, group, False)
    for chan, state in zip(group, states):
        h_ref[chan] = state
    fars = far_parts(states, consts, lead_slot, group, q_ref)
    for chan, out, far in zip(group, outs, fars):
        y_flat[pl.ds(chan, rows, stride=chans), :] = out[:, 128:] + far


def backward_group(group, chans, rows, consts, lead_slot, x_flat, dy_flat, q_ref, t_ref, h_ref, dx_flat, a_ref, b_ref, g_ref):
    places = iota((1, 128), 1).astype(F32)
    us = [x_flat[pl.ds(chan, rows, stride=chans), :] for chan in group]
    dys = [dy_flat[pl.ds(chan, rows, stride=chans), :] for chan in group]
    outs = []
    for chan, u, dy in zip(group, us, dys):
        high = dy.astype(BF16).astype(F32)
        left = twice(jnp.concatenate([high, dy - high, dy * places, u * places], axis=0).astype(BF16))
        outs.append(nn(left, wide(chan, q_ref, t_ref)))
    pairs = [tn(u.astype(BF16), dy.astype(BF16)) for u, dy in zip(us, dys)]
    d0s = [out[:rows, :128] + out[rows : 2 * rows, :128] for out in outs]
    d1s = [out[2 * rows : 3 * rows, :128] for out in outs]
    hs = [h_ref[chan] for chan in group]
    ends = scan(d0s, consts, 4, group, True)
    fars = far_parts(ends, consts, lead_slot, group, q_ref)
    for chan, out, far in zip(group, outs, fars):
        dx_flat[pl.ds(chan, rows, stride=chans), :] = out[:rows, 128:] + out[rows : 2 * rows, 128:] + far
    h1s = scan(
        [out[3 * rows :, :128] + 128.0 * times(h, const_of(consts, 4, chan)) for chan, out, h in zip(group, outs, hs)],
        consts, 4, group, False,
    )
    mask = is_left(hs[0].shape)

    def prod(p, q):
        q_swap = swap(q)
        return p * jnp.where(mask, q, q_swap) + swap(p) * jnp.where(mask, -q_swap, q)

    for chan, d0, d1, h, h1 in zip(group, d0s, d1s, hs, h1s):
        a_far = jnp.sum(prod(d0, h), axis=0, keepdims=True)
        b_far = a_far + jnp.sum(prod(d1, h) + prod(d0, h1), axis=0, keepdims=True)
        a_ref[pl.ds(chans + chan, 1), :] = a_far
        b_ref[pl.ds(chans + chan, 1), :] = b_far
    keep = iota((128, 128), 1) <= iota((128, 128), 0)
    for chan, pair in zip(group, pairs):
        skew = jnp.where(keep, pltpu.roll(pair, 1, 1, stride=1, stride_axis=0), 0.0)
        g_ref[pl.ds(chan, 1), :] = jnp.sum(skew, axis=0, keepdims=True)


def split_lags(g_ref, base):
    lags = g_ref[...]
    weighted = lags * iota(lags.shape, 1).astype(F32)
    for k, v in enumerate((lags, weighted)):
        high = v.astype(BF16).astype(F32)
        base[k] = high
        base[2 + k] = v - high
        base[4 + k] = jnp.zeros_like(v)
        base[6 + k] = jnp.zeros_like(v)


def near_sums(group, chans, base_flat, q_ref, a_ref, b_ref):
    outs = [nn(twice(base_flat[pl.ds(chan, 8, stride=chans), :].astype(BF16)), q_ref[chan]) for chan in group]
    for chan, out in zip(group, outs):
        a_ref[pl.ds(chan, 1), :] = out[0:1] + out[2:3]
        b_ref[pl.ds(chan, 1), :] = out[1:2] + out[3:4]


def groups(first, count, body, size=GROUP):
    size = min(size, count)

    def step(k, carry):
        body([first + k * size + i for i in range(size)])
        return carry

    if count > 0:
        lax.fori_loop(0, count // size, step, 0)


def finish(chans, ssm, a_ref, b_ref, g_ref):
    log_step, log_rate, frequency, coef = ssm
    step, rate, z, phi, slope = pole_parts(log_step, log_rate, frequency)
    b = (twice(coef[0]), twice(coef[1]))

    def dup(v):
        left = is_left(v.shape)
        moved = swap(v)
        return jnp.where(left, v, moved), jnp.where(left, moved, v)

    def total(ref):
        near, far = dup(ref[:chans, :]), dup(ref[chans:, :])
        far = cmul(far, z)
        return near[0] + far[0], near[1] + far[1]

    a, bb = total(a_ref), total(b_ref)
    residue = cmul(b, (step * phi[0], step * phi[1]))
    g_res = (2.0 * a[0], -2.0 * a[1])
    rb = cmul(residue, bb)
    g_pole = (2.0 * rb[0], -2.0 * rb[1])
    conj = lambda v: (v[0], -v[1])
    g_coef = cmul(conj((step * phi[0], step * phi[1])), g_res)
    bs = cmul(b, (step * slope[0], step * slope[1]))
    more = cmul(conj(bs), g_res)
    g_pole = (g_pole[0] + more[0], g_pole[1] + more[1])
    d_rate = -rate * g_pole[0]
    d_freq = step * g_pole[1]
    by_step = cmul(conj(cmul(b, phi)), g_res)[0] + g_pole[1] * twice(frequency)
    left = is_left(by_step.shape)
    d_step = step * jnp.sum(jnp.where(left, by_step, 0.0), axis=1, keepdims=True)
    return jnp.where(left, d_rate, d_freq), jnp.where(left, g_coef[0], g_coef[1]), d_step, g_ref[:, 0:1]


def n_consts(rows):
    return 2 * (4 + (rows - 1).bit_length() + 2)


def gelu_parts(v):
    scale = 0.7978845608028654
    square = v * v
    bend = jnp.tanh(scale * v * (1.0 + 0.044715 * square))
    half = 0.5 + 0.5 * bend
    slope = half + 0.5 * v * (1.0 - bend * bend) * (scale * (1.0 + 0.134145 * square))
    return v * half, slope


def layer_norm(values, gain, shift):
    center = values - jnp.mean(values, axis=-1, keepdims=True)
    scale = lax.rsqrt(jnp.mean(center * center, axis=-1, keepdims=True) + NORM_EPSILON)
    normed = center * scale
    return normed * gain + shift, normed, scale


def norm_back(grad_out, gain, normed, scale):
    scaled = grad_out * gain
    return scale * (
        scaled
        - jnp.mean(scaled, axis=-1, keepdims=True)
        - normed * jnp.mean(scaled * normed, axis=-1, keepdims=True)
    )


def token_sum(values):
    return jnp.sum(values, axis=0, keepdims=True)


class Load:
    def __init__(self, src, dst, sem):
        self.copy, self.done = pltpu.make_async_copy(src, dst, sem), False
        self.copy.start()

    def wait(self):
        if not self.done:
            self.done = True
            self.copy.wait()


class Batch:
    def __init__(self, links, moves, total, send=None):
        self.total, self.recv, self.arrived, self.left = total, links.recv.at[links.used_recv], False, False
        links.used_recv += 1
        if send is None:
            send = links.send.at[links.used_send]
            links.used_send += 1
        self.send = send
        links.open.append(self)
        self.copies = []
        for src, dst, dp_mask, blk_mask in moves:
            copy = pltpu.make_async_remote_copy(
                src_ref=src,
                dst_ref=dst,
                send_sem=self.send,
                recv_sem=self.recv,
                device_id=(links.dp_peer(dp_mask), links.blk_peer(blk_mask)),
                device_id_type=pl.DeviceIdType.MESH,
            )
            copy.start()
            self.copies.append(copy)

    def wait_recv(self):
        if not self.arrived:
            self.arrived = True
            if len(self.copies) == 1:
                self.copies[0].wait_recv()
            else:
                pltpu.make_async_copy(self.total, self.total, self.recv).wait()

    def wait_send(self):
        if not self.left:
            self.left = True
            if len(self.copies) == 1:
                self.copies[0].wait_send()
            else:
                pltpu.make_async_copy(self.total, self.total, self.send).wait()


class Links:
    def __init__(self, send, recv, n_dp, n_blk):
        self.send, self.recv, self.used_send, self.used_recv, self.open = send, recv, 0, 0, []
        self.n_dp, self.n_blk = n_dp, n_blk
        self.dp, self.blk = lax.axis_index("dp"), lax.axis_index("blk")

    def dp_peer(self, mask):
        return jnp.bitwise_xor(self.dp, mask)

    def blk_peer(self, mask):
        return jnp.bitwise_xor(self.blk, mask)

    def greet(self):
        barrier = pltpu.get_barrier_semaphore()
        for mask in range(1, self.n_dp):
            pl.semaphore_signal(
                barrier, inc=1, device_id=(self.dp_peer(mask), self.blk), device_id_type=pl.DeviceIdType.MESH
            )
        for mask in range(1, self.n_blk):
            pl.semaphore_signal(
                barrier, inc=1, device_id=(self.dp, self.blk_peer(mask)), device_id_type=pl.DeviceIdType.MESH
            )

    def meet(self):
        pl.semaphore_wait(pltpu.get_barrier_semaphore(), self.n_dp + self.n_blk - 2)

    def finish(self):
        for batch in self.open:
            batch.wait_send()

    def stop(self):
        for batch in self.open:
            batch.wait_recv()
        for load in self.loads:
            load.wait()
        self.finish()

    def exchange(self, src, dst, first, size):
        part = pl.ds(first, size)
        moves = [(src.at[self.blk_peer(mask), part], dst.at[self.blk, part], 0, mask) for mask in range(1, self.n_blk)]
        batch = Batch(self, moves, dst.at[pl.ds(0, self.n_blk - 1), part])
        dst[self.blk, part] = src[self.blk, part]
        return batch


class Gather:
    def __init__(self, links, buf):
        self.links, self.buf, self.got = links, buf, {}
        self.bits = [1 << k for k in range(links.n_dp.bit_length() - 1)]
        self.forward(0)

    def forward(self, mask):
        low = mask & -mask if mask else self.links.n_dp
        if mask:
            self.got[mask].wait_recv()
        slot = self.buf.at[self.links.dp_peer(mask)]
        for bit in reversed(self.bits):
            if bit < low:
                self.got[mask | bit] = Batch(self.links, [(slot, slot, bit, 0)], slot)

    def relay(self):
        for mask in sorted(range(1, self.links.n_dp), key=lambda m: bin(m).count("1")):
            self.forward(mask)


def bit_names(n_dp, n_blk):
    blk = [("blk", 1 << k) for k in range(n_blk.bit_length() - 1)]
    dp = [("dp", 1 << k) for k in range(n_dp.bit_length() - 1)]
    return {"x": blk[:1], "z0": blk[1:2], "z1": blk[2:], "c": dp[:1], "y": dp[1:]}


class Chunk:
    def __init__(self, links, rows, part, out, landing, every, plan, measure):
        self.measure = measure
        names = bit_names(links.n_dp, links.n_blk)
        order, late = plan
        spread = lambda tokens: [bit for token in tokens for bit in names[token]]
        self.links, self.rows, self.part, self.out, self.landing = links, rows, part, out, landing
        self.halving = spread(order)
        back = [token for token in reversed(order) if token not in "cy"]
        back = back[:late] + ["y"] + back[late:] + ["c"]
        self.doubling = []
        for token in back:
            bits = names[token]
            self.doubling += bits if token in "cy" else bits[::-1]
        self.held = list(range(links.n_dp)) if every else [0]
        self.walk = self.steps()
        self.live = True

    def advance(self):
        self.live = next(self.walk, "end") != "end"

    def steps(self):
        links = self.links
        held, low, size, lows, at, last_batch = self.held, 0, self.rows, [], 0, None
        send = links.send.at[links.used_send]
        links.used_send += 1

        def move(moves, total):
            if last_batch is not None:
                last_batch.wait_send()
            return Batch(links, moves, total, send)

        for k, (axis, bit) in enumerate(self.halving):
            last = k + 1 == len(self.halving)
            if axis == "blk":
                half = size // 2
                mine = (links.blk // bit) % 2
                keep = pl.multiple_of(low + mine * half, 8)
                away = pl.multiple_of(low + (1 - mine) * half, 8)
                moves = [(mask, mask, away) for mask in held]
                lows.append(low)
                low, size = keep, half
            else:
                moves = [(mask, mask ^ bit, low) for mask in held if mask & bit]
                held = [mask for mask in held if not mask & bit]
            slots, copies, start = {}, [], at
            dp_mask, blk_mask = (0, bit) if axis == "blk" else (bit, 0)
            for mask, there, row in moves:
                slots[there] = self.landing.at[pl.ds(at, size), :]
                at += size
                copies.append((self.part(mask, row, size), slots[there], dp_mask, blk_mask))
            last_batch = move(copies, self.landing.at[pl.ds(start, at - start), :])
            yield
            last_batch.wait_recv()
            for mask in held:
                own = self.part(mask, low, size)
                goal = self.out(mask, low, size) if last else own
                goal[...] = own[...] + slots[mask][...]
        for axis, bit in self.doubling:
            place = [self.out(mask, low, size) for mask in held]
            dp_mask, blk_mask = (0, bit) if axis == "blk" else (bit, 0)
            total = self.measure.at[pl.ds(0, size * len(held)), pl.ds(0, place[0].shape[1])]
            last_batch = move([(v, v, dp_mask, blk_mask) for v in place], total)
            if axis == "blk":
                low, size = lows.pop(), size * 2
            else:
                held = held + [mask | bit for mask in held]
            yield
            last_batch.wait_recv()


def landing_rows(rows, order, n_dp, n_blk, every):
    names, held, total = bit_names(n_dp, n_blk), n_dp if every else 1, 0
    for token in order:
        for axis, _ in names[token]:
            if axis == "blk":
                rows //= 2
            else:
                held //= 2
            total += held * rows
    return total


VEC_ROWS = 16


def whole_kernel(
    n_dp, n_blk, x_hbm, lengths, cot_hbm, log_rate, frequency, out_coef, glu_hbm, in_hbm, out_hbm,
    n1g_hbm, n1b_hbm, log_step_hbm, skip_hbm, glu_b_hbm, n2g_hbm, n2b_hbm, in_b_hbm, out_b_hbm,
    block_out, grad_in, sum_glu, sum_in, sum_out, vec_out, par_out,
    send_sems, recv_sems, load_sems, x_ref, cot_ref, n1g, n1b, log_step, skip_gain, glu_b, n2g, n2b, in_b, out_b, glu_w, ffn_in, ffn_out, windows, rate_own, freq_own, coef_own, step_own,
    a_send, x_all, y_send, y_all, dy_send, dy_all, dx_send, dx_all,
    q_ref, t_ref, h_ref, consts, base, taps, a_ref, b_ref, g_ref,
    result_all, feed_all, dglu, hidden_grad, slice_grad, hidden_s, pre_s, hidden_own, pre_own, slope_keep, unit_keep, residual_keep, gate_keep,
    gelu_keep, acc_out, acc_feed, residual_grad, part_glu, part_in, part_out,
    own_par, dp_par, sum_par, blk_par, all_par, flat_par, vec, dp_vec, sum_vec, blk_vec, *landings,
):
    rows, width = x_ref.shape
    ff = ffn_in.shape[1]
    chans = width // n_blk
    quarter = chans // n_dp
    size = min(GROUP, chans)
    parts = [(first, size) for first in range(0, chans, size)]
    first_parts = [(0, chans)] if FIRST_WHOLE else parts
    links = Links(send_sems, recv_sems, n_dp, n_blk)
    dp, blk = links.dp, links.blk
    lanes_at = pl.multiple_of(blk * chans // 128 * 128, 128)

    links.loads = []
    sources = {
        "x": (x_hbm, x_ref), "n1g": (n1g_hbm, n1g), "n1b": (n1b_hbm, n1b), "cot": (cot_hbm, cot_ref),
        "rate": (log_rate.at[:, pl.ds(lanes_at, 128)], windows.at[0]),
        "freq": (frequency.at[:, pl.ds(lanes_at, 128)], windows.at[1]),
        "coef": (out_coef.at[:, :, pl.ds(lanes_at, 128)], windows.at[pl.ds(2, 2)]),
        "step": (log_step_hbm, log_step), "skip": (skip_hbm, skip_gain), "out": (out_hbm, ffn_out),
        "glu": (glu_hbm, glu_w), "glu_b": (glu_b_hbm, glu_b), "n2g": (n2g_hbm, n2g), "n2b": (n2b_hbm, n2b),
        "in": (in_hbm, ffn_in), "in_b": (in_b_hbm, in_b), "out_b": (out_b_hbm, out_b),
    }
    loads = {}

    def fetch(names):
        for name in names:
            loads[name] = Load(*sources[name], load_sems.at[len(loads)])
            links.loads.append(loads[name])

    def need(*names):
        for name in names:
            loads[name].wait()

    links.greet()
    fetch(list(sources))
    need("x", "n1g", "n1b")

    places = blk * rows + iota((rows, 1), 0)
    live = (places < lengths[0]).astype(F32)
    inputs = x_ref[...].astype(F32)
    normed, unit, scale1 = layer_norm(inputs, n1g[...], n1b[...])
    unit_keep[...] = unit
    mixed = normed.astype(BF16) * live.astype(BF16)
    flip = jnp.where(iota((rows, rows), 0) + iota((rows, rows), 1) == rows - 1, 1.0, 0.0).astype(BF16)
    a_send[...] = nn(flip, mixed).T
    links.meet()
    to_x = [links.exchange(a_send.reshape(n_blk, chans, rows), x_all, *part) for part in first_parts]
    need("cot")
    cot = cot_ref[...].astype(F32)
    result = live * cot
    result_all[dp] = result
    gather_result = Gather(links, result_all)

    need("step", "skip", "rate", "freq", "coef")
    turn = (128 - blk * chans % 128) % 128
    own = [pltpu.roll(windows[k], turn, 1).T[:chans] for k in range(4)]
    rate_own[...], freq_own[...], coef_own[0], coef_own[1] = own
    column = lambda ref: pltpu.roll(jnp.broadcast_to(ref[:, pl.ds(lanes_at, 128)], (128, 128)), turn, 1).T[:chans]
    step_own[...] = column(log_step)
    own_skip = column(skip_gain)

    def ssm():
        return step_own[...], rate_own[...], freq_own[...], (coef_own[0], coef_own[1])

    kern_slot = ssm_setup(n_blk, ssm(), consts, base)
    lead_slot = kern_slot - 1
    base_flat = base.reshape(8 * chans, 128)
    groups(0, chans, lambda group: make_powers(group, chans, consts, kern_slot, base_flat, q_ref, taps), 2 * GROUP)
    shift_taps(own_skip, taps, base)

    x_flat = x_all.reshape(n_blk * chans, 128)
    y_flat = y_send.reshape(n_blk * chans, 128)
    to_y = []
    for k, part in enumerate(parts):
        groups(*part, lambda group: make_band(group, chans, base_flat, t_ref))
        if k < len(to_x):
            to_x[k].wait_recv()
        groups(*part, lambda group: forward_group(group, chans, n_blk, consts, lead_slot, x_flat, q_ref, t_ref, h_ref, y_flat))
        to_y.append(links.exchange(y_send, y_all, *part))

    gather_result.relay()
    need("out")
    low = result.astype(BF16)
    step = ff // 4
    for k in range(4):
        hidden_grad[:, k * step : (k + 1) * step] = nt(low, ffn_out[k * step : (k + 1) * step, :])
    part_ff = ff // n_dp
    rows_s = pl.multiple_of(dp * part_ff, 128)
    out_slice = ffn_out[pl.ds(rows_s, part_ff), :]
    for k in range(n_dp):
        slice_grad[k * rows : (k + 1) * rows, :] = nt(result_all[k].astype(BF16), out_slice)
    need("glu", "glu_b", "n2g", "n2b", "in", "in_b", "out_b")

    for batch in to_y:
        batch.wait_recv()
    conv = y_all.reshape(width, rows)[...].T
    gelu_out, gelu_slope = gelu_parts(conv)
    slope_keep[...] = gelu_slope
    gelu_low = gelu_out.astype(BF16)
    gelu_keep[...] = gelu_low
    glu_pre = nn(gelu_low, glu_w[...]) + glu_b[...]
    left = glu_pre[:, :width]
    gate = 0.5 + 0.5 * jnp.tanh(0.5 * glu_pre[:, width:])
    gate_keep[0] = left
    gate_keep[1] = gate
    residual = x_ref[...].astype(F32) + live * left * gate
    normed_mid, unit_mid, scale_mid = layer_norm(residual, n2g[...], n2b[...])
    feed = normed_mid.astype(BF16)
    feed_all[dp] = feed.astype(F32)
    gather_feed = Gather(links, feed_all)
    residual_keep[0] = residual
    residual_keep[1] = unit_mid

    pieces, arrivals = {}, {}

    def piece(work):
        pieces[work.__name__] = work

    @piece
    def own():
        for k in range(4):
            cut = slice(k * step, (k + 1) * step)
            hidden, slope = gelu_parts(nn(feed, ffn_in[:, cut]) + in_b[:, cut])
            grad_pre = (hidden_grad[:, cut] * slope).astype(BF16)
            hidden_own[:, cut] = hidden.astype(BF16)
            pre_own[:, cut] = grad_pre
            back = nt(grad_pre, ffn_in[:, cut])
            acc_feed[...] = back if k == 0 else acc_feed[...] + back

    @piece
    def glubwd():
        unit_mid = residual_keep[1]
        grad_res = cot_ref[...].astype(F32) + norm_back(acc_feed[...], n2g[...], unit_mid, scale_mid)
        residual_grad[...] = grad_res
        grad_left = live * grad_res
        left, gate = gate_keep[0], gate_keep[1]
        dglu[:, :width] = (grad_left * gate).astype(BF16)
        dglu[:, width:] = (grad_left * left * gate * (1.0 - gate)).astype(BF16)

    @piece
    def late():
        for k in range(4):
            cut = slice(k * step, (k + 1) * step)
            forward = nn(hidden_own[:, cut], ffn_out[cut, :])
            acc_out[...] = forward if k == 0 else acc_out[...] + forward
            vec[7 + k : 8 + k, :] = token_sum(pre_own[:, cut].astype(F32))
        block_out[...] = (residual_keep[0] + live * (acc_out[...] + out_b[...])).astype(BF16)
        grad_feed = acc_feed[...]
        vec[2:3, :] = token_sum(grad_feed * residual_keep[1])
        vec[3:4, :] = token_sum(grad_feed)
        vec[4:5, :] = token_sum(result_all[dp])
        vec[5:6, :] = token_sum(dglu[:, :width].astype(F32))
        vec[6:7, :] = token_sum(dglu[:, width:].astype(F32))

    @piece
    def dy():
        dy_send[...] = (nt(dglu[...], glu_w[...]) * slope_keep[...]).T
        arrivals["dy"] = links.exchange(dy_send.reshape(n_blk, chans, rows), dy_all, 0, chans)

    @piece
    def slice_all():
        gather_feed.relay()
        in_slice = ffn_in[:, pl.ds(rows_s, part_ff)]
        in_b_slice = in_b[:, pl.ds(rows_s, part_ff)]
        for k in range(n_dp):
            hidden, slope = gelu_parts(nn(feed_all[k].astype(BF16), in_slice) + in_b_slice)
            cut = slice(k * rows, (k + 1) * rows)
            hidden_s[cut, :] = hidden.astype(BF16)
            pre_s[cut, :] = (slice_grad[cut, :] * slope).astype(BF16)

    part_gl = 2 * width // n_dp
    shapes = piece_shapes(n_dp, n_blk, width, ff)
    chunks = {}

    def window(ref, row0, col0, rows_at, cols):
        def view(mask, row, size):
            slot = links.dp_peer(mask)
            row_at = pl.multiple_of(slot * rows_at[0] + row0 + row, 8)
            col_at = pl.multiple_of(slot * rows_at[1] + col0, 128) if rows_at[1] else col0
            return ref.at[pl.ds(row_at, size), pl.ds(col_at, cols)]
        return view

    def start_chunk(k):
        if k not in shapes:
            return
        kind, row0, col0, rows_k, cols_k, plan = shapes[k]
        rows_cut, cols_cut = slice(row0, row0 + rows_k), slice(col0, col0 + cols_k)
        if kind == "glu":
            part_glu[rows_cut, :] = tn(gelu_keep[:, rows_cut], dglu[...])
            part = window(part_glu, row0, 0, (0, part_gl), part_gl)
            total = window(sum_glu, row0, 0, (0, part_gl), part_gl)
        elif kind == "out":
            results = result_all[:, :, cols_cut].reshape(n_dp * rows, cols_k).astype(BF16)
            part_out[rows_cut, cols_cut] = tn(hidden_s[:, rows_cut], results)
            part = window(part_out, row0, col0, (0, 0), cols_k)
            total = window(sum_out, row0, col0, (part_ff, 0), cols_k)
        else:
            feeds = feed_all[:, :, rows_cut].reshape(n_dp * rows, rows_k).astype(BF16)
            part_in[rows_cut, cols_cut] = tn(feeds, pre_s[:, cols_cut])
            part = window(part_in, row0, col0, (0, 0), cols_k)
            total = window(sum_in, row0, col0, (0, part_ff), cols_k)
        chunks[k] = Chunk(links, rows_k, part, total, landings[k], kind == "glu", plan, sum_out)
        chunks[k].advance()

    dy_flat = dy_all.reshape(n_blk * chans, 128)
    dx_flat = dx_send.reshape(n_blk * chans, 128)

    def backward(k):
        if k == 0:
            arrivals["dy"].wait_recv()
        size = min(GROUP, chans)
        if k * size < chans:
            backward_group([k * size + i for i in range(size)], chans, n_blk, consts, lead_slot, x_flat, dy_flat, q_ref, t_ref, h_ref, dx_flat, a_ref, b_ref, g_ref)
        if k == 3:
            groups(4 * size, chans - 4 * size, lambda group: backward_group(group, chans, n_blk, consts, lead_slot, x_flat, dy_flat, q_ref, t_ref, h_ref, dx_flat, a_ref, b_ref, g_ref))
            arrivals["dx"] = links.exchange(dx_send, dx_all, 0, chans)

    @piece
    def near():
        split_lags(g_ref, base)
        groups(0, chans, lambda group: near_sums(group, chans, base_flat, q_ref, a_ref, b_ref))
        rate_freq, coefs, d_step, d_skip = finish(chans, ssm(), a_ref, b_ref, g_ref)
        own_par[:, 0, :] = rate_freq
        own_par[:, 1, :] = coefs
        lane = iota((chans, 128), 1)
        pair = jnp.where(lane == 0, d_step, jnp.where(lane == 1, d_skip, 0.0))
        if chans < 128:
            pair = jnp.concatenate([pair, jnp.zeros((128 - chans, 128), F32)], axis=0)
        pair = pair.T[0:8]
        if width > 128:
            pair = jnp.concatenate([pair, jnp.zeros((8, width - 128), F32)], axis=1)
        pair = pltpu.roll(pair, blk * chans, 1)
        vec[11:13, :] = pair[0:2]
        vec[13:16, :] = jnp.zeros((3, width), F32)

    @piece
    def ln1():
        arrivals["dx"].wait_recv()
        back = dx_all.reshape(width, rows)[...].T
        high, rest = split(back)
        rest, last = split(back - high.astype(F32))
        grad_normed = live * (nn(flip, high) + (nn(flip, rest) + nn(flip, last)))
        unit = unit_keep[...]
        vec[0:1, :] = token_sum(grad_normed * unit)
        vec[1:2, :] = token_sum(grad_normed)
        grad_in[...] = residual_grad[...] + norm_back(grad_normed, n1g[...], unit, scale1)

    @piece
    def s0():
        moves = [
            (own_par.at[pl.ds(links.dp_peer(mask) * quarter, quarter)], dp_par.at[dp], mask, 0) for mask in range(1, n_dp)
        ]
        arrivals["s0"] = [
            Batch(links, moves, dp_par.at[pl.ds(0, n_dp - 1)]),
            Batch(links, [(vec, dp_vec.at[dp], mask, 0) for mask in range(1, n_dp)], dp_vec.at[pl.ds(0, n_dp - 1)]),
        ]
        dp_par[dp] = own_par[pl.ds(dp * quarter, quarter)]
        dp_vec[dp] = vec[...]

    @piece
    def s1():
        for batch in arrivals["s0"]:
            batch.wait_recv()
        sum_par[...] = sum_slots(dp_par, n_dp)
        sum_vec[...] = sum_slots(dp_vec, n_dp)
        arrivals["s1"] = [
            Batch(links, [(src, dst.at[blk], 0, mask) for mask in range(1, n_blk)], dst.at[pl.ds(0, n_blk - 1)])
            for src, dst in ((sum_par, blk_par), (sum_vec, blk_vec))
        ]
        blk_par[blk] = sum_par[...]
        blk_vec[blk] = sum_vec[...]

    @piece
    def s2():
        for batch in arrivals["s1"]:
            batch.wait_recv()
        all_par[dp] = blk_par[...]
        arrivals["s2"] = Gather(links, all_par)
        vec_out[...] = sum_slots(blk_vec, n_blk)

    @piece
    def s3():
        arrivals["s2"].relay()
        state = par_out.shape[0] // 4
        for b in range(n_blk):
            for d in range(n_dp):
                at = b * chans + d * quarter
                block = all_par[d, b]
                flat_par[0, at : at + quarter, :] = block[:, 0, :]
                flat_par[1, at : at + quarter, :] = block[:, 1, :]
        par_out[: 2 * state, :] = flat_par[0].T
        par_out[2 * state :, :] = flat_par[1].T

    for token in ORDER:
        if isinstance(token, int):
            if token in chunks:
                chunks[token].advance()
        elif token.startswith("part"):
            start_chunk(int(token[4:]))
        elif token.startswith("bwd"):
            backward(int(token[3:]))
        else:
            pieces["slice_all" if token == "slice" else token]()
    while any(chunk.live for chunk in chunks.values()):
        for chunk in chunks.values():
            chunk.advance()
    links.finish()


def piece_shapes(n_dp, n_blk, width, ff):
    shapes = {}
    n_glu, n_ffn = len(GLU_PLANS), len(FFN_PLANS) // 2
    cuts = min(n_glu, width // (8 * n_blk))
    size = width // cuts
    for k, plan in enumerate(GLU_PLANS[:cuts]):
        shapes[k] = ("glu", k * size, 0, size, 2 * width // n_dp, plan)
    for kind, at, height, breadth in (("out", n_glu, ff // n_dp, width), ("in", n_glu + n_ffn, width, ff // n_dp)):
        cols = min(n_ffn, breadth // 128)
        cuts = min(n_ffn // cols, height // (8 * n_blk))
        high, wide = height // cuts, breadth // cols
        for k in range(cols * cuts):
            shapes[at + k] = (kind, k % cuts * high, k // cuts * wide, high, wide, FFN_PLANS[at - n_glu + k])
    return shapes


def sum_slots(ref, count):
    total = ref[0]
    for k in range(1, count):
        total = total + ref[k]
    return total


def deliver_kernel(big_in, vec, par, rows_out, big_out, rate, freq, coef, rows_buf, sems):
    states = rate.shape[0]
    moves = list(zip(big_in, big_out))
    moves += [(par.at[pl.ds(0, states)], rate), (par.at[pl.ds(states, states)], freq)]
    moves += [(par.at[pl.ds((2 + k) * states, states)], coef.at[k]) for k in range(2)]
    copies = [pltpu.make_async_copy(src, dst, sems.at[k]) for k, (src, dst) in enumerate(moves)]
    for copy in copies:
        copy.start()
    row = 0
    for k, (buf, out) in enumerate(zip(rows_buf, rows_out)):
        for part in range(out.shape[1] // vec.shape[1]):
            buf[:, part * vec.shape[1] : (part + 1) * vec.shape[1]] = vec[row : row + 1, :]
            row += 1
        copies.append(pltpu.make_async_copy(buf, out, sems.at[len(moves) + k]))
        copies[-1].start()
    for copy in copies:
        copy.wait()


def on_device(n_dp, n_blk, block_in, seq_lengths, norm1_gain, norm1_bias, log_step, log_rate, frequency, out_coef, skip_gain, glu_weight, glu_bias, norm2_gain, norm2_bias, ffn_in, ffn_in_bias, ffn_out, ffn_out_bias, cotangent):
    _, rows, width = block_in.shape
    ff = ffn_in.shape[1]
    states = log_rate.shape[1]
    chans, quarter = width // n_blk, width // n_blk // n_dp
    row = lambda v: v.reshape(1, -1)
    vmem, anywhere = pl.BlockSpec(memory_space=VMEM), pl.BlockSpec(memory_space=pl.ANY)
    shape = jax.ShapeDtypeStruct
    outs = [
        shape((rows, width), BF16), shape((rows, width), F32),
        shape((width, 2 * width), F32), shape((width, ff), F32), shape((ff, width), F32),
        shape((VEC_ROWS, width), F32), shape((4 * states, width), F32),
    ]
    part_ff, part_gl = ff // n_dp, 2 * width // n_dp
    tokens = n_dp * rows
    f32 = lambda *dims: VMEM(dims, F32)
    bf16 = lambda *dims: VMEM(dims, BF16)
    dma = lambda n: pltpu.SemaphoreType.DMA((n,))
    shapes = piece_shapes(n_dp, n_blk, width, ff)
    landings = []
    for k in range(len(GLU_PLANS) + len(FFN_PLANS)):
        kind, _, _, rows_k, cols_k, plan = shapes.get(k, ("out", 0, 0, 8 * n_blk, 128, FFN_PLANS[0]))
        landings.append(f32(landing_rows(rows_k, plan[0], n_dp, n_blk, kind == "glu"), cols_k))
    scratch = [
        dma(SEND_SEMS), dma(RECV_SEMS), dma(20),
        bf16(rows, width), bf16(rows, width), f32(1, width), f32(1, width), f32(1, width), f32(1, width), f32(1, 2 * width),
        f32(1, width), f32(1, width), f32(1, ff), f32(1, width),
        bf16(width, 2 * width), bf16(width, ff), bf16(ff, width),
        f32(4, states, 128), f32(chans, states), f32(chans, states), f32(2, chans, states), f32(chans, 128),
        f32(width, rows), f32(n_blk, chans, rows), f32(n_blk, chans, rows), f32(n_blk, chans, rows),
        f32(width, rows), f32(n_blk, chans, rows), f32(n_blk, chans, rows), f32(n_blk, chans, rows),
        bf16(chans, 256, 128), bf16(chans, 256, 128), f32(chans, n_blk, 128), f32(n_consts(n_blk), chans, 128),
        f32(8, chans, 128), f32(chans, 128), f32(2 * chans, 128), f32(2 * chans, 128), f32(chans, 128),
        f32(n_dp, rows, width), f32(n_dp, rows, width),
        bf16(rows, 2 * width),
        f32(rows, ff), f32(tokens, part_ff), bf16(tokens, part_ff), bf16(tokens, part_ff), bf16(rows, ff), bf16(rows, ff),
        f32(rows, width), f32(rows, width), f32(2, rows, width), f32(2, rows, width),
        bf16(rows, width), f32(rows, width), f32(rows, width), f32(rows, width),
        f32(width, 2 * width), f32(width, part_ff), f32(part_ff, width),
        f32(chans, 2, 128), f32(n_dp, quarter, 2, 128), f32(quarter, 2, 128), f32(n_blk, quarter, 2, 128),
        f32(n_dp, n_blk, quarter, 2, 128), f32(2, width, 128),
        f32(VEC_ROWS, width), f32(n_dp, VEC_ROWS, width), f32(VEC_ROWS, width), f32(n_blk, VEC_ROWS, width),
        *landings,
    ]
    out = pl.pallas_call(
        functools.partial(whole_kernel, n_dp, n_blk),
        out_shape=[VMEM(v.shape, v.dtype) for v in outs],
        out_specs=[vmem] * len(outs),
        in_specs=[anywhere, pl.BlockSpec(memory_space=pltpu.SMEM)] + [anywhere] * 16,
        scratch_shapes=scratch,
        compiler_params=pltpu.CompilerParams(collective_id=0, has_side_effects=True, vmem_limit_bytes=44 * 2**20),
    )(
        block_in[0], seq_lengths, cotangent[0], log_rate.T, frequency.T, out_coef.swapaxes(1, 2), glu_weight, ffn_in, ffn_out,
        row(norm1_gain), row(norm1_bias), row(log_step), row(skip_gain), row(glu_bias), row(norm2_gain), row(norm2_bias),
        row(ffn_in_bias), row(ffn_out_bias),
    )
    block_out, grad_in, g_glu, g_in, g_out, vec, par = out
    widths = [width, width, width, width, width, 2 * width, ff, width, width]
    made = [shape((rows, width), BF16), shape((rows, width), F32)]
    big = [shape(v.shape, F32) for v in (g_glu, g_in, g_out)]
    small = [shape((1, w), F32) for w in widths]
    params = [shape((states, width), F32), shape((states, width), F32), shape((2, states, width), F32)]
    out_shapes = made + big + small + params

    def deliver(block_out, grad_in, g_glu, g_in, g_out, vec, par, *rest):
        outs, rows_buf, sems = rest[:17], rest[17:-1], rest[-1]
        big = [g_out, g_in, g_glu, grad_in, block_out]
        deliver_kernel(big, vec, par, outs[5:14], [outs[4], outs[3], outs[2], outs[1], outs[0]], *outs[14:], rows_buf, sems)

    done = pl.pallas_call(
        deliver,
        out_shape=out_shapes,
        in_specs=[vmem] * 7,
        out_specs=[anywhere] * 17,
        scratch_shapes=[f32(1, w) for w in widths] + [dma(18)],
        compiler_params=pltpu.CompilerParams(vmem_limit_bytes=8 * 2**20),
    )(*out)
    flat = [v.reshape(-1) for v in done[5:14]]
    n1_gain, n1_bias, n2_gain, n2_bias, ffn_out_b, glu_b, ffn_in_b, d_step, d_skip = flat
    return (
        done[0][None], done[1][None], n1_gain, n1_bias, d_step, done[14].T, done[15].T, done[16].swapaxes(1, 2), d_skip,
        done[2], glu_b, n2_gain, n2_bias, done[3], ffn_in_b, done[4], ffn_out_b,
    )


def solution(mesh):
    split_spec, whole = P("dp", "blk", None), P()
    return jax.shard_map(
        functools.partial(on_device, mesh.shape["dp"], mesh.shape["blk"]),
        mesh=mesh,
        in_specs=(split_spec, P("dp")) + (whole,) * 15 + (split_spec,),
        out_specs=(split_spec, split_spec) + (whole,) * 15,
        check_vma=False,
    )
```
